32 devices in a mesh: aux: 2 (over core), row: 4 (over z), col: 4 (over y, x).
Axes of the slice: x: 2, y: 2, z: 4, core: 2. Of those that a mesh axis runs over, the one named last changes fastest.
Arguments:
- coulomb: bfloat16 [64, 2048, 2048], P('aux', 'row', 'col'), may hold values from -6 to 6
- occupied: bfloat16 [2048, 2048], P('row'), may hold values from -0.125 to 0.125
- virtual: bfloat16 [2048, 2048], P('row'), may hold values from -0.125 to 0.125
- tile_mask: int32 [16, 16], replicated, may hold values 0 or 1
Outputs:
- chi: float32 [64, 64], P('aux')
The draws below stay inside these ranges and needn't reach their ends.
All inputs are finite; a program needn't handle non-finite values.
Results may differ from the reference program's by a relative error of at most 0.0042.
Values may be sent and summed in bfloat16 or wider, within the bound.
No kernel may reach another device: no remote copies, remote signals or barrier semaphores. Data moves between devices by JAX's collectives and lax.ppermute only.
A program may use at most 192 MiB of HBM per device.

```python
import jax
import jax.numpy as jnp
from jax import lax

NAO = 2048
TILE = 128
NAUX = 64
NT = 16


def place_ends(entries, rng, least, largest):
    place = [jax.random.randint(jax.random.fold_in(rng, axis), (), 0, length) for axis, length in enumerate(entries.shape)]
    longest = entries.shape.index(max(entries.shape))
    neighbour = place[:longest] + [(place[longest] + 1) % entries.shape[longest]] + place[longest + 1:]
    return entries.at[tuple(place)].set(least).at[tuple(neighbour)].set(largest)


def level_of(own_key, dims, pieces, smallest, largest):
    level, own = 1.0, jax.random.fold_in(own_key, 6)
    for dim, parts in pieces:
        heights = jnp.exp(jax.random.uniform(jax.random.fold_in(own, dim), (parts,), jnp.float32, smallest / len(pieces), largest / len(pieces)))
        level = level * jnp.repeat(heights, dims[dim] // parts).reshape([-1 if axis == dim else 1 for axis in range(len(dims))])
    return level


def centred(rng, extent, spread, most, cuts=(), dtype=jnp.bfloat16):
    result = spread * jax.random.normal(rng, extent, jnp.float32)
    if cuts:
        result = result * level_of(rng, extent, cuts, -0.22, 0.18)
    return jnp.clip(result, -most, most).astype(dtype)


def setup_inputs(seed: int = 0) -> dict:
    streams_of = jax.random.split(jax.random.key(seed), 5)
    coulomb = centred(streams_of[0], (NAUX, NAO, NAO), 1.0, 6.0, ((0, 2), (1, 4), (2, 4)))
    occupied = centred(streams_of[1], (NAO, NAO), NAO ** -0.5, 0.125, ((0, 4),))
    virtual = centred(streams_of[2], (NAO, NAO), NAO ** -0.5, 0.125, ((0, 4),))
    tile_mask = place_ends((jax.random.randint(streams_of[3], (NT, NT), 0, 4) < 3).astype(jnp.int32), jax.random.fold_in(streams_of[3], 1), 0, 1)
    return {"coulomb": coulomb, "occupied": occupied, "virtual": virtual, "tile_mask": tile_mask}


def reference(coulomb, occupied, virtual, tile_mask):
    full_mask = jnp.repeat(jnp.repeat(tile_mask, TILE, axis=0), TILE, axis=1)
    screened = coulomb * full_mask.astype(jnp.bfloat16)[None]
    left_t = occupied.T

    def dress_one(block):
        half = jnp.dot(left_t, block, preferred_element_type=jnp.float32).astype(jnp.bfloat16)
        return jnp.dot(half, virtual, preferred_element_type=jnp.float32).astype(jnp.bfloat16)

    dressed = lax.map(dress_one, screened)
    flat_x = dressed.reshape(NAUX, NAO * NAO)
    flat_b = screened.reshape(NAUX, NAO * NAO)
    chi = jnp.dot(flat_x, flat_b.T, preferred_element_type=jnp.float32)
    return chi / NAO
```

```python
import jax
import jax.numpy as jnp
from jax import lax
from jax.sharding import PartitionSpec as P

NAO = 2048
TILE = 128


def swapped(value, axis, apart):
    mask = 2**apart
    pairs = [(source, source ^ mask) for source in range(lax.axis_size(axis))]
    return lax.ppermute(value, axis, pairs)


def gathered(block):
    share = lax.axis_size("col") * lax.axis_size("aux")
    part = block.shape[0] // share
    place = lax.axis_index("col") * lax.axis_size("aux") + lax.axis_index("aux")
    mine = lax.dynamic_slice(block, (place * part, 0), (part, block.shape[1]))
    along = lax.all_gather(mine, "row", axis=0, tiled=False)
    return lax.all_gather(along, ("col", "aux"), axis=0, tiled=False)


def shards(coulomb, occupied, virtual, tile_mask):
    rows = lax.axis_size("row")
    cols = lax.axis_size("col")
    pdev, mrow, ncol = coulomb.shape
    nao = mrow * rows
    jpart = mrow // cols
    pieces = pdev // rows
    row_idx = lax.axis_index("row")
    col_idx = lax.axis_index("col")
    aux_idx = lax.axis_index("aux")
    tiles_r = mrow // TILE
    tiles_c = ncol // TILE
    local_tiles = lax.dynamic_slice(
        tile_mask, (row_idx * tiles_r, col_idx * tiles_c), (tiles_r, tiles_c)
    )
    local_mask = jnp.repeat(jnp.repeat(local_tiles, TILE, axis=0), TILE, axis=1).astype(
        jnp.bfloat16
    )
    by_row = coulomb.reshape(rows, pieces, mrow, ncol)
    moved = []
    for piece in range(pieces):
        part = by_row[:, piece] * local_mask[None]
        moved.append(lax.all_to_all(part, "row", split_axis=0, concat_axis=0, tiled=True))

    occ_all = gathered(occupied).transpose(1, 0, 2, 3).reshape(nao, rows, cols, jpart)
    occ_t = occ_all.transpose(2, 1, 3, 0).reshape(nao, nao)
    virt_all = gathered(virtual).transpose(1, 0, 2, 3).reshape(nao, nao)

    screened = coulomb * local_mask[None]
    apart = screened.reshape(pdev, cols, jpart, ncol).transpose(1, 0, 2, 3)
    strips = lax.all_to_all(apart, "col", split_axis=0, concat_axis=0, tiled=True)
    strips = strips.transpose(1, 2, 0, 3).reshape(pdev, jpart, nao)
    theirs = swapped(strips, "aux", 0)
    both = jnp.concatenate(
        [jnp.where(aux_idx == 0, strips, theirs), jnp.where(aux_idx == 0, theirs, strips)]
    )

    parts = []
    for piece in range(pieces):
        half = jnp.dot(
            occ_t, moved[piece].reshape(nao, ncol), preferred_element_type=jnp.float32
        ).astype(jnp.bfloat16)
        spread = lax.all_to_all(
            half.reshape(cols, rows * jpart, ncol), "col", split_axis=0, concat_axis=0, tiled=True
        )
        wide = spread.transpose(1, 0, 2).reshape(rows * jpart, nao)
        dressed = jnp.dot(wide, virt_all, preferred_element_type=jnp.float32).astype(jnp.bfloat16)
        back = lax.all_to_all(
            dressed.reshape(rows, jpart, nao), "row", split_axis=0, concat_axis=0, tiled=True
        )
        parts.append(
            jnp.einsum("pls,qls->pq", back, both, preferred_element_type=jnp.float32)
        )
    partial_chi = jnp.stack(parts, axis=1).reshape(pdev, 2 * pdev)
    total_chi = lax.psum(partial_chi, ("row", "col"))
    return total_chi / NAO


def solution(mesh):
    placed = (P("aux", "row", "col"), P("row", None), P("row", None), P())
    return jax.shard_map(
        shards, mesh=mesh, in_specs=placed, out_specs=P("aux", None), check_vma=False
    )
```

```python
import jax
import jax.numpy as jnp
from jax import lax
from jax.experimental import pallas as pl
from jax.experimental.pallas import tpu as pltpu
from jax.sharding import PartitionSpec as P

NAO = 2048
TILE = 128
PER = 2
VMEM_BYTES = 48 * 2**20
F32 = jnp.float32
BF16 = jnp.bfloat16
ANY = pl.BlockSpec(memory_space=pl.ANY)
WHOLE = pl.BlockSpec(memory_space=pltpu.VMEM)


def swapped(value, axis, apart):
    if apart == 0:
        return value
    pairs = [(source, source ^ apart) for source in range(lax.axis_size(axis))]
    return lax.ppermute(value, axis, pairs)


def gathered(block, flip):
    rows = lax.axis_size("row")
    share = lax.axis_size("col") * lax.axis_size("aux")
    part = block.shape[0] // share
    place = lax.axis_index("col") * lax.axis_size("aux") + lax.axis_index("aux")
    mine = lax.dynamic_slice(block, (place * part, 0), (part, block.shape[1]))
    along = lax.all_gather(mine, "row", axis=0, tiled=False)
    whole = lax.all_gather(along, ("col", "aux"), axis=0, tiled=False)
    nao = rows * block.shape[0]
    return whole.transpose((3, 1, 0, 2) if flip else (1, 0, 2, 3)).reshape(nao, nao)


def cost(flops, moved):
    return pl.CostEstimate(flops=flops, bytes_accessed=moved, transcendentals=0)


def params():
    return pltpu.CompilerParams(vmem_limit_bytes=VMEM_BYTES)


def masked_piece(by_source, tiles, piece, after):
    rows, _, mrow, ncol = by_source.shape

    def body(tiles_ref, source, *refs):
        target = refs[len(after)]
        tile_row = pl.program_id(0)
        for tile in range(ncol // TILE):
            keep = tiles_ref[tile_row, tile] != 0
            span = slice(tile * TILE, (tile + 1) * TILE)
            block = source[:, :, :, span]
            target[:, :, :, span] = jnp.where(keep, block, jnp.zeros_like(block))

    shape = (rows, PER, TILE, ncol)
    return pl.pallas_call(
        body,
        grid_spec=pltpu.PrefetchScalarGridSpec(
            num_scalar_prefetch=1,
            grid=(mrow // TILE,),
            in_specs=[pl.BlockSpec(shape, lambda r, t: (0, piece, r, 0))] + [ANY] * len(after),
            out_specs=pl.BlockSpec(shape, lambda r, t: (0, 0, r, 0)),
        ),
        out_shape=jax.ShapeDtypeStruct((rows, PER, mrow, ncol), BF16),
        cost_estimate=cost(0, 4 * rows * PER * mrow * ncol),
        compiler_params=params(),
        name="masked_piece",
    )(tiles, by_source, *after)


def masked_strips(coulomb, tiles, order, jpart, after):
    count = order.shape[0]
    pdev, mrow, ncol = coulomb.shape

    def body(order_ref, tiles_ref, *refs):
        ins, outs = refs[:count], refs[count + len(after) :]
        for step, (source, target) in enumerate(zip(ins, outs)):
            tile_row = lax.div(order_ref[step] * jpart, TILE)
            for tile in range(ncol // TILE):
                keep = tiles_ref[tile_row, tile] != 0
                span = slice(tile * TILE, (tile + 1) * TILE)
                block = source[:, :, span]
                target[:, :, span] = jnp.where(keep, block, jnp.zeros_like(block))

    some = pdev // 8

    def strip(step):
        return pl.BlockSpec((some, jpart, ncol), lambda p, order, tiles: (p, order[step], 0))

    return pl.pallas_call(
        body,
        grid_spec=pltpu.PrefetchScalarGridSpec(
            num_scalar_prefetch=2,
            grid=(pdev // some,),
            in_specs=[strip(step) for step in range(count)] + [ANY] * len(after),
            out_specs=[pl.BlockSpec((some, jpart, ncol), lambda p, order, tiles: (p, 0, 0))] * count,
        ),
        out_shape=[jax.ShapeDtypeStruct((pdev, jpart, ncol), BF16)] * count,
        cost_estimate=cost(0, 4 * count * pdev * jpart * ncol),
        compiler_params=params(),
        name="masked_strips",
    )(order, tiles, *([coulomb] * count), *after)


def block_order(matrix, places, height, width, after):
    down, across = places[0].shape[0], places[1].shape[0]

    def body(first_ref, second_ref, source, *refs):
        refs[len(after)][...] = source[...]

    return pl.pallas_call(
        body,
        grid_spec=pltpu.PrefetchScalarGridSpec(
            num_scalar_prefetch=2,
            grid=(down, across),
            in_specs=[pl.BlockSpec((height, width), lambda i, k, f, s: (f[i], s[k]))]
            + [ANY] * len(after),
            out_specs=pl.BlockSpec((height, width), lambda i, k, f, s: (i, k)),
        ),
        out_shape=jax.ShapeDtypeStruct(matrix.shape, BF16),
        cost_estimate=cost(0, 4 * matrix.size),
        compiler_params=params(),
        name="block_order",
    )(*places, matrix, *after)


def half_transformed(occ_t, moved, parts, after):
    nao = occ_t.shape[0]
    rows, per, mrow, ncol = moved.shape
    span = nao // parts
    chunk = min(span, 256)

    def body(occ_ref, moved_ref, *refs):
        for part, target in enumerate(refs[len(after) :]):

            @pl.loop(0, span // chunk)
            def _(turn):
                local = pl.multiple_of(turn * chunk, chunk)
                here = pl.ds(pl.multiple_of(part * span + local, chunk), chunk)
                for one in range(per):
                    total = jnp.zeros((chunk, ncol), F32)
                    for row in range(rows):
                        left = occ_ref[here, row * mrow : (row + 1) * mrow]
                        total += jnp.dot(left, moved_ref[row, one], preferred_element_type=F32)
                    target[one, pl.ds(local, chunk), :] = total.astype(BF16)

    return pl.pallas_call(
        body,
        in_specs=[WHOLE, WHOLE] + [ANY] * len(after),
        out_specs=[WHOLE] * parts,
        out_shape=[jax.ShapeDtypeStruct((per, span, ncol), BF16)] * parts,
        cost_estimate=cost(2 * per * nao * nao * ncol, 2 * nao * nao + 4 * per * nao * ncol),
        compiler_params=params(),
        name="half_transformed",
    )(occ_t, moved, *after)


def fully_transformed(blocks, virt, rows, after):
    nao = virt.shape[0]
    per, height, ncol = blocks[0].shape
    span = height // rows
    chunk = 256
    count = len(blocks)

    def body(virt_ref, *refs):
        ins, target = refs[:count], refs[count + len(after)]

        @pl.loop(0, nao // chunk)
        def _(turn):
            across = pl.ds(pl.multiple_of(turn * chunk, chunk), chunk)
            for one in range(per):
                total = jnp.zeros((height, chunk), F32)
                for step, block in enumerate(ins):
                    right = virt_ref[step * ncol : (step + 1) * ncol, across]
                    total += jnp.dot(block[one], right, preferred_element_type=F32)
                done = total.astype(BF16)
                for row in range(rows):
                    target[row, one, :, across] = done[row * span : (row + 1) * span]

    return pl.pallas_call(
        body,
        in_specs=[WHOLE] + [WHOLE] * count + [ANY] * len(after),
        out_specs=WHOLE,
        out_shape=jax.ShapeDtypeStruct((rows, per, span, nao), BF16),
        cost_estimate=cost(2 * per * nao * nao * height, 2 * nao * nao + 4 * per * nao * height),
        compiler_params=params(),
        name="fully_transformed",
    )(virt, *blocks, *after)


def shards(coulomb, occupied, virtual, tile_mask):
    rows = lax.axis_size("row")
    cols = lax.axis_size("col")
    pdev, mrow, ncol = coulomb.shape
    jpart = mrow // cols
    pieces = pdev // rows // PER
    row_idx = lax.axis_index("row")
    col_idx = lax.axis_index("col")
    aux_idx = lax.axis_index("aux")
    col_order = col_idx ^ jnp.arange(cols, dtype=jnp.int32)
    tiles_r = mrow // TILE
    tiles_c = ncol // TILE
    tiles = lax.dynamic_slice(
        tile_mask, (row_idx * tiles_r, col_idx * tiles_c), (tiles_r, tiles_c)
    )
    by_source = coulomb.reshape(rows, pieces * PER, mrow, ncol)

    def along_row(value):
        return lax.all_to_all(value, "row", split_axis=0, concat_axis=0, tiled=True)

    def along_col(blocks):
        return [swapped(block, "col", step) for step, block in enumerate(blocks)]

    masked = []
    for piece in range(pieces):
        masked.append(masked_piece(by_source, tiles, piece, masked[-1:]))
    moved = [along_row(piece) for piece in masked]

    lam_order = (jnp.arange(rows, dtype=jnp.int32) * cols + col_order[:, None]).reshape(-1)
    occ_t = gathered(occupied, True)
    occ_t = block_order(occ_t, (lam_order, jnp.zeros((1,), jnp.int32)), jpart, rows * mrow, masked[-1:])
    virt = block_order(gathered(virtual, False), (col_order, col_order), ncol, ncol, [occ_t])

    strips = masked_strips(coulomb, tiles, col_order, jpart, [moved[0]])
    strips = jnp.concatenate(along_col(strips), axis=2)
    both = jnp.concatenate([strips, swapped(strips, "aux", 1)])

    spread, dressed, back, parts = [], [], [], []
    latest = []
    for turn in range(pieces + 1):
        if turn < pieces:
            half = half_transformed(occ_t, moved[turn], cols, latest)
            spread.append(along_col(half))
            latest = [half[0]]
        if turn > 0:
            dressed.append(fully_transformed(spread[turn - 1], virt, rows, latest))
            latest = [dressed[-1]]
    for piece in range(pieces):
        back.append(along_row(dressed[piece]))
        parts.append(jnp.einsum("zpls,qls->zpq", back[piece], both, preferred_element_type=F32))

    chi = jnp.stack(parts, axis=1).reshape(pdev, 2, pdev)
    chi = jnp.where(aux_idx == 0, chi, chi[:, ::-1]).reshape(pdev, 2 * pdev)
    for axis, size in (("row", rows), ("col", cols)):
        step = 1
        while step < size:
            chi = chi + swapped(chi, axis, step)
            step *= 2
    return chi / NAO


def solution(mesh):
    placed = (P("aux", "row", "col"), P("row", None), P("row", None), P())
    return jax.shard_map(
        shards, mesh=mesh, in_specs=placed, out_specs=P("aux", None), check_vma=False
    )
```

```python
import jax
import jax.numpy as jnp
from jax import lax
from jax.experimental import pallas as pl
from jax.experimental.pallas import tpu as pltpu
from jax.sharding import PartitionSpec as P

NAO = 2048
TILE = 128
FORWARD = 2
PIECES = 4
VMEM_BYTES = 48 * 2**20
F32 = jnp.float32
BF16 = jnp.bfloat16
ANY = pl.BlockSpec(memory_space=pl.ANY)
WHOLE = pl.BlockSpec(memory_space=pltpu.VMEM)


def swapped(value, axis, apart):
    if apart == 0:
        return value
    pairs = [(source, source ^ apart) for source in range(lax.axis_size(axis))]
    return lax.ppermute(value, axis, pairs)


def gathered(blocks):
    rows = lax.axis_size("row")
    share = lax.axis_size("col") * lax.axis_size("aux")
    mrow, nao = blocks[0].shape
    part = mrow // share
    place = lax.axis_index("col") * lax.axis_size("aux") + lax.axis_index("aux")
    mine = jnp.stack([lax.dynamic_slice(b, (place * part, 0), (part, nao)) for b in blocks])
    along = lax.all_gather(mine, "row", axis=0, tiled=False)
    whole = lax.all_gather(along, ("col", "aux"), axis=0, tiled=False)
    first, second = whole[:, :, 0], whole[:, :, 1]
    return first.transpose(3, 1, 0, 2).reshape(nao, nao), second.transpose(1, 0, 2, 3).reshape(nao, nao)


def cost(flops, moved):
    return pl.CostEstimate(flops=flops, bytes_accessed=moved, transcendentals=0)


def params():
    return pltpu.CompilerParams(vmem_limit_bytes=VMEM_BYTES)


def masked_piece(by_source, tiles, piece, per, after):
    rows, _, mrow, ncol = by_source.shape

    def body(tiles_ref, source, *refs):
        target = refs[len(after)]
        tile_row = pl.program_id(0)
        for tile in range(ncol // TILE):
            keep = tiles_ref[tile_row, tile] != 0
            span = slice(tile * TILE, (tile + 1) * TILE)
            block = source[:, :, :, span]
            target[:, :, :, span] = jnp.where(keep, block, jnp.zeros_like(block))

    shape = (rows, per, TILE, ncol)
    return pl.pallas_call(
        body,
        grid_spec=pltpu.PrefetchScalarGridSpec(
            num_scalar_prefetch=1,
            grid=(mrow // TILE,),
            in_specs=[pl.BlockSpec(shape, lambda r, t: (0, piece, r, 0))] + [ANY] * len(after),
            out_specs=pl.BlockSpec(shape, lambda r, t: (0, 0, r, 0)),
        ),
        out_shape=jax.ShapeDtypeStruct((rows, per, mrow, ncol), BF16),
        cost_estimate=cost(0, 4 * rows * per * mrow * ncol),
        compiler_params=params(),
        name="masked_piece",
    )(tiles, by_source, *after)


def block_order(matrix, places, height, width, after):
    down, across = places[0].shape[0], places[1].shape[0]

    def body(first_ref, second_ref, source, *refs):
        refs[len(after)][...] = source[...]

    return pl.pallas_call(
        body,
        grid_spec=pltpu.PrefetchScalarGridSpec(
            num_scalar_prefetch=2,
            grid=(down, across),
            in_specs=[pl.BlockSpec((height, width), lambda i, k, f, s: (f[i], s[k]))]
            + [ANY] * len(after),
            out_specs=pl.BlockSpec((height, width), lambda i, k, f, s: (i, k)),
        ),
        out_shape=jax.ShapeDtypeStruct(matrix.shape, BF16),
        cost_estimate=cost(0, 4 * matrix.size),
        compiler_params=params(),
        name="block_order",
    )(*places, matrix, *after)


def half_transformed(occ_t, moved, first, per, parts, after):
    nao = occ_t.shape[0]
    rows, _, mrow, ncol = moved.shape
    span = nao // parts
    chunk = min(span, 256)

    def body(occ_ref, moved_ref, *refs):
        for part, target in enumerate(refs[len(after) :]):

            @pl.loop(0, span // chunk)
            def _(turn):
                local = pl.multiple_of(turn * chunk, chunk)
                here = pl.ds(pl.multiple_of(part * span + local, chunk), chunk)
                for one in range(per):
                    total = jnp.zeros((chunk, ncol), F32)
                    for row in range(rows):
                        left = occ_ref[here, row * mrow : (row + 1) * mrow]
                        total += jnp.dot(left, moved_ref[row, one], preferred_element_type=F32)
                    target[one, pl.ds(local, chunk), :] = total.astype(BF16)

    return pl.pallas_call(
        body,
        grid=(1,),
        in_specs=[
            pl.BlockSpec((nao, nao), lambda i: (0, 0), pipeline_mode=pl.Buffered(1)),
            pl.BlockSpec(
                (rows, per, mrow, ncol),
                lambda i: (0, first // per, 0, 0),
                pipeline_mode=pl.Buffered(1),
            ),
        ]
        + [ANY] * len(after),
        out_specs=[
            pl.BlockSpec((per, span, ncol), lambda i: (0, 0, 0), pipeline_mode=pl.Buffered(1))
        ]
        * parts,
        out_shape=[jax.ShapeDtypeStruct((per, span, ncol), BF16)] * parts,
        cost_estimate=cost(2 * per * nao * nao * ncol, 2 * nao * nao + 4 * per * nao * ncol),
        compiler_params=params(),
        name="half_transformed",
    )(occ_t, moved, *after)


def fully_transformed(blocks, virt, rows, after):
    nao = virt.shape[0]
    per, height, ncol = blocks[0].shape
    span = height // rows
    chunk = 256
    count = len(blocks)

    def body(virt_ref, *refs):
        ins, target = refs[:count], refs[count + len(after)]

        @pl.loop(0, nao // chunk)
        def _(turn):
            across = pl.ds(pl.multiple_of(turn * chunk, chunk), chunk)
            for one in range(per):
                total = jnp.zeros((height, chunk), F32)
                for step, block in enumerate(ins):
                    right = virt_ref[step * ncol : (step + 1) * ncol, across]
                    total += jnp.dot(block[one], right, preferred_element_type=F32)
                done = total.astype(BF16)
                for row in range(rows):
                    target[row, one, :, across] = done[row * span : (row + 1) * span]

    return pl.pallas_call(
        body,
        in_specs=[WHOLE] + [WHOLE] * count + [ANY] * len(after),
        out_specs=WHOLE,
        out_shape=jax.ShapeDtypeStruct((rows, per, span, nao), BF16),
        cost_estimate=cost(2 * per * nao * nao * height, 2 * nao * nao + 4 * per * nao * height),
        compiler_params=params(),
        name="fully_transformed",
    )(virt, *blocks, *after)


def shards(coulomb, occupied, virtual, tile_mask):
    rows = lax.axis_size("row")
    cols = lax.axis_size("col")
    pdev, mrow, ncol = coulomb.shape
    jpart = mrow // cols
    mine = pdev // rows
    row_idx = lax.axis_index("row")
    col_idx = lax.axis_index("col")
    aux_idx = lax.axis_index("aux")
    col_order = col_idx ^ jnp.arange(cols, dtype=jnp.int32)
    tiles_r = mrow // TILE
    tiles_c = ncol // TILE
    tiles = lax.dynamic_slice(
        tile_mask, (row_idx * tiles_r, col_idx * tiles_c), (tiles_r, tiles_c)
    )
    local_mask = jnp.repeat(jnp.repeat(tiles, TILE, axis=0), TILE, axis=1).astype(BF16)
    by_source = coulomb.reshape(rows, mine, mrow, ncol)

    def along_row(value):
        return lax.all_to_all(value, "row", split_axis=0, concat_axis=0, tiled=True)

    def along_col(blocks):
        return [swapped(block, "col", step) for step, block in enumerate(blocks)]

    occ_whole, virt_whole = gathered([occupied, virtual])

    batch = mine // FORWARD
    masked = []
    for piece in range(FORWARD):
        masked.append(masked_piece(by_source, tiles, piece, batch, masked[-1:]))
    moved = [along_row(piece) for piece in masked]

    lam_order = (jnp.arange(rows, dtype=jnp.int32) * cols + col_order[:, None]).reshape(-1)
    whole_row = jnp.zeros((1,), jnp.int32)
    occ_t = block_order(occ_whole, (lam_order, whole_row), jpart, rows * mrow, masked[-1:])
    virt = block_order(virt_whole, (col_order, col_order), ncol, ncol, [occ_t])

    strips = []
    for step in range(cols):
        first = (col_idx ^ step) * jpart
        strip = lax.dynamic_slice(coulomb, (0, first, 0), (pdev, jpart, ncol))
        strip = strip * lax.dynamic_slice(local_mask, (first, 0), (jpart, ncol))[None]
        strips.append(swapped(strip.transpose(1, 0, 2), "col", step))
    strips = jnp.concatenate(strips, axis=2)
    theirs = swapped(strips, "aux", 1)

    spread, parts = [], []
    latest = [virt]
    per = mine // PIECES
    for group in range(FORWARD):
        some = range(group * PIECES // FORWARD, (group + 1) * PIECES // FORWARD)
        for piece in some:
            first = piece * per - group * batch
            half = half_transformed(occ_t, moved[group], first, per, cols, latest)
            latest = [half[0]]
            spread.append(along_col(half))
        for piece in some:
            after = latest + ([parts[piece - 2]] if piece >= 2 else [])
            dressed = fully_transformed(spread[piece], virt, rows, after)
            latest = [dressed]
            back = along_row(dressed).transpose(2, 0, 1, 3).reshape(jpart, rows * per, -1)
            parts.append(
                jnp.concatenate(
                    [
                        jnp.einsum("lps,lqs->pq", back, half, preferred_element_type=F32)
                        for half in (strips, theirs)
                    ],
                    axis=1,
                )
            )

    chi = jnp.stack([part.reshape(rows, per, 2, pdev) for part in parts], axis=1)
    chi = jnp.where(aux_idx == 0, chi, chi[:, :, :, ::-1]).reshape(pdev, 2 * pdev)
    for axis, size in (("row", rows), ("col", cols)):
        step = 1
        while step < size:
            chi = chi + swapped(chi, axis, step)
            step *= 2
    return chi / NAO


def solution(mesh):
    placed = (P("aux", "row", "col"), P("row", None), P("row", None), P())
    return jax.shard_map(
        shards, mesh=mesh, in_specs=placed, out_specs=P("aux", None), check_vma=False
    )
```

```python
import jax
import jax.numpy as jnp
from jax import lax
from jax.experimental import pallas as pl
from jax.experimental.pallas import tpu as pltpu
from jax.sharding import PartitionSpec as P

NAO = 2048
TILE = 128
FORWARD = 2
PIECES = 4
VMEM_BYTES = 48 * 2**20
F32 = jnp.float32
BF16 = jnp.bfloat16
ANY = pl.BlockSpec(memory_space=pl.ANY)
WHOLE = pl.BlockSpec(memory_space=pltpu.VMEM)


def swapped(value, axis, apart):
    if apart == 0:
        return value
    pairs = [(source, source ^ apart) for source in range(lax.axis_size(axis))]
    return lax.ppermute(value, axis, pairs)


def cost(flops, moved):
    return pl.CostEstimate(flops=flops, bytes_accessed=moved, transcendentals=0)


def params():
    return pltpu.CompilerParams(vmem_limit_bytes=VMEM_BYTES)


def later(small, after):
    def body(source, *refs):
        refs[len(after)][...] = source[...]

    return pl.pallas_call(
        body,
        in_specs=[WHOLE] + [ANY] * len(after),
        out_specs=WHOLE,
        out_shape=jax.ShapeDtypeStruct(small.shape, small.dtype),
        name="later",
    )(small, *after)


def own_parts(blocks, place, part, after):
    count, nao = len(blocks), blocks[0].shape[1]

    def body(place_ref, *refs):
        for index in range(count):
            refs[count + len(after)][index] = refs[index][...]

    return pl.pallas_call(
        body,
        grid_spec=pltpu.PrefetchScalarGridSpec(
            num_scalar_prefetch=1,
            grid=(1,),
            in_specs=[pl.BlockSpec((part, nao), lambda i, place: (place[0], 0))] * count
            + [ANY] * len(after),
            out_specs=pl.BlockSpec((count, part, nao), lambda i, place: (0, 0, 0)),
        ),
        out_shape=jax.ShapeDtypeStruct((count, part, nao), BF16),
        name="own_parts",
    )(place.reshape(1), *blocks, *after)


def masked_piece(by_source, tiles, piece, per, after):
    rows, _, mrow, ncol = by_source.shape

    def body(tiles_ref, source, *refs):
        target = refs[len(after)]
        tile_row = pl.program_id(0)
        for tile in range(ncol // TILE):
            keep = tiles_ref[tile_row, tile] != 0
            span = slice(tile * TILE, (tile + 1) * TILE)
            block = source[:, :, :, span]
            target[:, :, :, span] = jnp.where(keep, block, jnp.zeros_like(block))

    shape = (rows, per, TILE, ncol)
    return pl.pallas_call(
        body,
        grid_spec=pltpu.PrefetchScalarGridSpec(
            num_scalar_prefetch=1,
            grid=(mrow // TILE,),
            in_specs=[pl.BlockSpec(shape, lambda r, t: (0, piece, r, 0))] + [ANY] * len(after),
            out_specs=pl.BlockSpec(shape, lambda r, t: (0, 0, r, 0)),
        ),
        out_shape=jax.ShapeDtypeStruct((rows, per, mrow, ncol), BF16),
        cost_estimate=cost(0, 4 * rows * per * mrow * ncol),
        compiler_params=params(),
        name="masked_piece",
    )(tiles, by_source, *after)


def block_order(matrix, places, height, width, after):
    down, across = places[0].shape[0], places[1].shape[0]

    def body(first_ref, second_ref, source, *refs):
        refs[len(after)][...] = source[...]

    return pl.pallas_call(
        body,
        grid_spec=pltpu.PrefetchScalarGridSpec(
            num_scalar_prefetch=2,
            grid=(down, across),
            in_specs=[pl.BlockSpec((height, width), lambda i, k, f, s: (f[i], s[k]))]
            + [ANY] * len(after),
            out_specs=pl.BlockSpec((height, width), lambda i, k, f, s: (i, k)),
        ),
        out_shape=jax.ShapeDtypeStruct(matrix.shape, BF16),
        cost_estimate=cost(0, 4 * matrix.size),
        compiler_params=params(),
        name="block_order",
    )(*places, matrix, *after)


def half_transformed(occ_t, moved, first, per, parts, after):
    nao = occ_t.shape[0]
    rows, _, mrow, ncol = moved.shape
    span = nao // parts
    chunk = min(span, 256)

    def body(occ_ref, moved_ref, *refs):
        for part, target in enumerate(refs[len(after) :]):

            @pl.loop(0, span // chunk)
            def _(turn):
                local = pl.multiple_of(turn * chunk, chunk)
                here = pl.ds(pl.multiple_of(part * span + local, chunk), chunk)
                for one in range(per):
                    total = jnp.zeros((chunk, ncol), F32)
                    for row in range(rows):
                        left = occ_ref[here, row * mrow : (row + 1) * mrow]
                        total += jnp.dot(left, moved_ref[row, one], preferred_element_type=F32)
                    target[one, pl.ds(local, chunk), :] = total.astype(BF16)

    return pl.pallas_call(
        body,
        grid=(1,),
        in_specs=[
            pl.BlockSpec((nao, nao), lambda i: (0, 0), pipeline_mode=pl.Buffered(1)),
            pl.BlockSpec(
                (rows, per, mrow, ncol),
                lambda i: (0, first // per, 0, 0),
                pipeline_mode=pl.Buffered(1),
            ),
        ]
        + [ANY] * len(after),
        out_specs=[
            pl.BlockSpec((per, span, ncol), lambda i: (0, 0, 0), pipeline_mode=pl.Buffered(1))
        ]
        * parts,
        out_shape=[jax.ShapeDtypeStruct((per, span, ncol), BF16)] * parts,
        cost_estimate=cost(2 * per * nao * nao * ncol, 2 * nao * nao + 4 * per * nao * ncol),
        compiler_params=params(),
        name="half_transformed",
    )(occ_t, moved, *after)


def fully_transformed(blocks, virt, rows, after):
    nao = virt.shape[0]
    per, height, ncol = blocks[0].shape
    span = height // rows
    chunk = 256
    count = len(blocks)

    def body(virt_ref, *refs):
        ins, target = refs[:count], refs[count + len(after)]

        @pl.loop(0, nao // chunk)
        def _(turn):
            across = pl.ds(pl.multiple_of(turn * chunk, chunk), chunk)
            for one in range(per):
                total = jnp.zeros((height, chunk), F32)
                for step, block in enumerate(ins):
                    right = virt_ref[step * ncol : (step + 1) * ncol, across]
                    total += jnp.dot(block[one], right, preferred_element_type=F32)
                done = total.astype(BF16)
                for row in range(rows):
                    target[row, one, :, across] = done[row * span : (row + 1) * span]

    return pl.pallas_call(
        body,
        in_specs=[WHOLE] + [WHOLE] * count + [ANY] * len(after),
        out_specs=WHOLE,
        out_shape=jax.ShapeDtypeStruct((rows, per, span, nao), BF16),
        cost_estimate=cost(2 * per * nao * nao * height, 2 * nao * nao + 4 * per * nao * height),
        compiler_params=params(),
        name="fully_transformed",
    )(virt, *blocks, *after)


def shards(coulomb, occupied, virtual, tile_mask):
    rows = lax.axis_size("row")
    cols = lax.axis_size("col")
    pdev, mrow, ncol = coulomb.shape
    jpart = mrow // cols
    nao = mrow * rows
    mine = pdev // rows
    row_idx = lax.axis_index("row")
    col_idx = lax.axis_index("col")
    aux_idx = lax.axis_index("aux")
    col_order = col_idx ^ jnp.arange(cols, dtype=jnp.int32)
    tiles_r = mrow // TILE
    tiles_c = ncol // TILE
    tiles = lax.dynamic_slice(
        tile_mask, (row_idx * tiles_r, col_idx * tiles_c), (tiles_r, tiles_c)
    )
    by_source = coulomb.reshape(rows, mine, mrow, ncol)

    def along_row(value):
        return lax.all_to_all(value, "row", split_axis=0, concat_axis=0, tiled=True)

    def along_col(blocks):
        return [swapped(block, "col", step) for step, block in enumerate(blocks)]

    batch = mine // FORWARD
    masked = [masked_piece(by_source, tiles, 0, batch, [])]

    share = cols * lax.axis_size("aux")
    place = (col_idx * lax.axis_size("aux") + aux_idx).astype(jnp.int32)
    whole = own_parts([occupied, virtual], place, mrow // share, masked)
    whole = lax.all_gather(whole, "row", axis=0, tiled=False)
    whole = lax.all_gather(whole, ("col", "aux"), axis=0, tiled=False)
    occ_t = whole[:, :, 0].transpose(3, 1, 0, 2).reshape(nao, nao)
    virt = whole[:, :, 1].transpose(1, 0, 2, 3).reshape(nao, nao)

    def strip(step, after):
        mask = later(tiles, after)
        mask = jnp.repeat(jnp.repeat(mask, TILE, axis=0), TILE, axis=1).astype(BF16)
        first = (col_idx ^ step) * jpart
        value = lax.dynamic_slice(coulomb, (0, first, 0), (pdev, jpart, ncol))
        value = value * lax.dynamic_slice(mask, (first, 0), (jpart, ncol))[None]
        return value.transpose(1, 0, 2)

    early = [strip(step, [whole]) for step in range(cols - 1)]

    lam_order = (jnp.arange(rows, dtype=jnp.int32) * cols + col_order[:, None]).reshape(-1)
    whole_row = jnp.zeros((1,), jnp.int32)
    occ_t = block_order(occ_t, (lam_order, whole_row), jpart, nao, early)
    virt = block_order(virt, (col_order, col_order), ncol, ncol, [occ_t])

    for piece in range(1, FORWARD):
        masked.append(masked_piece(by_source, tiles, piece, batch, [virt]))
    moved = [along_row(piece) for piece in masked]

    strips = along_col(early)
    back = []
    latest = masked[-1:] + strips[1:]
    per = mine // PIECES
    for group in range(FORWARD):
        some = range(group * PIECES // FORWARD, (group + 1) * PIECES // FORWARD)
        spread = []
        for piece in some:
            first = piece * per - group * batch
            half = half_transformed(occ_t, moved[group], first, per, cols, latest)
            latest = [half[0]]
            spread.append(along_col(half))
        if group == FORWARD - 1:
            strips.append(swapped(strip(cols - 1, latest), "col", cols - 1))
        for blocks in spread:
            dressed = fully_transformed(blocks, virt, rows, latest)
            latest = [dressed]
            back.append(along_row(dressed))

    theirs = [swapped(value, "aux", 1) for value in strips]
    both = jnp.concatenate(
        [jnp.concatenate(strips, axis=2), jnp.concatenate(theirs, axis=2)], axis=1
    )
    parts = []
    for returned in back:
        returned = returned.transpose(2, 0, 1, 3).reshape(jpart, rows * per, nao)
        parts.append(jnp.einsum("lps,lqs->pq", returned, both, preferred_element_type=F32))

    chi = jnp.stack([part.reshape(rows, per, 2, pdev) for part in parts], axis=1)
    chi = jnp.where(aux_idx == 0, chi, chi[:, :, :, ::-1]).reshape(pdev, 2 * pdev)
    for axis, size in (("row", rows), ("col", cols)):
        step = 1
        while step < size:
            chi = chi + swapped(chi, axis, step)
            step *= 2
    return chi / NAO


def solution(mesh):
    placed = (P("aux", "row", "col"), P("row", None), P("row", None), P())
    return jax.shard_map(
        shards, mesh=mesh, in_specs=placed, out_specs=P("aux", None), check_vma=False
    )
```

```python
import jax
import jax.numpy as jnp
from jax import lax
from jax.experimental import pallas as pl
from jax.experimental.pallas import tpu as pltpu
from jax.sharding import PartitionSpec as P

NAO = 2048
TILE = 128
VMEM_BYTES = 48 * 2**20
F32 = jnp.float32
BF16 = jnp.bfloat16
ANY = pl.BlockSpec(memory_space=pl.ANY)
WHOLE = pl.BlockSpec(memory_space=pltpu.VMEM)


def swapped(value, axis, apart):
    if apart == 0:
        return value
    pairs = [(source, source ^ apart) for source in range(lax.axis_size(axis))]
    return lax.ppermute(value, axis, pairs)


def cost(flops, moved):
    return pl.CostEstimate(flops=flops, bytes_accessed=moved, transcendentals=0)


def params():
    return pltpu.CompilerParams(vmem_limit_bytes=VMEM_BYTES)


def later(small, after):
    def body(source, *refs):
        refs[len(after)][...] = source[...]

    return pl.pallas_call(
        body,
        in_specs=[WHOLE] + [ANY] * len(after),
        out_specs=WHOLE,
        out_shape=jax.ShapeDtypeStruct(small.shape, small.dtype),
        name="later",
    )(small, *after)


def own_parts(blocks, place, part, after):
    count, nao = len(blocks), blocks[0].shape[1]

    def body(place_ref, *refs):
        for index in range(count):
            refs[count + len(after)][index] = refs[index][...]

    return pl.pallas_call(
        body,
        grid_spec=pltpu.PrefetchScalarGridSpec(
            num_scalar_prefetch=1,
            grid=(1,),
            in_specs=[pl.BlockSpec((part, nao), lambda i, place: (place[0], 0))] * count
            + [ANY] * len(after),
            out_specs=pl.BlockSpec((count, part, nao), lambda i, place: (0, 0, 0)),
        ),
        out_shape=jax.ShapeDtypeStruct((count, part, nao), BF16),
        name="own_parts",
    )(place.reshape(1), *blocks, *after)


def masked_piece(by_source, tiles, first, per, after):
    rows, _, mrow, ncol = by_source.shape

    def body(tiles_ref, source, *refs):
        target = refs[len(after)]
        for down in range(mrow // TILE):
            for across in range(ncol // TILE):
                keep = tiles_ref[down, across] != 0
                here = slice(down * TILE, (down + 1) * TILE), slice(across * TILE, (across + 1) * TILE)
                block = source[:, 0, here[0], here[1]]
                target[:, 0, here[0], here[1]] = jnp.where(keep, block, jnp.zeros_like(block))

    shape = (rows, 1, mrow, ncol)
    return pl.pallas_call(
        body,
        grid_spec=pltpu.PrefetchScalarGridSpec(
            num_scalar_prefetch=1,
            grid=(per,),
            in_specs=[pl.BlockSpec(shape, lambda i, t: (0, first + i, 0, 0))] + [ANY] * len(after),
            out_specs=pl.BlockSpec(shape, lambda i, t: (0, i, 0, 0)),
        ),
        out_shape=jax.ShapeDtypeStruct((rows, per, mrow, ncol), BF16),
        cost_estimate=cost(0, 4 * rows * per * mrow * ncol),
        compiler_params=params(),
        name="masked_piece",
    )(tiles, by_source, *after)


def masked_strips(coulomb, tiles, order, jpart, after):
    count = order.shape[0]
    pdev, mrow, ncol = coulomb.shape
    some = pdev // 8

    def body(order_ref, tiles_ref, *refs):
        ins, outs = refs[:count], refs[count + len(after) :]
        for step, (source, target) in enumerate(zip(ins, outs)):
            down = lax.div(order_ref[step] * jpart, TILE)
            for across in range(ncol // TILE):
                keep = tiles_ref[down, across] != 0
                span = slice(across * TILE, (across + 1) * TILE)
                block = source[:, :, span]
                target[:, :, span] = jnp.where(keep, block, jnp.zeros_like(block))

    def strip(step):
        return pl.BlockSpec((some, jpart, ncol), lambda p, order, tiles: (p, order[step], 0))

    return pl.pallas_call(
        body,
        grid_spec=pltpu.PrefetchScalarGridSpec(
            num_scalar_prefetch=2,
            grid=(pdev // some,),
            in_specs=[strip(step) for step in range(count)] + [ANY] * len(after),
            out_specs=[pl.BlockSpec((some, jpart, ncol), lambda p, order, tiles: (p, 0, 0))] * count,
        ),
        out_shape=[jax.ShapeDtypeStruct((pdev, jpart, ncol), BF16)] * count,
        cost_estimate=cost(0, 4 * count * pdev * jpart * ncol),
        compiler_params=params(),
        name="masked_strips",
    )(order, tiles, *([coulomb] * count), *after)


def occupied_order(whole, order, jpart, after):
    share, rows, _, part, nao = whole.shape
    mrow = share * part
    cols = order.shape[0]

    def body(order_ref, source, *refs):
        target, flipped = refs[len(after)], refs[len(after) + 1]
        flipped[...] = source[...].reshape(mrow, mrow).T
        for step in range(cols):
            first = pl.multiple_of(order_ref[step] * jpart, jpart)
            target[step, 0] = flipped[pl.ds(first, jpart), :]

    result = pl.pallas_call(
        body,
        grid_spec=pltpu.PrefetchScalarGridSpec(
            num_scalar_prefetch=1,
            grid=(rows, rows),
            in_specs=[pl.BlockSpec((share, 1, 1, part, mrow), lambda i, k, o: (0, k, 0, 0, i))]
            + [ANY] * len(after),
            out_specs=pl.BlockSpec((cols, 1, jpart, mrow), lambda i, k, o: (0, i, 0, k)),
            scratch_shapes=[pltpu.VMEM((mrow, mrow), BF16)],
        ),
        out_shape=jax.ShapeDtypeStruct((cols, rows, jpart, nao), BF16),
        cost_estimate=cost(0, 4 * nao * nao),
        compiler_params=params(),
        name="occupied_order",
    )(order, whole, *after)
    return result.reshape(nao, nao)


def virtual_order(whole, order, ncol, after):
    share, rows, _, part, nao = whole.shape
    cols = order.shape[0]
    units = ncol // part
    groups = share // units

    def body(order_ref, source, *refs):
        refs[len(after)][...] = source[...].reshape(ncol, ncol)

    return pl.pallas_call(
        body,
        grid_spec=pltpu.PrefetchScalarGridSpec(
            num_scalar_prefetch=1,
            grid=(cols, cols),
            in_specs=[
                pl.BlockSpec(
                    (units, 1, 1, part, ncol),
                    lambda i, k, o: (lax.rem(o[i], groups), lax.div(o[i], groups), 1, 0, o[k]),
                )
            ]
            + [ANY] * len(after),
            out_specs=pl.BlockSpec((ncol, ncol), lambda i, k, o: (i, k)),
        ),
        out_shape=jax.ShapeDtypeStruct((nao, nao), BF16),
        cost_estimate=cost(0, 4 * nao * nao),
        compiler_params=params(),
        name="virtual_order",
    )(order, whole, *after)


def contracted(returned, strips, after):
    rows, per, jpart, nao = returned.shape
    pdev, _, ncol = strips[0][0].shape
    left = rows * per
    group = min(jpart, 32 if left <= 8 else 16)
    count = len(strips) * len(strips[0])
    flat = [value for half in strips for value in half]

    def body(returned_ref, *refs):
        ins, target = refs[:count], refs[count + len(after)]

        @pl.when(pl.program_id(0) == 0)
        def _():
            target[...] = jnp.zeros_like(target)

        mine = returned_ref[...].reshape(left * group, nao)
        shape = (group, left * group)
        equal = lax.broadcasted_iota(jnp.int32, shape, 0) == (
            lax.rem(lax.broadcasted_iota(jnp.int32, shape, 1), group)
        )
        for half in range(len(strips)):
            total = jnp.zeros((pdev * group, left * group), F32)
            for step in range(len(strips[0])):
                other = ins[half * len(strips[0]) + step][...].reshape(pdev * group, ncol)
                total += lax.dot_general(
                    other,
                    mine[:, step * ncol : (step + 1) * ncol],
                    (((1,), (1,)), ((), ())),
                    preferred_element_type=F32,
                )
            total = jnp.where(equal[None], total.reshape(pdev, group, left * group), 0.0)
            target[half] += jnp.sum(total, axis=1)

    result = pl.pallas_call(
        body,
        grid=(jpart // group,),
        in_specs=[pl.BlockSpec((rows, per, group, nao), lambda i: (0, 0, i, 0))]
        + [pl.BlockSpec((pdev, group, ncol), lambda i: (0, i, 0))] * count
        + [ANY] * len(after),
        out_specs=pl.BlockSpec((len(strips), pdev, left * group), lambda i: (0, 0, 0)),
        out_shape=jax.ShapeDtypeStruct((len(strips), pdev, left * group), F32),
        cost_estimate=cost(
            2 * len(strips) * pdev * left * group * jpart * nao,
            2 * jpart * nao * (len(strips) * pdev + left),
        ),
        compiler_params=params(),
        name="contracted",
    )(returned, *flat, *after)
    result = result.reshape(len(strips), pdev, rows, per, group).sum(axis=-1)
    return result.transpose(2, 3, 0, 1)


def half_transformed(occ_t, moved, first, per, parts, after):
    nao = occ_t.shape[0]
    rows, _, mrow, ncol = moved.shape
    span = nao // parts
    chunk = min(span, 256)

    def body(occ_ref, moved_ref, *refs):
        for part, target in enumerate(refs[len(after) :]):

            @pl.loop(0, span // chunk)
            def _(turn):
                local = pl.multiple_of(turn * chunk, chunk)
                here = pl.ds(pl.multiple_of(part * span + local, chunk), chunk)
                for one in range(per):
                    total = jnp.zeros((chunk, ncol), F32)
                    for row in range(rows):
                        left = occ_ref[here, row * mrow : (row + 1) * mrow]
                        total += jnp.dot(left, moved_ref[row, one], preferred_element_type=F32)
                    target[one, pl.ds(local, chunk), :] = total.astype(BF16)

    return pl.pallas_call(
        body,
        grid=(1,),
        in_specs=[
            pl.BlockSpec((nao, nao), lambda i: (0, 0), pipeline_mode=pl.Buffered(1)),
            pl.BlockSpec(
                (rows, per, mrow, ncol),
                lambda i: (0, first // per, 0, 0),
                pipeline_mode=pl.Buffered(1),
            ),
        ]
        + [ANY] * len(after),
        out_specs=[
            pl.BlockSpec((per, span, ncol), lambda i: (0, 0, 0), pipeline_mode=pl.Buffered(1))
        ]
        * parts,
        out_shape=[jax.ShapeDtypeStruct((per, span, ncol), BF16)] * parts,
        cost_estimate=cost(2 * per * nao * nao * ncol, 2 * nao * nao + 4 * per * nao * ncol),
        compiler_params=params(),
        name="half_transformed",
    )(occ_t, moved, *after)


def fully_transformed(blocks, virt, rows, after):
    nao = virt.shape[0]
    per, height, ncol = blocks[0].shape
    span = height // rows
    chunk = 256
    count = len(blocks)

    def body(virt_ref, *refs):
        ins, target = refs[:count], refs[count + len(after)]

        @pl.loop(0, nao // chunk)
        def _(turn):
            across = pl.ds(pl.multiple_of(turn * chunk, chunk), chunk)
            for one in range(per):
                total = jnp.zeros((height, chunk), F32)
                for step, block in enumerate(ins):
                    right = virt_ref[step * ncol : (step + 1) * ncol, across]
                    total += jnp.dot(block[one], right, preferred_element_type=F32)
                done = total.astype(BF16)
                for row in range(rows):
                    target[row, one, :, across] = done[row * span : (row + 1) * span]

    return pl.pallas_call(
        body,
        in_specs=[WHOLE] + [WHOLE] * count + [ANY] * len(after),
        out_specs=WHOLE,
        out_shape=jax.ShapeDtypeStruct((rows, per, span, nao), BF16),
        cost_estimate=cost(2 * per * nao * nao * height, 2 * nao * nao + 4 * per * nao * height),
        compiler_params=params(),
        name="fully_transformed",
    )(virt, *blocks, *after)


def shards(coulomb, occupied, virtual, tile_mask):
    rows = lax.axis_size("row")
    cols = lax.axis_size("col")
    pdev, mrow, ncol = coulomb.shape
    jpart = mrow // cols
    nao = mrow * rows
    mine = pdev // rows
    row_idx = lax.axis_index("row")
    col_idx = lax.axis_index("col")
    aux_idx = lax.axis_index("aux")
    col_order = col_idx ^ jnp.arange(cols, dtype=jnp.int32)
    tiles_r = mrow // TILE
    tiles_c = ncol // TILE
    tiles = lax.dynamic_slice(
        tile_mask, (row_idx * tiles_r, col_idx * tiles_c), (tiles_r, tiles_c)
    )
    by_source = coulomb.reshape(rows, mine, mrow, ncol)

    def along_row(value):
        return lax.all_to_all(value, "row", split_axis=0, concat_axis=0, tiled=True)

    def along_col(blocks):
        return [swapped(block, "col", step) for step, block in enumerate(blocks)]

    small, middle = max(1, mine // 8), mine // 2
    sizes = [[small], [middle // 2] * 2, [mine - small - middle]]

    masked = []
    for index, pieces in enumerate(sizes):
        first = sum(sum(before) for before in sizes[:index])
        masked.append(masked_piece(by_source, tiles, first, sum(pieces), masked[-1:]))
    moved = [along_row(piece) for piece in masked]

    share = cols * lax.axis_size("aux")
    place = (col_idx * lax.axis_size("aux") + aux_idx).astype(jnp.int32)
    whole = own_parts([occupied, virtual], place, mrow // share, masked[:1])
    whole = lax.all_gather(whole, "row", axis=0, tiled=False)
    whole = later(whole, moved[:1])
    whole = lax.all_gather(whole, ("col", "aux"), axis=0, tiled=False)

    early = masked_strips(coulomb, tiles, col_order[:-1], jpart, [whole])
    strips = along_col(early)

    occ_t = occupied_order(whole, col_order, jpart, strips[1:])
    virt = virtual_order(whole, col_order, ncol, [occ_t])

    back = []
    latest = [virt]
    for index, pieces in enumerate(sizes):
        spread = []
        for number, per in enumerate(pieces):
            half = half_transformed(occ_t, moved[index], number * per, per, cols, latest)
            latest = [half[0]]
            spread.append(along_col(half))
        if index == len(sizes) - 1:
            last = masked_strips(coulomb, tiles, col_order[-1:], jpart, back_from)
            strips.append(swapped(last[0], "col", cols - 1))
        for blocks in spread:
            dressed = fully_transformed(blocks, virt, rows, latest)
            latest = [dressed]
            back.append(along_row(dressed))
        back_from = latest

    theirs = [swapped(value, "aux", 1) for value in strips]
    parts = [contracted(returned, [strips, theirs], latest) for returned in back]

    chi = jnp.concatenate(parts, axis=1)
    chi = jnp.where(aux_idx == 0, chi, chi[:, :, ::-1]).reshape(pdev, 2 * pdev)
    for axis, size in (("row", rows), ("col", cols)):
        step = 1
        while step < size:
            chi = chi + swapped(chi, axis, step)
            step *= 2
    return chi / NAO


def solution(mesh):
    placed = (P("aux", "row", "col"), P("row", None), P("row", None), P())
    return jax.shard_map(
        shards, mesh=mesh, in_specs=placed, out_specs=P("aux", None), check_vma=False
    )
```

```python
import jax
import jax.numpy as jnp
from jax import lax
from jax.experimental import pallas as pl
from jax.experimental.pallas import tpu as pltpu
from jax.sharding import PartitionSpec as P

NAO = 2048
TILE = 128
VMEM_BYTES = 48 * 2**20
F32 = jnp.float32
BF16 = jnp.bfloat16
ANY = pl.BlockSpec(memory_space=pl.ANY)
WHOLE = pl.BlockSpec(memory_space=pltpu.VMEM)


def swapped(value, axis, apart):
    if apart == 0:
        return value
    pairs = [(source, source ^ apart) for source in range(lax.axis_size(axis))]
    return lax.ppermute(value, axis, pairs)


def cost(flops, moved):
    return pl.CostEstimate(flops=flops, bytes_accessed=moved, transcendentals=0)


def params():
    return pltpu.CompilerParams(vmem_limit_bytes=VMEM_BYTES)


def later(small, after):
    def body(source, *refs):
        refs[len(after)][...] = source[...]

    return pl.pallas_call(
        body,
        in_specs=[WHOLE] + [ANY] * len(after),
        out_specs=WHOLE,
        out_shape=jax.ShapeDtypeStruct(small.shape, small.dtype),
        name="later",
    )(small, *after)


def ordered(value, after):
    def body(*refs):
        del refs

    return pl.pallas_call(
        body,
        in_specs=[ANY] * (1 + len(after)),
        out_specs=ANY,
        out_shape=jax.ShapeDtypeStruct(value.shape, value.dtype),
        input_output_aliases={0: 0},
        name="ordered",
    )(value, *after)


def own_parts(blocks, place, part, after):
    count, nao = len(blocks), blocks[0].shape[1]

    def body(place_ref, *refs):
        for index in range(count):
            refs[count + len(after)][index] = refs[index][...]

    return pl.pallas_call(
        body,
        grid_spec=pltpu.PrefetchScalarGridSpec(
            num_scalar_prefetch=1,
            grid=(1,),
            in_specs=[pl.BlockSpec((part, nao), lambda i, place: (place[0], 0))] * count
            + [ANY] * len(after),
            out_specs=pl.BlockSpec((count, part, nao), lambda i, place: (0, 0, 0)),
        ),
        out_shape=jax.ShapeDtypeStruct((count, part, nao), BF16),
        name="own_parts",
    )(place.reshape(1), *blocks, *after)


def masked_piece(by_source, tiles, first, per, after):
    rows, _, mrow, ncol = by_source.shape

    def body(tiles_ref, source, *refs):
        target = refs[len(after)]
        for down in range(mrow // TILE):
            for across in range(ncol // TILE):
                keep = tiles_ref[down, across] != 0
                here = slice(down * TILE, (down + 1) * TILE), slice(across * TILE, (across + 1) * TILE)
                block = source[:, 0, here[0], here[1]]
                target[:, 0, here[0], here[1]] = jnp.where(keep, block, jnp.zeros_like(block))

    shape = (rows, 1, mrow, ncol)
    return pl.pallas_call(
        body,
        grid_spec=pltpu.PrefetchScalarGridSpec(
            num_scalar_prefetch=1,
            grid=(per,),
            in_specs=[pl.BlockSpec(shape, lambda i, t: (0, first + i, 0, 0))] + [ANY] * len(after),
            out_specs=pl.BlockSpec(shape, lambda i, t: (0, i, 0, 0)),
        ),
        out_shape=jax.ShapeDtypeStruct((rows, per, mrow, ncol), BF16),
        cost_estimate=cost(0, 4 * rows * per * mrow * ncol),
        compiler_params=params(),
        name="masked_piece",
    )(tiles, by_source, *after)


def masked_strips(coulomb, tiles, order, jpart, after):
    count = order.shape[0]
    pdev, mrow, ncol = coulomb.shape
    some = pdev // 8

    def body(order_ref, tiles_ref, *refs):
        ins, outs = refs[:count], refs[count + len(after) :]
        for step, (source, target) in enumerate(zip(ins, outs)):
            down = lax.div(order_ref[step] * jpart, TILE)
            for across in range(ncol // TILE):
                keep = tiles_ref[down, across] != 0
                span = slice(across * TILE, (across + 1) * TILE)
                block = source[:, :, span]
                target[:, :, span] = jnp.where(keep, block, jnp.zeros_like(block))

    def strip(step):
        return pl.BlockSpec((some, jpart, ncol), lambda p, order, tiles: (p, order[step], 0))

    return pl.pallas_call(
        body,
        grid_spec=pltpu.PrefetchScalarGridSpec(
            num_scalar_prefetch=2,
            grid=(pdev // some,),
            in_specs=[strip(step) for step in range(count)] + [ANY] * len(after),
            out_specs=[pl.BlockSpec((some, jpart, ncol), lambda p, order, tiles: (p, 0, 0))] * count,
        ),
        out_shape=[jax.ShapeDtypeStruct((pdev, jpart, ncol), BF16)] * count,
        cost_estimate=cost(0, 4 * count * pdev * jpart * ncol),
        compiler_params=params(),
        name="masked_strips",
    )(order, tiles, *([coulomb] * count), *after)


def occupied_order(whole, order, jpart, after):
    share, rows, _, part, nao = whole.shape
    mrow = share * part
    cols = order.shape[0]

    def body(order_ref, source, *refs):
        target, flipped = refs[len(after)], refs[len(after) + 1]
        flipped[...] = source[...].reshape(mrow, mrow).T
        for step in range(cols):
            first = pl.multiple_of(order_ref[step] * jpart, jpart)
            target[step, 0] = flipped[pl.ds(first, jpart), :]

    result = pl.pallas_call(
        body,
        grid_spec=pltpu.PrefetchScalarGridSpec(
            num_scalar_prefetch=1,
            grid=(rows, rows),
            in_specs=[pl.BlockSpec((share, 1, 1, part, mrow), lambda i, k, o: (0, k, 0, 0, i))]
            + [ANY] * len(after),
            out_specs=pl.BlockSpec((cols, 1, jpart, mrow), lambda i, k, o: (0, i, 0, k)),
            scratch_shapes=[pltpu.VMEM((mrow, mrow), BF16)],
        ),
        out_shape=jax.ShapeDtypeStruct((cols, rows, jpart, nao), BF16),
        cost_estimate=cost(0, 4 * nao * nao),
        compiler_params=params(),
        name="occupied_order",
    )(order, whole, *after)
    return result.reshape(nao, nao)


def virtual_order(whole, order, ncol, after):
    share, rows, _, part, nao = whole.shape
    cols = order.shape[0]
    units = ncol // part
    groups = share // units

    def body(order_ref, source, *refs):
        refs[len(after)][...] = source[...].reshape(ncol, ncol)

    return pl.pallas_call(
        body,
        grid_spec=pltpu.PrefetchScalarGridSpec(
            num_scalar_prefetch=1,
            grid=(cols, cols),
            in_specs=[
                pl.BlockSpec(
                    (units, 1, 1, part, ncol),
                    lambda i, k, o: (lax.rem(o[i], groups), lax.div(o[i], groups), 1, 0, o[k]),
                )
            ]
            + [ANY] * len(after),
            out_specs=pl.BlockSpec((ncol, ncol), lambda i, k, o: (i, k)),
        ),
        out_shape=jax.ShapeDtypeStruct((nao, nao), BF16),
        cost_estimate=cost(0, 4 * nao * nao),
        compiler_params=params(),
        name="virtual_order",
    )(order, whole, *after)


def contracted(returned, strips, after):
    rows, per, jpart, nao = returned.shape
    pdev, _, ncol = strips[0][0].shape
    left = rows * per
    group = min(jpart, 32 if left <= 8 else 16)
    count = len(strips) * len(strips[0])
    flat = [value for half in strips for value in half]

    def body(returned_ref, *refs):
        ins, target = refs[:count], refs[count + len(after)]

        @pl.when(pl.program_id(0) == 0)
        def _():
            target[...] = jnp.zeros_like(target)

        mine = returned_ref[...].reshape(left * group, nao)
        shape = (group, left * group)
        equal = lax.broadcasted_iota(jnp.int32, shape, 0) == (
            lax.rem(lax.broadcasted_iota(jnp.int32, shape, 1), group)
        )
        for half in range(len(strips)):
            total = jnp.zeros((pdev * group, left * group), F32)
            for step in range(len(strips[0])):
                other = ins[half * len(strips[0]) + step][...].reshape(pdev * group, ncol)
                total += lax.dot_general(
                    other,
                    mine[:, step * ncol : (step + 1) * ncol],
                    (((1,), (1,)), ((), ())),
                    preferred_element_type=F32,
                )
            total = jnp.where(equal[None], total.reshape(pdev, group, left * group), 0.0)
            target[half] += jnp.sum(total, axis=1)

    result = pl.pallas_call(
        body,
        grid=(jpart // group,),
        in_specs=[pl.BlockSpec((rows, per, group, nao), lambda i: (0, 0, i, 0))]
        + [pl.BlockSpec((pdev, group, ncol), lambda i: (0, i, 0))] * count
        + [ANY] * len(after),
        out_specs=pl.BlockSpec((len(strips), pdev, left * group), lambda i: (0, 0, 0)),
        out_shape=jax.ShapeDtypeStruct((len(strips), pdev, left * group), F32),
        cost_estimate=cost(
            2 * len(strips) * pdev * left * group * jpart * nao,
            2 * jpart * nao * (len(strips) * pdev + left),
        ),
        compiler_params=params(),
        name="contracted",
    )(returned, *flat, *after)
    result = result.reshape(len(strips), pdev, rows, per, group).sum(axis=-1)
    return result.transpose(2, 3, 0, 1)


def half_transformed(occ_t, moved, first, per, parts, after):
    nao = occ_t.shape[0]
    rows, _, mrow, ncol = moved.shape
    span = nao // parts
    chunk = min(span, 256)

    def body(occ_ref, moved_ref, *refs):
        for part, target in enumerate(refs[len(after) :]):

            @pl.loop(0, span // chunk)
            def _(turn):
                local = pl.multiple_of(turn * chunk, chunk)
                here = pl.ds(pl.multiple_of(part * span + local, chunk), chunk)
                for one in range(per):
                    total = jnp.zeros((chunk, ncol), F32)
                    for row in range(rows):
                        left = occ_ref[here, row * mrow : (row + 1) * mrow]
                        total += jnp.dot(left, moved_ref[row, one], preferred_element_type=F32)
                    target[one, pl.ds(local, chunk), :] = total.astype(BF16)

    return pl.pallas_call(
        body,
        grid=(1,),
        in_specs=[
            pl.BlockSpec((nao, nao), lambda i: (0, 0), pipeline_mode=pl.Buffered(1)),
            pl.BlockSpec(
                (rows, per, mrow, ncol),
                lambda i: (0, first // per, 0, 0),
                pipeline_mode=pl.Buffered(1),
            ),
        ]
        + [ANY] * len(after),
        out_specs=[
            pl.BlockSpec((per, span, ncol), lambda i: (0, 0, 0), pipeline_mode=pl.Buffered(1))
        ]
        * parts,
        out_shape=[jax.ShapeDtypeStruct((per, span, ncol), BF16)] * parts,
        cost_estimate=cost(2 * per * nao * nao * ncol, 2 * nao * nao + 4 * per * nao * ncol),
        compiler_params=params(),
        name="half_transformed",
    )(occ_t, moved, *after)


def fully_transformed(blocks, virt, rows, after):
    nao = virt.shape[0]
    per, height, ncol = blocks[0].shape
    span = height // rows
    chunk = 256
    count = len(blocks)

    def body(virt_ref, *refs):
        ins, target = refs[:count], refs[count + len(after)]

        @pl.loop(0, nao // chunk)
        def _(turn):
            across = pl.ds(pl.multiple_of(turn * chunk, chunk), chunk)
            for one in range(per):
                total = jnp.zeros((height, chunk), F32)
                for step, block in enumerate(ins):
                    right = virt_ref[step * ncol : (step + 1) * ncol, across]
                    total += jnp.dot(block[one], right, preferred_element_type=F32)
                done = total.astype(BF16)
                for row in range(rows):
                    target[row, one, :, across] = done[row * span : (row + 1) * span]

    return pl.pallas_call(
        body,
        in_specs=[WHOLE] + [WHOLE] * count + [ANY] * len(after),
        out_specs=WHOLE,
        out_shape=jax.ShapeDtypeStruct((rows, per, span, nao), BF16),
        cost_estimate=cost(2 * per * nao * nao * height, 2 * nao * nao + 4 * per * nao * height),
        compiler_params=params(),
        name="fully_transformed",
    )(virt, *blocks, *after)


def shards(coulomb, occupied, virtual, tile_mask):
    rows = lax.axis_size("row")
    cols = lax.axis_size("col")
    pdev, mrow, ncol = coulomb.shape
    jpart = mrow // cols
    nao = mrow * rows
    mine = pdev // rows
    row_idx = lax.axis_index("row")
    col_idx = lax.axis_index("col")
    aux_idx = lax.axis_index("aux")
    col_order = col_idx ^ jnp.arange(cols, dtype=jnp.int32)
    tiles_r = mrow // TILE
    tiles_c = ncol // TILE
    tiles = lax.dynamic_slice(
        tile_mask, (row_idx * tiles_r, col_idx * tiles_c), (tiles_r, tiles_c)
    )
    by_source = coulomb.reshape(rows, mine, mrow, ncol)

    def along_row(value):
        return lax.all_to_all(value, "row", split_axis=0, concat_axis=0, tiled=True)

    def along_col(blocks):
        return [swapped(block, "col", step) for step, block in enumerate(blocks)]

    small, middle = max(1, mine // 8), mine // 2
    sizes = [[small], [middle // 2] * 2, [mine - small - middle]]

    masked = []
    for index, pieces in enumerate(sizes):
        first = sum(sum(before) for before in sizes[:index])
        masked.append(masked_piece(by_source, tiles, first, sum(pieces), masked[-1:]))
    moved = [along_row(masked[0]), along_row(masked[1])]
    for piece in masked[2:]:
        moved.append(along_row(ordered(piece, moved[-1:])))

    early = masked_strips(coulomb, tiles, col_order[:-1], jpart, masked[:1])
    strips = along_col(early)

    share = cols * lax.axis_size("aux")
    place = (col_idx * lax.axis_size("aux") + aux_idx).astype(jnp.int32)
    whole = own_parts([occupied, virtual], place, mrow // share, early[:1])
    whole = lax.all_gather(whole, "row", axis=0, tiled=False)
    whole = later(whole, moved[:1] + strips[1:] + masked[1:2])
    whole = lax.all_gather(whole, ("col", "aux"), axis=0, tiled=False)

    occ_t = occupied_order(whole, col_order, jpart, masked[2:])
    virt = virtual_order(whole, col_order, ncol, [occ_t])

    back = []
    latest = [virt]
    for index, pieces in enumerate(sizes):
        spread = []
        for number, per in enumerate(pieces):
            half = half_transformed(occ_t, moved[index], number * per, per, cols, latest)
            latest = [half[0]]
            spread.append(along_col(half))
        if index == len(sizes) - 1:
            last = masked_strips(coulomb, tiles, col_order[-1:], jpart, back_from)
            strips.append(swapped(last[0], "col", cols - 1))
        for blocks in spread:
            dressed = fully_transformed(blocks, virt, rows, latest)
            latest = [dressed]
            back.append(along_row(dressed))
        back_from = latest

    theirs = [swapped(value, "aux", 1) for value in strips]
    parts = [contracted(returned, [strips, theirs], latest) for returned in back]

    chi = jnp.concatenate(parts, axis=1)
    chi = jnp.where(aux_idx == 0, chi, chi[:, :, ::-1]).reshape(pdev, 2 * pdev)
    for axis, size in (("row", rows), ("col", cols)):
        step = 1
        while step < size:
            chi = chi + swapped(chi, axis, step)
            step *= 2
    return chi / NAO


def solution(mesh):
    placed = (P("aux", "row", "col"), P("row", None), P("row", None), P())
    return jax.shard_map(
        shards, mesh=mesh, in_specs=placed, out_specs=P("aux", None), check_vma=False
    )
```

```python
import jax
import jax.numpy as jnp
from jax import lax
from jax.experimental import pallas as pl
from jax.experimental.pallas import tpu as pltpu
from jax.sharding import PartitionSpec as P

NAO = 2048
TILE = 128
VMEM_BYTES = 48 * 2**20
F32 = jnp.float32
BF16 = jnp.bfloat16
ANY = pl.BlockSpec(memory_space=pl.ANY)
WHOLE = pl.BlockSpec(memory_space=pltpu.VMEM)


def swapped(value, axis, apart):
    if apart == 0:
        return value
    pairs = [(source, source ^ apart) for source in range(lax.axis_size(axis))]
    return lax.ppermute(value, axis, pairs)


def cost(flops, moved):
    return pl.CostEstimate(flops=flops, bytes_accessed=moved, transcendentals=0)


def params():
    return pltpu.CompilerParams(vmem_limit_bytes=VMEM_BYTES)


def later(small, after):
    def body(source, *refs):
        refs[len(after)][...] = source[...]

    return pl.pallas_call(
        body,
        in_specs=[WHOLE] + [ANY] * len(after),
        out_specs=WHOLE,
        out_shape=jax.ShapeDtypeStruct(small.shape, small.dtype),
        name="later",
    )(small, *after)


def ordered(value, after):
    def body(*refs):
        del refs

    return pl.pallas_call(
        body,
        in_specs=[ANY] * (1 + len(after)),
        out_specs=ANY,
        out_shape=jax.ShapeDtypeStruct(value.shape, value.dtype),
        input_output_aliases={0: 0},
        name="ordered",
    )(value, *after)


def own_parts(blocks, place, part, after):
    count, nao = len(blocks), blocks[0].shape[1]

    def body(place_ref, *refs):
        for index in range(count):
            refs[count + len(after)][index] = refs[index][...]

    return pl.pallas_call(
        body,
        grid_spec=pltpu.PrefetchScalarGridSpec(
            num_scalar_prefetch=1,
            grid=(1,),
            in_specs=[pl.BlockSpec((part, nao), lambda i, place: (place[0], 0))] * count
            + [ANY] * len(after),
            out_specs=pl.BlockSpec((count, part, nao), lambda i, place: (0, 0, 0)),
        ),
        out_shape=jax.ShapeDtypeStruct((count, part, nao), BF16),
        name="own_parts",
    )(place.reshape(1), *blocks, *after)


def masked_piece(by_source, tiles, first, per, after):
    rows, _, mrow, ncol = by_source.shape

    def body(tiles_ref, source, *refs):
        target = refs[len(after)]
        for down in range(mrow // TILE):
            for across in range(ncol // TILE):
                keep = tiles_ref[down, across] != 0
                here = slice(down * TILE, (down + 1) * TILE), slice(across * TILE, (across + 1) * TILE)
                block = source[:, 0, here[0], here[1]]
                target[:, 0, here[0], here[1]] = jnp.where(keep, block, jnp.zeros_like(block))

    shape = (rows, 1, mrow, ncol)
    return pl.pallas_call(
        body,
        grid_spec=pltpu.PrefetchScalarGridSpec(
            num_scalar_prefetch=1,
            grid=(per,),
            in_specs=[pl.BlockSpec(shape, lambda i, t: (0, first + i, 0, 0))] + [ANY] * len(after),
            out_specs=pl.BlockSpec(shape, lambda i, t: (0, i, 0, 0)),
        ),
        out_shape=jax.ShapeDtypeStruct((rows, per, mrow, ncol), BF16),
        cost_estimate=cost(0, 4 * rows * per * mrow * ncol),
        compiler_params=params(),
        name="masked_piece",
    )(tiles, by_source, *after)


def masked_strips(coulomb, tiles, order, jpart, after):
    count = order.shape[0]
    pdev, mrow, ncol = coulomb.shape
    some = pdev // 8

    def body(order_ref, tiles_ref, *refs):
        ins, outs = refs[:count], refs[count + len(after) :]
        for step, (source, target) in enumerate(zip(ins, outs)):
            down = lax.div(order_ref[step] * jpart, TILE)
            for across in range(ncol // TILE):
                keep = tiles_ref[down, across] != 0
                span = slice(across * TILE, (across + 1) * TILE)
                block = source[:, :, span]
                target[:, :, span] = jnp.where(keep, block, jnp.zeros_like(block))

    def strip(step):
        return pl.BlockSpec((some, jpart, ncol), lambda p, order, tiles: (p, order[step], 0))

    return pl.pallas_call(
        body,
        grid_spec=pltpu.PrefetchScalarGridSpec(
            num_scalar_prefetch=2,
            grid=(pdev // some,),
            in_specs=[strip(step) for step in range(count)] + [ANY] * len(after),
            out_specs=[pl.BlockSpec((some, jpart, ncol), lambda p, order, tiles: (p, 0, 0))] * count,
        ),
        out_shape=[jax.ShapeDtypeStruct((pdev, jpart, ncol), BF16)] * count,
        cost_estimate=cost(0, 4 * count * pdev * jpart * ncol),
        compiler_params=params(),
        name="masked_strips",
    )(order, tiles, *([coulomb] * count), *after)


def occupied_order(whole, order, jpart, after):
    share, rows, _, part, nao = whole.shape
    mrow = share * part
    cols = order.shape[0]

    def body(order_ref, source, *refs):
        target, flipped = refs[len(after)], refs[len(after) + 1]
        flipped[...] = source[...].reshape(mrow, mrow).T
        for step in range(cols):
            first = pl.multiple_of(order_ref[step] * jpart, jpart)
            target[step, 0] = flipped[pl.ds(first, jpart), :]

    result = pl.pallas_call(
        body,
        grid_spec=pltpu.PrefetchScalarGridSpec(
            num_scalar_prefetch=1,
            grid=(rows, rows),
            in_specs=[pl.BlockSpec((share, 1, 1, part, mrow), lambda i, k, o: (0, k, 0, 0, i))]
            + [ANY] * len(after),
            out_specs=pl.BlockSpec((cols, 1, jpart, mrow), lambda i, k, o: (0, i, 0, k)),
            scratch_shapes=[pltpu.VMEM((mrow, mrow), BF16)],
        ),
        out_shape=jax.ShapeDtypeStruct((cols, rows, jpart, nao), BF16),
        cost_estimate=cost(0, 4 * nao * nao),
        compiler_params=params(),
        name="occupied_order",
    )(order, whole, *after)
    return result.reshape(nao, nao)


def virtual_order(whole, order, ncol, after):
    share, rows, _, part, nao = whole.shape
    cols = order.shape[0]
    units = ncol // part
    groups = share // units

    def body(order_ref, source, *refs):
        refs[len(after)][...] = source[...].reshape(ncol, ncol)

    return pl.pallas_call(
        body,
        grid_spec=pltpu.PrefetchScalarGridSpec(
            num_scalar_prefetch=1,
            grid=(cols, cols),
            in_specs=[
                pl.BlockSpec(
                    (units, 1, 1, part, ncol),
                    lambda i, k, o: (lax.rem(o[i], groups), lax.div(o[i], groups), 1, 0, o[k]),
                )
            ]
            + [ANY] * len(after),
            out_specs=pl.BlockSpec((ncol, ncol), lambda i, k, o: (i, k)),
        ),
        out_shape=jax.ShapeDtypeStruct((nao, nao), BF16),
        cost_estimate=cost(0, 4 * nao * nao),
        compiler_params=params(),
        name="virtual_order",
    )(order, whole, *after)


def contracted(returned, strips, after):
    rows, per, jpart, nao = returned.shape
    pdev, _, ncol = strips[0][0].shape
    left = rows * per
    group = min(jpart, 32 if left <= 8 else 16)
    count = len(strips) * len(strips[0])
    flat = [value for half in strips for value in half]

    def body(returned_ref, *refs):
        ins, target = refs[:count], refs[count + len(after)]

        @pl.when(pl.program_id(0) == 0)
        def _():
            target[...] = jnp.zeros_like(target)

        mine = returned_ref[...].reshape(left * group, nao)
        shape = (group, left * group)
        equal = lax.broadcasted_iota(jnp.int32, shape, 0) == (
            lax.rem(lax.broadcasted_iota(jnp.int32, shape, 1), group)
        )
        for half in range(len(strips)):
            total = jnp.zeros((pdev * group, left * group), F32)
            for step in range(len(strips[0])):
                other = ins[half * len(strips[0]) + step][...].reshape(pdev * group, ncol)
                total += lax.dot_general(
                    other,
                    mine[:, step * ncol : (step + 1) * ncol],
                    (((1,), (1,)), ((), ())),
                    preferred_element_type=F32,
                )
            total = jnp.where(equal[None], total.reshape(pdev, group, left * group), 0.0)
            target[half] += jnp.sum(total, axis=1)

    result = pl.pallas_call(
        body,
        grid=(jpart // group,),
        in_specs=[pl.BlockSpec((rows, per, group, nao), lambda i: (0, 0, i, 0))]
        + [pl.BlockSpec((pdev, group, ncol), lambda i: (0, i, 0))] * count
        + [ANY] * len(after),
        out_specs=pl.BlockSpec((len(strips), pdev, left * group), lambda i: (0, 0, 0)),
        out_shape=jax.ShapeDtypeStruct((len(strips), pdev, left * group), F32),
        cost_estimate=cost(
            2 * len(strips) * pdev * left * group * jpart * nao,
            2 * jpart * nao * (len(strips) * pdev + left),
        ),
        compiler_params=params(),
        name="contracted",
    )(returned, *flat, *after)
    result = result.reshape(len(strips), pdev, rows, per, group).sum(axis=-1)
    return result.transpose(2, 3, 0, 1)


def half_transformed(occ_t, moved, first, per, parts, after):
    nao = occ_t.shape[0]
    rows, _, mrow, ncol = moved.shape
    span = nao // parts
    chunk = min(span, 256)

    def body(occ_ref, moved_ref, *refs):
        for part, target in enumerate(refs[len(after) :]):

            @pl.loop(0, span // chunk)
            def _(turn):
                local = pl.multiple_of(turn * chunk, chunk)
                here = pl.ds(pl.multiple_of(part * span + local, chunk), chunk)
                for one in range(per):
                    total = jnp.zeros((chunk, ncol), F32)
                    for row in range(rows):
                        left = occ_ref[here, row * mrow : (row + 1) * mrow]
                        total += jnp.dot(left, moved_ref[row, one], preferred_element_type=F32)
                    target[one, pl.ds(local, chunk), :] = total.astype(BF16)

    return pl.pallas_call(
        body,
        grid=(1,),
        in_specs=[
            pl.BlockSpec((nao, nao), lambda i: (0, 0), pipeline_mode=pl.Buffered(1)),
            pl.BlockSpec(
                (rows, per, mrow, ncol),
                lambda i: (0, first // per, 0, 0),
                pipeline_mode=pl.Buffered(1),
            ),
        ]
        + [ANY] * len(after),
        out_specs=[
            pl.BlockSpec((per, span, ncol), lambda i: (0, 0, 0), pipeline_mode=pl.Buffered(1))
        ]
        * parts,
        out_shape=[jax.ShapeDtypeStruct((per, span, ncol), BF16)] * parts,
        cost_estimate=cost(2 * per * nao * nao * ncol, 2 * nao * nao + 4 * per * nao * ncol),
        compiler_params=params(),
        name="half_transformed",
    )(occ_t, moved, *after)


def fully_transformed(blocks, virt, rows, base, index, total, after):
    nao = virt.shape[0]
    per, height, ncol = blocks[0].shape
    span = height // rows
    chunk = 256
    count = len(blocks)
    rest = ([] if base is None else [base]) + after

    def body(virt_ref, *refs):
        ins, target = refs[:count], refs[count + len(rest)]

        @pl.loop(0, nao // chunk)
        def _(turn):
            across = pl.ds(pl.multiple_of(turn * chunk, chunk), chunk)
            for one in range(per):
                total = jnp.zeros((height, chunk), F32)
                for step, block in enumerate(ins):
                    right = virt_ref[step * ncol : (step + 1) * ncol, across]
                    total += jnp.dot(block[one], right, preferred_element_type=F32)
                done = total.astype(BF16)
                for row in range(rows):
                    target[row, one, :, across] = done[row * span : (row + 1) * span]

    def alone(shape, place):
        return pl.BlockSpec(shape, lambda i: place, pipeline_mode=pl.Buffered(1))

    return pl.pallas_call(
        body,
        grid=(1,),
        in_specs=[alone((nao, nao), (0, 0))]
        + [alone((per, height, ncol), (0, 0, 0))] * count
        + [ANY] * len(rest),
        out_specs=alone((rows, per, span, nao), (0, index, 0, 0)),
        out_shape=jax.ShapeDtypeStruct((rows, total, span, nao), BF16),
        input_output_aliases={} if base is None else {1 + count: 0},
        cost_estimate=cost(2 * per * nao * nao * height, 2 * nao * nao + 4 * per * nao * height),
        compiler_params=params(),
        name="fully_transformed",
    )(virt, *blocks, *rest)


def shards(coulomb, occupied, virtual, tile_mask):
    rows = lax.axis_size("row")
    cols = lax.axis_size("col")
    pdev, mrow, ncol = coulomb.shape
    jpart = mrow // cols
    nao = mrow * rows
    mine = pdev // rows
    row_idx = lax.axis_index("row")
    col_idx = lax.axis_index("col")
    aux_idx = lax.axis_index("aux")
    col_order = col_idx ^ jnp.arange(cols, dtype=jnp.int32)
    tiles_r = mrow // TILE
    tiles_c = ncol // TILE
    tiles = lax.dynamic_slice(
        tile_mask, (row_idx * tiles_r, col_idx * tiles_c), (tiles_r, tiles_c)
    )
    by_source = coulomb.reshape(rows, mine, mrow, ncol)

    def along_row(value):
        return lax.all_to_all(value, "row", split_axis=0, concat_axis=0, tiled=True)

    def along_col(blocks):
        return [swapped(block, "col", step) for step, block in enumerate(blocks)]

    large, small = mine // 2, max(1, mine // 8)
    halves, last = large // 2, mine - large - small

    masked_small = masked_piece(by_source, tiles, large, small, [])
    masked_large = masked_piece(by_source, tiles, 0, large, [masked_small])
    masked_last = masked_piece(by_source, tiles, large + small, last, [masked_large])
    moved_small = along_row(masked_small)
    moved_large = along_row(masked_large)

    strips = [None] * cols
    early = masked_strips(coulomb, tiles, col_order[1:-1], jpart, [masked_small])
    for step, strip in enumerate(early, 1):
        strips[step] = swapped(strip, "col", step)

    share = cols * lax.axis_size("aux")
    place = (col_idx * lax.axis_size("aux") + aux_idx).astype(jnp.int32)
    whole = own_parts([occupied, virtual], place, mrow // share, early[:1])
    whole = lax.all_gather(whole, "row", axis=0, tiled=False)
    whole = later(whole, [moved_small, masked_large] + strips[1:-1])
    whole = lax.all_gather(whole, ("col", "aux"), axis=0, tiled=False)
    occ_t = occupied_order(whole, col_order, jpart, [masked_last])
    virt = virtual_order(whole, col_order, ncol, [occ_t])

    half = half_transformed(occ_t, moved_small, 0, small, cols, [virt])
    first = fully_transformed(
        along_col(half), virt, rows, None, large // small, large + small, [half[0]]
    )
    released = ordered(masked_last, [moved_large, first])
    moved_last = along_row(released)

    latest, spread = [released], []
    for number in range(2):
        half = half_transformed(occ_t, moved_large, number * halves, halves, cols, latest)
        latest = [half[0]]
        spread.append(along_col(half))
    for number, blocks in enumerate(spread):
        first = fully_transformed(
            blocks, virt, rows, first, number, large + small, latest if number == 0 else []
        )
    back = [along_row(first)]

    half = half_transformed(occ_t, moved_last, 0, last, cols, [first])
    late = masked_strips(coulomb, tiles, jnp.stack([col_order[0], col_order[-1]]), jpart, [half[0]])
    strips[0], strips[-1] = late[0], swapped(late[1], "col", cols - 1)
    second = fully_transformed(along_col(half), virt, rows, None, 0, last, [half[0]])
    back.append(along_row(second))
    latest = [second]

    theirs = [swapped(value, "aux", 1) for value in strips]
    parts = [contracted(returned, [strips, theirs], latest) for returned in back]

    chi = jnp.concatenate(parts, axis=1)
    chi = jnp.where(aux_idx == 0, chi, chi[:, :, ::-1]).reshape(pdev, 2 * pdev)
    for axis, size in (("row", rows), ("col", cols)):
        step = 1
        while step < size:
            chi = chi + swapped(chi, axis, step)
            step *= 2
    return chi / NAO


def solution(mesh):
    placed = (P("aux", "row", "col"), P("row", None), P("row", None), P())
    return jax.shard_map(
        shards, mesh=mesh, in_specs=placed, out_specs=P("aux", None), check_vma=False
    )
```

```python
import jax
import jax.numpy as jnp
from jax import lax
from jax.experimental import pallas as pl
from jax.experimental.pallas import tpu as pltpu
from jax.sharding import PartitionSpec as P

NAO = 2048
TILE = 128
VMEM_BYTES = 48 * 2**20
F32 = jnp.float32
BF16 = jnp.bfloat16
ANY = pl.BlockSpec(memory_space=pl.ANY)
WHOLE = pl.BlockSpec(memory_space=pltpu.VMEM)


def swapped(value, axis, apart):
    if apart == 0:
        return value
    pairs = [(source, source ^ apart) for source in range(lax.axis_size(axis))]
    return lax.ppermute(value, axis, pairs)


def cost(flops, moved):
    return pl.CostEstimate(flops=flops, bytes_accessed=moved, transcendentals=0)


def params():
    return pltpu.CompilerParams(vmem_limit_bytes=VMEM_BYTES)


def later(small, after):
    def body(source, *refs):
        refs[len(after)][...] = source[...]

    return pl.pallas_call(
        body,
        in_specs=[WHOLE] + [ANY] * len(after),
        out_specs=WHOLE,
        out_shape=jax.ShapeDtypeStruct(small.shape, small.dtype),
        name="later",
    )(small, *after)


def ordered(value, after):
    def body(*refs):
        del refs

    return pl.pallas_call(
        body,
        in_specs=[ANY] * (1 + len(after)),
        out_specs=ANY,
        out_shape=jax.ShapeDtypeStruct(value.shape, value.dtype),
        input_output_aliases={0: 0},
        name="ordered",
    )(value, *after)


def own_parts(blocks, place, part, after):
    count, nao = len(blocks), blocks[0].shape[1]

    def body(place_ref, *refs):
        for index in range(count):
            refs[count + len(after)][index] = refs[index][...]

    return pl.pallas_call(
        body,
        grid_spec=pltpu.PrefetchScalarGridSpec(
            num_scalar_prefetch=1,
            grid=(1,),
            in_specs=[pl.BlockSpec((part, nao), lambda i, place: (place[0], 0))] * count
            + [ANY] * len(after),
            out_specs=pl.BlockSpec((count, part, nao), lambda i, place: (0, 0, 0)),
        ),
        out_shape=jax.ShapeDtypeStruct((count, part, nao), BF16),
        name="own_parts",
    )(place.reshape(1), *blocks, *after)


def masked_piece(by_source, tiles, first, per, after):
    rows, _, mrow, ncol = by_source.shape

    def body(tiles_ref, source, *refs):
        target = refs[len(after)]
        for down in range(mrow // TILE):
            for across in range(ncol // TILE):
                keep = tiles_ref[down, across] != 0
                here = slice(down * TILE, (down + 1) * TILE), slice(across * TILE, (across + 1) * TILE)
                block = source[:, 0, here[0], here[1]]
                target[:, 0, here[0], here[1]] = jnp.where(keep, block, jnp.zeros_like(block))

    shape = (rows, 1, mrow, ncol)
    return pl.pallas_call(
        body,
        grid_spec=pltpu.PrefetchScalarGridSpec(
            num_scalar_prefetch=1,
            grid=(per,),
            in_specs=[pl.BlockSpec(shape, lambda i, t: (0, first + i, 0, 0))] + [ANY] * len(after),
            out_specs=pl.BlockSpec(shape, lambda i, t: (0, i, 0, 0)),
        ),
        out_shape=jax.ShapeDtypeStruct((rows, per, mrow, ncol), BF16),
        cost_estimate=cost(0, 4 * rows * per * mrow * ncol),
        compiler_params=params(),
        name="masked_piece",
    )(tiles, by_source, *after)


def masked_strips(coulomb, tiles, order, jpart, after):
    count = order.shape[0]
    pdev, mrow, ncol = coulomb.shape
    some = pdev // 4

    def body(order_ref, tiles_ref, *refs):
        ins, outs = refs[:count], refs[count + len(after) :]
        for step, (source, target) in enumerate(zip(ins, outs)):
            down = lax.div(order_ref[step] * jpart, TILE)
            for across in range(ncol // TILE):
                keep = tiles_ref[down, across] != 0
                span = slice(across * TILE, (across + 1) * TILE)
                block = source[:, :, span]
                target[:, :, span] = jnp.where(keep, block, jnp.zeros_like(block))

    def strip(step):
        return pl.BlockSpec((some, jpart, ncol), lambda p, order, tiles: (p, order[step], 0))

    return pl.pallas_call(
        body,
        grid_spec=pltpu.PrefetchScalarGridSpec(
            num_scalar_prefetch=2,
            grid=(pdev // some,),
            in_specs=[strip(step) for step in range(count)] + [ANY] * len(after),
            out_specs=[pl.BlockSpec((some, jpart, ncol), lambda p, order, tiles: (p, 0, 0))] * count,
        ),
        out_shape=[jax.ShapeDtypeStruct((pdev, jpart, ncol), BF16)] * count,
        cost_estimate=cost(0, 4 * count * pdev * jpart * ncol),
        compiler_params=params(),
        name="masked_strips",
    )(order, tiles, *([coulomb] * count), *after)


def occupied_order(whole, order, jpart, after):
    share, rows, _, part, nao = whole.shape
    mrow = share * part
    cols = order.shape[0]

    def body(order_ref, source, *refs):
        target, flipped = refs[len(after)], refs[len(after) + 1]
        flipped[...] = source[...].reshape(mrow, mrow).T
        for step in range(cols):
            first = pl.multiple_of(order_ref[step] * jpart, jpart)
            target[step, 0] = flipped[pl.ds(first, jpart), :]

    result = pl.pallas_call(
        body,
        grid_spec=pltpu.PrefetchScalarGridSpec(
            num_scalar_prefetch=1,
            grid=(rows, rows),
            in_specs=[pl.BlockSpec((share, 1, 1, part, mrow), lambda i, k, o: (0, k, 0, 0, i))]
            + [ANY] * len(after),
            out_specs=pl.BlockSpec((cols, 1, jpart, mrow), lambda i, k, o: (0, i, 0, k)),
            scratch_shapes=[pltpu.VMEM((mrow, mrow), BF16)],
        ),
        out_shape=jax.ShapeDtypeStruct((cols, rows, jpart, nao), BF16),
        cost_estimate=cost(0, 4 * nao * nao),
        compiler_params=params(),
        name="occupied_order",
    )(order, whole, *after)
    return result.reshape(nao, nao)


def virtual_order(whole, order, ncol, after):
    share, rows, _, part, nao = whole.shape
    cols = order.shape[0]
    units = ncol // part
    groups = share // units

    def body(order_ref, source, *refs):
        refs[len(after)][...] = source[...].reshape(ncol, ncol)

    return pl.pallas_call(
        body,
        grid_spec=pltpu.PrefetchScalarGridSpec(
            num_scalar_prefetch=1,
            grid=(cols, cols),
            in_specs=[
                pl.BlockSpec(
                    (units, 1, 1, part, ncol),
                    lambda i, k, o: (lax.rem(o[i], groups), lax.div(o[i], groups), 1, 0, o[k]),
                )
            ]
            + [ANY] * len(after),
            out_specs=pl.BlockSpec((ncol, ncol), lambda i, k, o: (i, k)),
        ),
        out_shape=jax.ShapeDtypeStruct((nao, nao), BF16),
        cost_estimate=cost(0, 4 * nao * nao),
        compiler_params=params(),
        name="virtual_order",
    )(order, whole, *after)


def contracted(returned, strips, after):
    rows, per, jpart, nao = returned.shape
    pdev, _, ncol = strips[0][0].shape
    left = rows * per
    group = min(jpart, 32 if left <= 8 else 16)
    count = len(strips) * len(strips[0])
    flat = [value for half in strips for value in half]

    def body(returned_ref, *refs):
        ins, target = refs[:count], refs[count + len(after)]

        @pl.when(pl.program_id(0) == 0)
        def _():
            target[...] = jnp.zeros_like(target)

        mine = returned_ref[...].reshape(left * group, nao)
        shape = (group, left * group)
        equal = lax.broadcasted_iota(jnp.int32, shape, 0) == (
            lax.rem(lax.broadcasted_iota(jnp.int32, shape, 1), group)
        )
        for half in range(len(strips)):
            begin = half * len(strips[0])
            other = jnp.concatenate(
                [ref[...].reshape(pdev * group, ncol) for ref in ins[begin : begin + len(strips[0])]],
                axis=1,
            )
            total = lax.dot_general(
                other, mine, (((1,), (1,)), ((), ())), preferred_element_type=F32
            )
            total = jnp.where(equal[None], total.reshape(pdev, group, left * group), 0.0)
            target[half] += jnp.sum(total, axis=1)

    result = pl.pallas_call(
        body,
        grid=(jpart // group,),
        in_specs=[pl.BlockSpec((rows, per, group, nao), lambda i: (0, 0, i, 0))]
        + [pl.BlockSpec((pdev, group, ncol), lambda i: (0, i, 0))] * count
        + [ANY] * len(after),
        out_specs=pl.BlockSpec((len(strips), pdev, left * group), lambda i: (0, 0, 0)),
        out_shape=jax.ShapeDtypeStruct((len(strips), pdev, left * group), F32),
        cost_estimate=cost(
            2 * len(strips) * pdev * left * group * jpart * nao,
            2 * jpart * nao * (len(strips) * pdev + left),
        ),
        compiler_params=params(),
        name="contracted",
    )(returned, *flat, *after)
    result = result.reshape(len(strips), pdev, rows, per, group).sum(axis=-1)
    return result.transpose(2, 3, 0, 1)


def half_transformed(occ_t, moved, first, per, parts, after):
    nao = occ_t.shape[0]
    rows, _, mrow, ncol = moved.shape
    span = nao // parts
    chunk = min(span, 256)

    def body(occ_ref, moved_ref, *refs):
        for part, target in enumerate(refs[len(after) :]):

            @pl.loop(0, span // chunk)
            def _(turn):
                local = pl.multiple_of(turn * chunk, chunk)
                here = pl.ds(pl.multiple_of(part * span + local, chunk), chunk)
                for one in range(per):
                    total = jnp.zeros((chunk, ncol), F32)
                    for row in range(rows):
                        left = occ_ref[here, row * mrow : (row + 1) * mrow]
                        total += jnp.dot(left, moved_ref[row, one], preferred_element_type=F32)
                    target[one, pl.ds(local, chunk), :] = total.astype(BF16)

    return pl.pallas_call(
        body,
        grid=(1,),
        in_specs=[
            pl.BlockSpec((nao, nao), lambda i: (0, 0), pipeline_mode=pl.Buffered(1)),
            pl.BlockSpec(
                (rows, per, mrow, ncol),
                lambda i: (0, first // per, 0, 0),
                pipeline_mode=pl.Buffered(1),
            ),
        ]
        + [ANY] * len(after),
        out_specs=[
            pl.BlockSpec((per, span, ncol), lambda i: (0, 0, 0), pipeline_mode=pl.Buffered(1))
        ]
        * parts,
        out_shape=[jax.ShapeDtypeStruct((per, span, ncol), BF16)] * parts,
        cost_estimate=cost(2 * per * nao * nao * ncol, 2 * nao * nao + 4 * per * nao * ncol),
        compiler_params=params(),
        name="half_transformed",
    )(occ_t, moved, *after)


def fully_transformed(blocks, virt, rows, base, index, total, after):
    nao = virt.shape[0]
    per, height, ncol = blocks[0].shape
    span = height // rows
    chunk = 256
    count = len(blocks)
    rest = ([] if base is None else [base]) + after

    def body(virt_ref, *refs):
        ins, target = refs[:count], refs[count + len(rest)]

        @pl.loop(0, nao // chunk)
        def _(turn):
            across = pl.ds(pl.multiple_of(turn * chunk, chunk), chunk)
            for one in range(per):
                total = jnp.zeros((height, chunk), F32)
                for step, block in enumerate(ins):
                    right = virt_ref[step * ncol : (step + 1) * ncol, across]
                    total += jnp.dot(block[one], right, preferred_element_type=F32)
                done = total.astype(BF16)
                for row in range(rows):
                    target[row, one, :, across] = done[row * span : (row + 1) * span]

    def alone(shape, place):
        return pl.BlockSpec(shape, lambda i: place, pipeline_mode=pl.Buffered(1))

    return pl.pallas_call(
        body,
        grid=(1,),
        in_specs=[alone((nao, nao), (0, 0))]
        + [alone((per, height, ncol), (0, 0, 0))] * count
        + [ANY] * len(rest),
        out_specs=alone((rows, per, span, nao), (0, index, 0, 0)),
        out_shape=jax.ShapeDtypeStruct((rows, total, span, nao), BF16),
        input_output_aliases={} if base is None else {1 + count: 0},
        cost_estimate=cost(2 * per * nao * nao * height, 2 * nao * nao + 4 * per * nao * height),
        compiler_params=params(),
        name="fully_transformed",
    )(virt, *blocks, *rest)


def shards(coulomb, occupied, virtual, tile_mask):
    rows = lax.axis_size("row")
    cols = lax.axis_size("col")
    pdev, mrow, ncol = coulomb.shape
    jpart = mrow // cols
    nao = mrow * rows
    mine = pdev // rows
    row_idx = lax.axis_index("row")
    col_idx = lax.axis_index("col")
    aux_idx = lax.axis_index("aux")
    col_order = col_idx ^ jnp.arange(cols, dtype=jnp.int32)
    tiles_r = mrow // TILE
    tiles_c = ncol // TILE
    tiles = lax.dynamic_slice(
        tile_mask, (row_idx * tiles_r, col_idx * tiles_c), (tiles_r, tiles_c)
    )
    by_source = coulomb.reshape(rows, mine, mrow, ncol)

    def along_row(value):
        return lax.all_to_all(value, "row", split_axis=0, concat_axis=0, tiled=True)

    def along_col(blocks):
        return [swapped(block, "col", step) for step, block in enumerate(blocks)]

    large, small = mine // 2, max(1, mine // 8)
    halves, last = large // 2, mine - large - small

    masked_small = masked_piece(by_source, tiles, large, small, [])
    masked_large = masked_piece(by_source, tiles, 0, large, [masked_small])
    masked_last = masked_piece(by_source, tiles, large + small, last, [masked_large])
    moved_small = along_row(masked_small)
    moved_large = along_row(masked_large)

    strips = [None] * cols
    early = masked_strips(coulomb, tiles, col_order[1:-1], jpart, [masked_small])
    for step, strip in enumerate(early, 1):
        strips[step] = swapped(strip, "col", step)

    share = cols * lax.axis_size("aux")
    place = (col_idx * lax.axis_size("aux") + aux_idx).astype(jnp.int32)
    whole = own_parts([occupied, virtual], place, mrow // share, early[:1])
    whole = lax.all_gather(whole, "row", axis=0, tiled=False)
    whole = later(whole, [moved_small, masked_large] + strips[1:-1])
    whole = lax.all_gather(whole, ("col", "aux"), axis=0, tiled=False)
    occ_t = occupied_order(whole, col_order, jpart, [masked_last])
    virt = virtual_order(whole, col_order, ncol, [occ_t])

    half = half_transformed(occ_t, moved_small, 0, small, cols, [virt])
    first = fully_transformed(
        along_col(half), virt, rows, None, large // small, large + small, [half[0]]
    )
    released = ordered(masked_last, [moved_large, first])
    moved_last = along_row(released)

    latest, spread = [released], []
    for number in range(2):
        half = half_transformed(occ_t, moved_large, number * halves, halves, cols, latest)
        latest = [half[0]]
        spread.append(along_col(half))
    for number, blocks in enumerate(spread):
        first = fully_transformed(
            blocks, virt, rows, first, number, large + small, latest if number == 0 else []
        )
    back = [along_row(first)]

    half = half_transformed(occ_t, moved_last, 0, last, cols, [first])
    late = masked_strips(coulomb, tiles, jnp.stack([col_order[0], col_order[-1]]), jpart, [half[0]])
    strips[0], strips[-1] = late[0], swapped(late[1], "col", cols - 1)
    second = fully_transformed(along_col(half), virt, rows, None, 0, last, [half[0]])
    second = ordered(second, strips[-1:])
    back.append(along_row(second))
    latest = [second]

    theirs = [swapped(value, "aux", 1) for value in strips]
    parts = [contracted(returned, [strips, theirs], latest) for returned in back]

    chi = jnp.concatenate(parts, axis=1)
    chi = jnp.where(aux_idx == 0, chi, chi[:, :, ::-1]).reshape(pdev, 2 * pdev)
    for axis, size in (("row", rows), ("col", cols)):
        chi = sum([swapped(chi, axis, step) for step in range(size)])
    return chi / NAO


def solution(mesh):
    placed = (P("aux", "row", "col"), P("row", None), P("row", None), P())
    return jax.shard_map(
        shards, mesh=mesh, in_specs=placed, out_specs=P("aux", None), check_vma=False
    )
```

```python
import jax
import jax.numpy as jnp
from jax import lax
from jax.experimental import pallas as pl
from jax.experimental.pallas import tpu as pltpu
from jax.sharding import PartitionSpec as P

NAO = 2048
TILE = 128
VMEM_BYTES = 48 * 2**20
F32 = jnp.float32
BF16 = jnp.bfloat16
ANY = pl.BlockSpec(memory_space=pl.ANY)
WHOLE = pl.BlockSpec(memory_space=pltpu.VMEM)


def swapped(value, axis, apart):
    if apart == 0:
        return value
    pairs = [(source, source ^ apart) for source in range(lax.axis_size(axis))]
    return lax.ppermute(value, axis, pairs)


def cost(flops, moved):
    return pl.CostEstimate(flops=flops, bytes_accessed=moved, transcendentals=0)


def params():
    return pltpu.CompilerParams(vmem_limit_bytes=VMEM_BYTES)


def ordered(value, after):
    def body(*refs):
        del refs

    return pl.pallas_call(
        body,
        in_specs=[ANY] * (1 + len(after)),
        out_specs=ANY,
        out_shape=jax.ShapeDtypeStruct(value.shape, value.dtype),
        input_output_aliases={0: 0},
        name="ordered",
    )(value, *after)


def own_parts(blocks, place, part, after):
    count, nao = len(blocks), blocks[0].shape[1]

    def body(place_ref, *refs):
        for index in range(count):
            refs[count + len(after)][index] = refs[index][...]

    return pl.pallas_call(
        body,
        grid_spec=pltpu.PrefetchScalarGridSpec(
            num_scalar_prefetch=1,
            grid=(1,),
            in_specs=[pl.BlockSpec((part, nao), lambda i, place: (place[0], 0))] * count
            + [ANY] * len(after),
            out_specs=pl.BlockSpec((count, part, nao), lambda i, place: (0, 0, 0)),
        ),
        out_shape=jax.ShapeDtypeStruct((count, part, nao), BF16),
        name="own_parts",
    )(place.reshape(1), *blocks, *after)


def masked_piece(by_source, tiles, first, per, after):
    rows, _, mrow, ncol = by_source.shape

    def body(tiles_ref, source, *refs):
        target = refs[len(after)]
        for down in range(mrow // TILE):
            for across in range(ncol // TILE):
                keep = tiles_ref[down, across] != 0
                here = slice(down * TILE, (down + 1) * TILE), slice(across * TILE, (across + 1) * TILE)
                block = source[:, 0, here[0], here[1]]
                target[:, 0, here[0], here[1]] = jnp.where(keep, block, jnp.zeros_like(block))

    shape = (rows, 1, mrow, ncol)
    return pl.pallas_call(
        body,
        grid_spec=pltpu.PrefetchScalarGridSpec(
            num_scalar_prefetch=1,
            grid=(per,),
            in_specs=[pl.BlockSpec(shape, lambda i, t: (0, first + i, 0, 0))] + [ANY] * len(after),
            out_specs=pl.BlockSpec(shape, lambda i, t: (0, i, 0, 0)),
        ),
        out_shape=jax.ShapeDtypeStruct((rows, per, mrow, ncol), BF16),
        cost_estimate=cost(0, 4 * rows * per * mrow * ncol),
        compiler_params=params(),
        name="masked_piece",
    )(tiles, by_source, *after)


def masked_strips(coulomb, tiles, order, jpart, after):
    count = order.shape[0]
    pdev, mrow, ncol = coulomb.shape
    some = pdev // 4

    def body(order_ref, tiles_ref, *refs):
        ins, outs = refs[:count], refs[count + len(after) :]
        for step, (source, target) in enumerate(zip(ins, outs)):
            down = lax.div(order_ref[step] * jpart, TILE)
            for across in range(ncol // TILE):
                keep = tiles_ref[down, across] != 0
                span = slice(across * TILE, (across + 1) * TILE)
                block = source[:, :, span]
                target[:, :, span] = jnp.where(keep, block, jnp.zeros_like(block))

    def strip(step):
        return pl.BlockSpec((some, jpart, ncol), lambda p, order, tiles: (p, order[step], 0))

    return pl.pallas_call(
        body,
        grid_spec=pltpu.PrefetchScalarGridSpec(
            num_scalar_prefetch=2,
            grid=(pdev // some,),
            in_specs=[strip(step) for step in range(count)] + [ANY] * len(after),
            out_specs=[pl.BlockSpec((some, jpart, ncol), lambda p, order, tiles: (p, 0, 0))] * count,
        ),
        out_shape=[jax.ShapeDtypeStruct((pdev, jpart, ncol), BF16)] * count,
        cost_estimate=cost(0, 4 * count * pdev * jpart * ncol),
        compiler_params=params(),
        name="masked_strips",
    )(order, tiles, *([coulomb] * count), *after)


def occupied_order(whole, order, jpart, after):
    share, rows, _, part, nao = whole.shape
    mrow = share * part
    cols = order.shape[0]

    def body(order_ref, source, *refs):
        target, flipped = refs[len(after)], refs[len(after) + 1]
        flipped[...] = source[...].reshape(mrow, mrow).T
        for step in range(cols):
            first = pl.multiple_of(order_ref[step] * jpart, jpart)
            target[step, 0] = flipped[pl.ds(first, jpart), :]

    result = pl.pallas_call(
        body,
        grid_spec=pltpu.PrefetchScalarGridSpec(
            num_scalar_prefetch=1,
            grid=(rows, rows),
            in_specs=[pl.BlockSpec((share, 1, 1, part, mrow), lambda i, k, o: (0, k, 0, 0, i))]
            + [ANY] * len(after),
            out_specs=pl.BlockSpec((cols, 1, jpart, mrow), lambda i, k, o: (0, i, 0, k)),
            scratch_shapes=[pltpu.VMEM((mrow, mrow), BF16)],
        ),
        out_shape=jax.ShapeDtypeStruct((cols, rows, jpart, nao), BF16),
        cost_estimate=cost(0, 4 * nao * nao),
        compiler_params=params(),
        name="occupied_order",
    )(order, whole, *after)
    return result.reshape(nao, nao)


def virtual_order(whole, order, ncol, after):
    share, rows, _, part, nao = whole.shape
    cols = order.shape[0]
    units = ncol // part
    groups = share // units

    def body(order_ref, source, *refs):
        refs[len(after)][...] = source[...].reshape(ncol, ncol)

    return pl.pallas_call(
        body,
        grid_spec=pltpu.PrefetchScalarGridSpec(
            num_scalar_prefetch=1,
            grid=(cols, cols),
            in_specs=[
                pl.BlockSpec(
                    (units, 1, 1, part, ncol),
                    lambda i, k, o: (lax.rem(o[i], groups), lax.div(o[i], groups), 1, 0, o[k]),
                )
            ]
            + [ANY] * len(after),
            out_specs=pl.BlockSpec((ncol, ncol), lambda i, k, o: (i, k)),
        ),
        out_shape=jax.ShapeDtypeStruct((nao, nao), BF16),
        cost_estimate=cost(0, 4 * nao * nao),
        compiler_params=params(),
        name="virtual_order",
    )(order, whole, *after)


def contracted(returned, strips, first, after):
    rows, per, jpart, nao = returned.shape
    pdev, _, ncol = strips[0][0].shape
    left = rows * per
    group = min(jpart, 32 if left <= 8 else 16)
    steps = len(strips[0])
    count = len(strips) * steps
    flat = [value for half in strips for value in half]
    width, place = (ncol, first) if steps == 1 else (nao, 0)
    begin = first * ncol - place * width

    def body(returned_ref, *refs):
        ins, target = refs[:count], refs[count + len(after)]

        @pl.when(pl.program_id(0) == 0)
        def _():
            target[...] = jnp.zeros_like(target)

        mine = returned_ref[...].reshape(left * group, width)[:, begin : begin + steps * ncol]
        shape = (group, left * group)
        equal = lax.broadcasted_iota(jnp.int32, shape, 0) == (
            lax.rem(lax.broadcasted_iota(jnp.int32, shape, 1), group)
        )
        for half in range(len(strips)):
            other = [ref[...].reshape(pdev * group, ncol) for ref in ins[half * steps : (half + 1) * steps]]
            total = lax.dot_general(
                jnp.concatenate(other, axis=1),
                mine,
                (((1,), (1,)), ((), ())),
                preferred_element_type=F32,
            )
            total = jnp.where(equal[None], total.reshape(pdev, group, left * group), 0.0)
            target[half] += jnp.sum(total, axis=1)

    result = pl.pallas_call(
        body,
        grid=(jpart // group,),
        in_specs=[pl.BlockSpec((rows, per, group, width), lambda i: (0, 0, i, place))]
        + [pl.BlockSpec((pdev, group, ncol), lambda i: (0, i, 0))] * count
        + [ANY] * len(after),
        out_specs=pl.BlockSpec((len(strips), pdev, left * group), lambda i: (0, 0, 0)),
        out_shape=jax.ShapeDtypeStruct((len(strips), pdev, left * group), F32),
        cost_estimate=cost(
            2 * count * pdev * left * group * jpart * ncol,
            2 * jpart * ncol * (count * pdev + steps * left),
        ),
        compiler_params=pltpu.CompilerParams(vmem_limit_bytes=26 * 2**20),
        name="contracted",
    )(returned, *flat, *after)
    result = result.reshape(len(strips), pdev, rows, per, group).sum(axis=-1)
    return result.transpose(2, 3, 0, 1)


def half_transformed(occ_t, moved, first, per, parts, after):
    nao = occ_t.shape[0]
    rows, _, mrow, ncol = moved.shape
    span = nao // parts
    chunk = min(span, 256)

    def body(occ_ref, moved_ref, *refs):
        for part, target in enumerate(refs[len(after) :]):

            @pl.loop(0, span // chunk)
            def _(turn):
                local = pl.multiple_of(turn * chunk, chunk)
                here = pl.ds(pl.multiple_of(part * span + local, chunk), chunk)
                for one in range(per):
                    total = jnp.zeros((chunk, ncol), F32)
                    for row in range(rows):
                        left = occ_ref[here, row * mrow : (row + 1) * mrow]
                        total += jnp.dot(left, moved_ref[row, one], preferred_element_type=F32)
                    target[one, pl.ds(local, chunk), :] = total.astype(BF16)

    return pl.pallas_call(
        body,
        grid=(1,),
        in_specs=[
            pl.BlockSpec((nao, nao), lambda i: (0, 0), pipeline_mode=pl.Buffered(1)),
            pl.BlockSpec(
                (rows, per, mrow, ncol),
                lambda i: (0, first // per, 0, 0),
                pipeline_mode=pl.Buffered(1),
            ),
        ]
        + [ANY] * len(after),
        out_specs=[
            pl.BlockSpec((per, span, ncol), lambda i: (0, 0, 0), pipeline_mode=pl.Buffered(1))
        ]
        * parts,
        out_shape=[jax.ShapeDtypeStruct((per, span, ncol), BF16)] * parts,
        cost_estimate=cost(2 * per * nao * nao * ncol, 2 * nao * nao + 4 * per * nao * ncol),
        compiler_params=params(),
        name="half_transformed",
    )(occ_t, moved, *after)


def fully_transformed(blocks, virt, rows, base, index, total, after):
    nao = virt.shape[0]
    per, height, ncol = blocks[0].shape
    span = height // rows
    chunk = 256
    count = len(blocks)
    rest = ([] if base is None else [base]) + after

    def body(virt_ref, *refs):
        ins, target = refs[:count], refs[count + len(rest)]

        @pl.loop(0, nao // chunk)
        def _(turn):
            across = pl.ds(pl.multiple_of(turn * chunk, chunk), chunk)
            for one in range(per):
                total = jnp.zeros((height, chunk), F32)
                for step, block in enumerate(ins):
                    right = virt_ref[step * ncol : (step + 1) * ncol, across]
                    total += jnp.dot(block[one], right, preferred_element_type=F32)
                done = total.astype(BF16)
                for row in range(rows):
                    target[row, one, :, across] = done[row * span : (row + 1) * span]

    def alone(shape, place):
        return pl.BlockSpec(shape, lambda i: place, pipeline_mode=pl.Buffered(1))

    return pl.pallas_call(
        body,
        grid=(1,),
        in_specs=[alone((nao, nao), (0, 0))]
        + [alone((per, height, ncol), (0, 0, 0))] * count
        + [ANY] * len(rest),
        out_specs=alone((rows, per, span, nao), (0, index, 0, 0)),
        out_shape=jax.ShapeDtypeStruct((rows, total, span, nao), BF16),
        input_output_aliases={} if base is None else {1 + count: 0},
        cost_estimate=cost(2 * per * nao * nao * height, 2 * nao * nao + 4 * per * nao * height),
        compiler_params=params(),
        name="fully_transformed",
    )(virt, *blocks, *rest)


def shards(coulomb, occupied, virtual, tile_mask):
    rows = lax.axis_size("row")
    cols = lax.axis_size("col")
    pdev, mrow, ncol = coulomb.shape
    jpart = mrow // cols
    nao = mrow * rows
    mine = pdev // rows
    row_idx = lax.axis_index("row")
    col_idx = lax.axis_index("col")
    aux_idx = lax.axis_index("aux")
    col_order = col_idx ^ jnp.arange(cols, dtype=jnp.int32)
    tiles_r = mrow // TILE
    tiles_c = ncol // TILE
    tiles = lax.dynamic_slice(
        tile_mask, (row_idx * tiles_r, col_idx * tiles_c), (tiles_r, tiles_c)
    )
    by_source = coulomb.reshape(rows, mine, mrow, ncol)

    def along_row(value):
        return lax.all_to_all(value, "row", split_axis=0, concat_axis=0, tiled=True)

    def along_col(blocks):
        return [swapped(block, "col", step) for step, block in enumerate(blocks)]

    large, small = mine // 2, max(1, mine // 8)
    halves, last = large // 2, mine - large - small

    masked_small = masked_piece(by_source, tiles, large, small, [])
    masked_large = masked_piece(by_source, tiles, 0, large, [masked_small])
    masked_last = masked_piece(by_source, tiles, large + small, last, [masked_large])
    moved_small = along_row(masked_small)
    moved_large = along_row(masked_large)

    share = cols * lax.axis_size("aux")
    place = (col_idx * lax.axis_size("aux") + aux_idx).astype(jnp.int32)
    whole = own_parts([occupied, virtual], place, mrow // share, [masked_small])
    whole = lax.all_gather(whole, "row", axis=0, tiled=False)
    whole = ordered(whole, [moved_small, masked_large])
    whole = lax.all_gather(whole, ("col", "aux"), axis=0, tiled=False)
    occ_t = occupied_order(whole, col_order, jpart, [masked_last])
    virt = virtual_order(whole, col_order, ncol, [occ_t])

    half = half_transformed(occ_t, moved_small, 0, small, cols, [virt])
    first = fully_transformed(
        along_col(half), virt, rows, None, large // small, large + small, [half[0]]
    )
    released = ordered(masked_last, [moved_large, first])
    moved_last = along_row(released)

    latest, spread = [released], []
    for number in range(2):
        half = half_transformed(occ_t, moved_large, number * halves, halves, cols, latest)
        latest = [half[0]]
        spread.append(along_col(half))
    for number, blocks in enumerate(spread):
        first = fully_transformed(
            blocks, virt, rows, first, number, large + small, latest if number == 0 else []
        )
    back = [along_row(first)]

    strips = masked_strips(coulomb, tiles, col_order[:-1], jpart, [first])
    strips = along_col(strips)
    theirs = [swapped(value, "aux", 1) for value in strips]

    half = half_transformed(occ_t, moved_last, 0, last, cols, [first])
    second = fully_transformed(
        along_col(half), virt, rows, None, 0, last, [half[0]] + strips[1:]
    )
    back.append(along_row(second))
    strips.append(swapped(masked_strips(coulomb, tiles, col_order[-1:], jpart, [second])[0], "col", cols - 1))
    theirs.append(swapped(strips[-1], "aux", 1))

    parts = [
        contracted(back[0], [strips[:-1], theirs[:-1]], 0, [second])
        + contracted(back[0], [strips[-1:], theirs[-1:]], cols - 1, [second]),
        contracted(back[1], [strips, theirs], 0, [second]),
    ]
    chi = jnp.concatenate(parts, axis=1)
    chi = jnp.where(aux_idx == 0, chi, chi[:, :, ::-1]).reshape(pdev, 2 * pdev)
    for axis, size in (("row", rows), ("col", cols)):
        chi = sum([swapped(chi, axis, step) for step in range(size)])
    return chi / NAO


def solution(mesh):
    placed = (P("aux", "row", "col"), P("row", None), P("row", None), P())
    return jax.shard_map(
        shards, mesh=mesh, in_specs=placed, out_specs=P("aux", None), check_vma=False
    )
```

```python
import jax
import jax.numpy as jnp
from jax import lax
from jax.experimental import pallas as pl
from jax.experimental.pallas import tpu as pltpu
from jax.sharding import PartitionSpec as P

NAO = 2048
TILE = 128
VMEM_BYTES = 48 * 2**20
F32 = jnp.float32
BF16 = jnp.bfloat16
ANY = pl.BlockSpec(memory_space=pl.ANY)
WHOLE = pl.BlockSpec(memory_space=pltpu.VMEM)


def swapped(value, axis, apart):
    if apart == 0:
        return value
    pairs = [(source, source ^ apart) for source in range(lax.axis_size(axis))]
    return lax.ppermute(value, axis, pairs)


def cost(flops, moved):
    return pl.CostEstimate(flops=flops, bytes_accessed=moved, transcendentals=0)


def params():
    return pltpu.CompilerParams(vmem_limit_bytes=VMEM_BYTES)


def ordered(value, after):
    def body(*refs):
        del refs

    return pl.pallas_call(
        body,
        in_specs=[ANY] * (1 + len(after)),
        out_specs=ANY,
        out_shape=jax.ShapeDtypeStruct(value.shape, value.dtype),
        input_output_aliases={0: 0},
        name="ordered",
    )(value, *after)


def own_parts(blocks, place, part, after):
    count, nao = len(blocks), blocks[0].shape[1]

    def body(place_ref, *refs):
        for index in range(count):
            refs[count + len(after)][index] = refs[index][...]

    return pl.pallas_call(
        body,
        grid_spec=pltpu.PrefetchScalarGridSpec(
            num_scalar_prefetch=1,
            grid=(1,),
            in_specs=[pl.BlockSpec((part, nao), lambda i, place: (place[0], 0))] * count
            + [ANY] * len(after),
            out_specs=pl.BlockSpec((count, part, nao), lambda i, place: (0, 0, 0)),
        ),
        out_shape=jax.ShapeDtypeStruct((count, part, nao), BF16),
        name="own_parts",
    )(place.reshape(1), *blocks, *after)


def masked_piece(by_source, tiles, first, per, after):
    rows, _, mrow, ncol = by_source.shape

    def body(tiles_ref, source, *refs):
        target = refs[len(after)]
        for down in range(mrow // TILE):
            for across in range(ncol // TILE):
                keep = tiles_ref[down, across] != 0
                here = slice(down * TILE, (down + 1) * TILE), slice(across * TILE, (across + 1) * TILE)
                block = source[:, 0, here[0], here[1]]
                target[:, 0, here[0], here[1]] = jnp.where(keep, block, jnp.zeros_like(block))

    shape = (rows, 1, mrow, ncol)
    return pl.pallas_call(
        body,
        grid_spec=pltpu.PrefetchScalarGridSpec(
            num_scalar_prefetch=1,
            grid=(per,),
            in_specs=[pl.BlockSpec(shape, lambda i, t: (0, first + i, 0, 0))] + [ANY] * len(after),
            out_specs=pl.BlockSpec(shape, lambda i, t: (0, i, 0, 0)),
        ),
        out_shape=jax.ShapeDtypeStruct((rows, per, mrow, ncol), BF16),
        cost_estimate=cost(0, 4 * rows * per * mrow * ncol),
        compiler_params=params(),
        name="masked_piece",
    )(tiles, by_source, *after)


def masked_strips(coulomb, tiles, order, jpart, after):
    count = order.shape[0]
    pdev, mrow, ncol = coulomb.shape
    some = pdev // 4

    def body(order_ref, tiles_ref, *refs):
        ins, outs = refs[:count], refs[count + len(after) :]
        for step, (source, target) in enumerate(zip(ins, outs)):
            down = lax.div(order_ref[step] * jpart, TILE)
            for across in range(ncol // TILE):
                keep = tiles_ref[down, across] != 0
                span = slice(across * TILE, (across + 1) * TILE)
                block = source[:, :, span]
                target[:, :, span] = jnp.where(keep, block, jnp.zeros_like(block))

    def strip(step):
        return pl.BlockSpec((some, jpart, ncol), lambda p, order, tiles: (p, order[step], 0))

    return pl.pallas_call(
        body,
        grid_spec=pltpu.PrefetchScalarGridSpec(
            num_scalar_prefetch=2,
            grid=(pdev // some,),
            in_specs=[strip(step) for step in range(count)] + [ANY] * len(after),
            out_specs=[pl.BlockSpec((some, jpart, ncol), lambda p, order, tiles: (p, 0, 0))] * count,
        ),
        out_shape=[jax.ShapeDtypeStruct((pdev, jpart, ncol), BF16)] * count,
        cost_estimate=cost(0, 4 * count * pdev * jpart * ncol),
        compiler_params=params(),
        name="masked_strips",
    )(order, tiles, *([coulomb] * count), *after)


def occupied_order(whole, order, jpart, after):
    share, rows, _, part, nao = whole.shape
    mrow = share * part
    cols = order.shape[0]

    def body(order_ref, source, *refs):
        target, flipped = refs[len(after)], refs[len(after) + 1]
        flipped[...] = source[...].reshape(mrow, mrow).T
        for step in range(cols):
            first = pl.multiple_of(order_ref[step] * jpart, jpart)
            target[step, 0] = flipped[pl.ds(first, jpart), :]

    result = pl.pallas_call(
        body,
        grid_spec=pltpu.PrefetchScalarGridSpec(
            num_scalar_prefetch=1,
            grid=(rows, rows),
            in_specs=[pl.BlockSpec((share, 1, 1, part, mrow), lambda i, k, o: (0, k, 0, 0, i))]
            + [ANY] * len(after),
            out_specs=pl.BlockSpec((cols, 1, jpart, mrow), lambda i, k, o: (0, i, 0, k)),
            scratch_shapes=[pltpu.VMEM((mrow, mrow), BF16)],
        ),
        out_shape=jax.ShapeDtypeStruct((cols, rows, jpart, nao), BF16),
        cost_estimate=cost(0, 4 * nao * nao),
        compiler_params=params(),
        name="occupied_order",
    )(order, whole, *after)
    return result.reshape(nao, nao)


def virtual_order(whole, order, ncol, after):
    share, rows, _, part, nao = whole.shape
    cols = order.shape[0]
    units = ncol // part
    groups = share // units

    def body(order_ref, source, *refs):
        refs[len(after)][...] = source[...].reshape(ncol, ncol)

    return pl.pallas_call(
        body,
        grid_spec=pltpu.PrefetchScalarGridSpec(
            num_scalar_prefetch=1,
            grid=(cols, cols),
            in_specs=[
                pl.BlockSpec(
                    (units, 1, 1, part, ncol),
                    lambda i, k, o: (lax.rem(o[i], groups), lax.div(o[i], groups), 1, 0, o[k]),
                )
            ]
            + [ANY] * len(after),
            out_specs=pl.BlockSpec((ncol, ncol), lambda i, k, o: (i, k)),
        ),
        out_shape=jax.ShapeDtypeStruct((nao, nao), BF16),
        cost_estimate=cost(0, 4 * nao * nao),
        compiler_params=params(),
        name="virtual_order",
    )(order, whole, *after)


def contracted(returned, strips, first, after):
    rows, per, jpart, nao = returned.shape
    pdev, _, ncol = strips[0][0].shape
    left = rows * per
    group = min(jpart, 32 if left <= 8 else 16)
    tall = min(jpart, 32)
    steps = len(strips[0])
    count = len(strips) * steps
    flat = [value for half in strips for value in half]
    width, place = (ncol, first) if steps == 1 else (nao, 0)
    begin = first * ncol - place * width

    def body(returned_ref, *refs):
        ins, target = refs[:count], refs[count + len(after)]

        @pl.when(pl.program_id(0) == 0)
        def _():
            target[...] = jnp.zeros_like(target)

        shape = (group, left * group)
        equal = lax.broadcasted_iota(jnp.int32, shape, 0) == (
            lax.rem(lax.broadcasted_iota(jnp.int32, shape, 1), group)
        )
        for lower in range(0, tall, group):
            here = slice(lower, lower + group)
            mine = returned_ref[:, :, here, begin : begin + steps * ncol]
            mine = mine.reshape(left * group, steps * ncol)
            for half in range(len(strips)):
                other = [
                    ref[:, here, :].reshape(pdev * group, ncol)
                    for ref in ins[half * steps : (half + 1) * steps]
                ]
                total = lax.dot_general(
                    jnp.concatenate(other, axis=1),
                    mine,
                    (((1,), (1,)), ((), ())),
                    preferred_element_type=F32,
                )
                total = jnp.where(equal[None], total.reshape(pdev, group, left * group), 0.0)
                target[half] += jnp.sum(total, axis=1)

    result = pl.pallas_call(
        body,
        grid=(jpart // tall,),
        in_specs=[pl.BlockSpec((rows, per, tall, width), lambda i: (0, 0, i, place))]
        + [pl.BlockSpec((pdev, tall, ncol), lambda i: (0, i, 0))] * count
        + [ANY] * len(after),
        out_specs=pl.BlockSpec((len(strips), pdev, left * group), lambda i: (0, 0, 0)),
        out_shape=jax.ShapeDtypeStruct((len(strips), pdev, left * group), F32),
        cost_estimate=cost(
            2 * count * pdev * left * group * jpart * ncol,
            2 * jpart * ncol * (count * pdev + steps * left),
        ),
        compiler_params=params(),
        name="contracted",
    )(returned, *flat, *after)
    result = result.reshape(len(strips), pdev, rows, per, group).sum(axis=-1)
    return result.transpose(2, 3, 0, 1)


def half_transformed(occ_t, moved, first, per, parts, after):
    nao = occ_t.shape[0]
    rows, _, mrow, ncol = moved.shape
    span = nao // parts
    chunk = min(span, 256)

    def body(occ_ref, moved_ref, *refs):
        for part, target in enumerate(refs[len(after) :]):

            @pl.loop(0, span // chunk)
            def _(turn):
                local = pl.multiple_of(turn * chunk, chunk)
                here = pl.ds(pl.multiple_of(part * span + local, chunk), chunk)
                for one in range(per):
                    total = jnp.zeros((chunk, ncol), F32)
                    for row in range(rows):
                        left = occ_ref[here, row * mrow : (row + 1) * mrow]
                        total += jnp.dot(left, moved_ref[row, one], preferred_element_type=F32)
                    target[one, pl.ds(local, chunk), :] = total.astype(BF16)

    return pl.pallas_call(
        body,
        grid=(1,),
        in_specs=[
            pl.BlockSpec((nao, nao), lambda i: (0, 0), pipeline_mode=pl.Buffered(1)),
            pl.BlockSpec(
                (rows, per, mrow, ncol),
                lambda i: (0, first // per, 0, 0),
                pipeline_mode=pl.Buffered(1),
            ),
        ]
        + [ANY] * len(after),
        out_specs=[
            pl.BlockSpec((per, span, ncol), lambda i: (0, 0, 0), pipeline_mode=pl.Buffered(1))
        ]
        * parts,
        out_shape=[jax.ShapeDtypeStruct((per, span, ncol), BF16)] * parts,
        cost_estimate=cost(2 * per * nao * nao * ncol, 2 * nao * nao + 4 * per * nao * ncol),
        compiler_params=params(),
        name="half_transformed",
    )(occ_t, moved, *after)


def fully_transformed(blocks, virt, rows, base, index, total, after):
    nao = virt.shape[0]
    per, height, ncol = blocks[0].shape
    span = height // rows
    chunk = 256
    count = len(blocks)
    rest = ([] if base is None else [base]) + after

    def body(virt_ref, *refs):
        ins, target = refs[:count], refs[count + len(rest)]

        @pl.loop(0, nao // chunk)
        def _(turn):
            across = pl.ds(pl.multiple_of(turn * chunk, chunk), chunk)
            for one in range(per):
                total = jnp.zeros((height, chunk), F32)
                for step, block in enumerate(ins):
                    right = virt_ref[step * ncol : (step + 1) * ncol, across]
                    total += jnp.dot(block[one], right, preferred_element_type=F32)
                done = total.astype(BF16)
                for row in range(rows):
                    target[row, one, :, across] = done[row * span : (row + 1) * span]

    def alone(shape, place):
        return pl.BlockSpec(shape, lambda i: place, pipeline_mode=pl.Buffered(1))

    return pl.pallas_call(
        body,
        grid=(1,),
        in_specs=[alone((nao, nao), (0, 0))]
        + [alone((per, height, ncol), (0, 0, 0))] * count
        + [ANY] * len(rest),
        out_specs=alone((rows, per, span, nao), (0, index, 0, 0)),
        out_shape=jax.ShapeDtypeStruct((rows, total, span, nao), BF16),
        input_output_aliases={} if base is None else {1 + count: 0},
        cost_estimate=cost(2 * per * nao * nao * height, 2 * nao * nao + 4 * per * nao * height),
        compiler_params=params(),
        name="fully_transformed",
    )(virt, *blocks, *rest)


def shards(coulomb, occupied, virtual, tile_mask):
    rows = lax.axis_size("row")
    cols = lax.axis_size("col")
    pdev, mrow, ncol = coulomb.shape
    jpart = mrow // cols
    nao = mrow * rows
    mine = pdev // rows
    row_idx = lax.axis_index("row")
    col_idx = lax.axis_index("col")
    aux_idx = lax.axis_index("aux")
    col_order = col_idx ^ jnp.arange(cols, dtype=jnp.int32)
    tiles_r = mrow // TILE
    tiles_c = ncol // TILE
    tiles = lax.dynamic_slice(
        tile_mask, (row_idx * tiles_r, col_idx * tiles_c), (tiles_r, tiles_c)
    )
    by_source = coulomb.reshape(rows, mine, mrow, ncol)

    def along_row(value):
        return lax.all_to_all(value, "row", split_axis=0, concat_axis=0, tiled=True)

    def along_col(blocks):
        return [swapped(block, "col", step) for step, block in enumerate(blocks)]

    large, small = mine // 2, max(1, mine // 8)
    halves, last = large // 2, mine - large - small

    masked_small = masked_piece(by_source, tiles, large, small, [])
    masked_large = masked_piece(by_source, tiles, 0, large, [masked_small])
    masked_last = masked_piece(by_source, tiles, large + small, last, [masked_large])
    moved_small = along_row(masked_small)
    moved_large = along_row(masked_large)

    share = cols * lax.axis_size("aux")
    place = (col_idx * lax.axis_size("aux") + aux_idx).astype(jnp.int32)
    whole = own_parts([occupied, virtual], place, mrow // share, [moved_small, masked_large])
    whole = lax.all_gather(whole, "row", axis=0, tiled=False)
    whole = lax.all_gather(whole, ("col", "aux"), axis=0, tiled=False)
    occ_t = occupied_order(whole, col_order, jpart, [masked_last])
    virt = virtual_order(whole, col_order, ncol, [occ_t])

    half = half_transformed(occ_t, moved_small, 0, small, cols, [virt])
    first = fully_transformed(
        along_col(half), virt, rows, None, large // small, large + small, [half[0]]
    )
    released = ordered(masked_last, [moved_large, virt])
    moved_last = along_row(released)

    latest, spread = [released], []
    for number in range(2):
        half = half_transformed(occ_t, moved_large, number * halves, halves, cols, latest)
        latest = [half[0]]
        spread.append(along_col(half))
    for number, blocks in enumerate(spread):
        first = fully_transformed(
            blocks, virt, rows, first, number, large + small, latest if number == 0 else []
        )
    back = [along_row(first)]

    strips = masked_strips(coulomb, tiles, col_order[:-1], jpart, [first])
    strips = along_col(strips)
    theirs = [swapped(value, "aux", 1) for value in strips]

    half = half_transformed(occ_t, moved_last, 0, last, cols, [first])
    second = fully_transformed(
        along_col(half), virt, rows, None, 0, last, [half[0]] + strips[1:]
    )
    back.append(along_row(second))
    strips.append(swapped(masked_strips(coulomb, tiles, col_order[-1:], jpart, [second])[0], "col", cols - 1))
    theirs.append(swapped(strips[-1], "aux", 1))

    parts = [
        contracted(back[0], [strips[:-1], theirs[:-1]], 0, [second])
        + contracted(back[0], [strips[-1:], theirs[-1:]], cols - 1, [second]),
        contracted(back[1], [strips, theirs], 0, [second]),
    ]
    chi = jnp.concatenate(parts, axis=1)
    chi = jnp.where(aux_idx == 0, chi, chi[:, :, ::-1]).reshape(pdev, 2 * pdev)
    for axis, size in (("row", rows), ("col", cols)):
        chi = sum([swapped(chi, axis, step) for step in range(size)])
    return chi / NAO


def solution(mesh):
    placed = (P("aux", "row", "col"), P("row", None), P("row", None), P())
    return jax.shard_map(
        shards, mesh=mesh, in_specs=placed, out_specs=P("aux", None), check_vma=False
    )
```

```python
import jax
import jax.numpy as jnp
from jax import lax
from jax.experimental import pallas as pl
from jax.experimental.pallas import tpu as pltpu
from jax.sharding import PartitionSpec as P

NAO = 2048
TILE = 128
VMEM_BYTES = 48 * 2**20
F32 = jnp.float32
BF16 = jnp.bfloat16
ANY = pl.BlockSpec(memory_space=pl.ANY)
WHOLE = pl.BlockSpec(memory_space=pltpu.VMEM)


def swapped(value, axis, apart):
    if apart == 0:
        return value
    pairs = [(source, source ^ apart) for source in range(lax.axis_size(axis))]
    return lax.ppermute(value, axis, pairs)


def cost(flops, moved):
    return pl.CostEstimate(flops=flops, bytes_accessed=moved, transcendentals=0)


def params():
    return pltpu.CompilerParams(vmem_limit_bytes=VMEM_BYTES)


def ordered(value, after):
    def body(*refs):
        del refs

    return pl.pallas_call(
        body,
        in_specs=[ANY] * (1 + len(after)),
        out_specs=ANY,
        out_shape=jax.ShapeDtypeStruct(value.shape, value.dtype),
        input_output_aliases={0: 0},
        name="ordered",
    )(value, *after)


def own_parts(blocks, place, part, after):
    count, nao = len(blocks), blocks[0].shape[1]

    def body(place_ref, *refs):
        for index in range(count):
            refs[count + len(after)][index] = refs[index][...]

    return pl.pallas_call(
        body,
        grid_spec=pltpu.PrefetchScalarGridSpec(
            num_scalar_prefetch=1,
            grid=(1,),
            in_specs=[pl.BlockSpec((part, nao), lambda i, place: (place[0], 0))] * count
            + [ANY] * len(after),
            out_specs=pl.BlockSpec((count, part, nao), lambda i, place: (0, 0, 0)),
        ),
        out_shape=jax.ShapeDtypeStruct((count, part, nao), BF16),
        name="own_parts",
    )(place.reshape(1), *blocks, *after)


def masked_piece(by_source, tiles, first, per, after):
    rows, _, mrow, ncol = by_source.shape

    def body(tiles_ref, source, *refs):
        target = refs[len(after)]
        for down in range(mrow // TILE):
            for across in range(ncol // TILE):
                keep = tiles_ref[down, across] != 0
                here = slice(down * TILE, (down + 1) * TILE), slice(across * TILE, (across + 1) * TILE)
                block = source[:, 0, here[0], here[1]]
                target[:, 0, here[0], here[1]] = jnp.where(keep, block, jnp.zeros_like(block))

    shape = (rows, 1, mrow, ncol)
    return pl.pallas_call(
        body,
        grid_spec=pltpu.PrefetchScalarGridSpec(
            num_scalar_prefetch=1,
            grid=(per,),
            in_specs=[pl.BlockSpec(shape, lambda i, t: (0, first + i, 0, 0))] + [ANY] * len(after),
            out_specs=pl.BlockSpec(shape, lambda i, t: (0, i, 0, 0)),
        ),
        out_shape=jax.ShapeDtypeStruct((rows, per, mrow, ncol), BF16),
        cost_estimate=cost(0, 4 * rows * per * mrow * ncol),
        compiler_params=params(),
        name="masked_piece",
    )(tiles, by_source, *after)


def masked_strips(coulomb, tiles, order, jpart, after):
    count = order.shape[0]
    pdev, mrow, ncol = coulomb.shape
    some = pdev // 4

    def body(order_ref, tiles_ref, *refs):
        ins, outs = refs[:count], refs[count + len(after) :]
        for step, (source, target) in enumerate(zip(ins, outs)):
            down = lax.div(order_ref[step] * jpart, TILE)
            for across in range(ncol // TILE):
                keep = tiles_ref[down, across] != 0
                span = slice(across * TILE, (across + 1) * TILE)
                block = source[:, :, span]
                target[:, :, span] = jnp.where(keep, block, jnp.zeros_like(block))

    def strip(step):
        return pl.BlockSpec((some, jpart, ncol), lambda p, order, tiles: (p, order[step], 0))

    return pl.pallas_call(
        body,
        grid_spec=pltpu.PrefetchScalarGridSpec(
            num_scalar_prefetch=2,
            grid=(pdev // some,),
            in_specs=[strip(step) for step in range(count)] + [ANY] * len(after),
            out_specs=[pl.BlockSpec((some, jpart, ncol), lambda p, order, tiles: (p, 0, 0))] * count,
        ),
        out_shape=[jax.ShapeDtypeStruct((pdev, jpart, ncol), BF16)] * count,
        cost_estimate=cost(0, 4 * count * pdev * jpart * ncol),
        compiler_params=params(),
        name="masked_strips",
    )(order, tiles, *([coulomb] * count), *after)


def occupied_order(whole, order, jpart, after):
    share, rows, _, part, nao = whole.shape
    mrow = share * part
    cols = order.shape[0]

    def body(order_ref, source, *refs):
        target, flipped = refs[len(after)], refs[len(after) + 1]
        flipped[...] = source[...].reshape(mrow, mrow).T
        for step in range(cols):
            first = pl.multiple_of(order_ref[step] * jpart, jpart)
            target[step, 0] = flipped[pl.ds(first, jpart), :]

    result = pl.pallas_call(
        body,
        grid_spec=pltpu.PrefetchScalarGridSpec(
            num_scalar_prefetch=1,
            grid=(rows, rows),
            in_specs=[pl.BlockSpec((share, 1, 1, part, mrow), lambda i, k, o: (0, k, 0, 0, i))]
            + [ANY] * len(after),
            out_specs=pl.BlockSpec((cols, 1, jpart, mrow), lambda i, k, o: (0, i, 0, k)),
            scratch_shapes=[pltpu.VMEM((mrow, mrow), BF16)],
        ),
        out_shape=jax.ShapeDtypeStruct((cols, rows, jpart, nao), BF16),
        cost_estimate=cost(0, 4 * nao * nao),
        compiler_params=params(),
        name="occupied_order",
    )(order, whole, *after)
    return result.reshape(nao, nao)


def virtual_order(whole, order, ncol, after):
    share, rows, _, part, nao = whole.shape
    cols = order.shape[0]
    units = ncol // part
    groups = share // units

    def body(order_ref, source, *refs):
        refs[len(after)][...] = source[...].reshape(ncol, ncol)

    return pl.pallas_call(
        body,
        grid_spec=pltpu.PrefetchScalarGridSpec(
            num_scalar_prefetch=1,
            grid=(cols, cols),
            in_specs=[
                pl.BlockSpec(
                    (units, 1, 1, part, ncol),
                    lambda i, k, o: (lax.rem(o[i], groups), lax.div(o[i], groups), 1, 0, o[k]),
                )
            ]
            + [ANY] * len(after),
            out_specs=pl.BlockSpec((ncol, ncol), lambda i, k, o: (i, k)),
        ),
        out_shape=jax.ShapeDtypeStruct((nao, nao), BF16),
        cost_estimate=cost(0, 4 * nao * nao),
        compiler_params=params(),
        name="virtual_order",
    )(order, whole, *after)


def contracted(returned, strips, first, after):
    rows, per, jpart, nao = returned.shape
    pdev, _, ncol = strips[0][0].shape
    left = rows * per
    group = min(jpart, 32 if left <= 8 else 16)
    tall = min(jpart, 32)
    steps = len(strips[0])
    count = len(strips) * steps
    flat = [value for half in strips for value in half]
    width, place = (ncol, first) if steps == 1 else (nao, 0)
    begin = first * ncol - place * width

    def body(returned_ref, *refs):
        ins, target = refs[:count], refs[count + len(after)]

        @pl.when(pl.program_id(0) == 0)
        def _():
            target[...] = jnp.zeros_like(target)

        shape = (group, left * group)
        equal = lax.broadcasted_iota(jnp.int32, shape, 0) == (
            lax.rem(lax.broadcasted_iota(jnp.int32, shape, 1), group)
        )
        for lower in range(0, tall, group):
            here = slice(lower, lower + group)
            mine = returned_ref[:, :, here, begin : begin + steps * ncol]
            mine = mine.reshape(left * group, steps * ncol)
            for half in range(len(strips)):
                other = [
                    ref[:, here, :].reshape(pdev * group, ncol)
                    for ref in ins[half * steps : (half + 1) * steps]
                ]
                total = lax.dot_general(
                    jnp.concatenate(other, axis=1),
                    mine,
                    (((1,), (1,)), ((), ())),
                    preferred_element_type=F32,
                )
                total = jnp.where(equal[None], total.reshape(pdev, group, left * group), 0.0)
                target[half] += jnp.sum(total, axis=1)

    result = pl.pallas_call(
        body,
        grid=(jpart // tall,),
        in_specs=[pl.BlockSpec((rows, per, tall, width), lambda i: (0, 0, i, place))]
        + [pl.BlockSpec((pdev, tall, ncol), lambda i: (0, i, 0))] * count
        + [ANY] * len(after),
        out_specs=pl.BlockSpec((len(strips), pdev, left * group), lambda i: (0, 0, 0)),
        out_shape=jax.ShapeDtypeStruct((len(strips), pdev, left * group), F32),
        cost_estimate=cost(
            2 * count * pdev * left * group * jpart * ncol,
            2 * jpart * ncol * (count * pdev + steps * left),
        ),
        compiler_params=params(),
        name="contracted",
    )(returned, *flat, *after)
    result = result.reshape(len(strips), pdev, rows, per, group).sum(axis=-1)
    return result.transpose(2, 3, 0, 1)


def half_transformed(occ_t, moved, first, per, parts, after):
    nao = occ_t.shape[0]
    rows, _, mrow, ncol = moved.shape
    span = nao // parts
    chunk = min(span, 256)

    def body(occ_ref, moved_ref, *refs):
        for part, target in enumerate(refs[len(after) :]):

            @pl.loop(0, span // chunk)
            def _(turn):
                local = pl.multiple_of(turn * chunk, chunk)
                here = pl.ds(pl.multiple_of(part * span + local, chunk), chunk)
                for one in range(per):
                    total = jnp.zeros((chunk, ncol), F32)
                    for row in range(rows):
                        left = occ_ref[here, row * mrow : (row + 1) * mrow]
                        total += jnp.dot(left, moved_ref[row, one], preferred_element_type=F32)
                    target[one, pl.ds(local, chunk), :] = total.astype(BF16)

    return pl.pallas_call(
        body,
        grid=(1,),
        in_specs=[
            pl.BlockSpec((nao, nao), lambda i: (0, 0), pipeline_mode=pl.Buffered(1)),
            pl.BlockSpec(
                (rows, per, mrow, ncol),
                lambda i: (0, first // per, 0, 0),
                pipeline_mode=pl.Buffered(1),
            ),
        ]
        + [ANY] * len(after),
        out_specs=[
            pl.BlockSpec((per, span, ncol), lambda i: (0, 0, 0), pipeline_mode=pl.Buffered(1))
        ]
        * parts,
        out_shape=[jax.ShapeDtypeStruct((per, span, ncol), BF16)] * parts,
        cost_estimate=cost(2 * per * nao * nao * ncol, 2 * nao * nao + 4 * per * nao * ncol),
        compiler_params=params(),
        name="half_transformed",
    )(occ_t, moved, *after)


def fully_transformed(blocks, virt, rows, base, index, total, after):
    nao = virt.shape[0]
    per, height, ncol = blocks[0].shape
    span = height // rows
    chunk = 256
    count = len(blocks)
    rest = ([] if base is None else [base]) + after

    def body(virt_ref, *refs):
        ins, target = refs[:count], refs[count + len(rest)]

        @pl.loop(0, nao // chunk)
        def _(turn):
            across = pl.ds(pl.multiple_of(turn * chunk, chunk), chunk)
            for one in range(per):
                total = jnp.zeros((height, chunk), F32)
                for step, block in enumerate(ins):
                    right = virt_ref[step * ncol : (step + 1) * ncol, across]
                    total += jnp.dot(block[one], right, preferred_element_type=F32)
                done = total.astype(BF16)
                for row in range(rows):
                    target[row, one, :, across] = done[row * span : (row + 1) * span]

    def alone(shape, place):
        return pl.BlockSpec(shape, lambda i: place, pipeline_mode=pl.Buffered(1))

    return pl.pallas_call(
        body,
        grid=(1,),
        in_specs=[alone((nao, nao), (0, 0))]
        + [alone((per, height, ncol), (0, 0, 0))] * count
        + [ANY] * len(rest),
        out_specs=alone((rows, per, span, nao), (0, index, 0, 0)),
        out_shape=jax.ShapeDtypeStruct((rows, total, span, nao), BF16),
        input_output_aliases={} if base is None else {1 + count: 0},
        cost_estimate=cost(2 * per * nao * nao * height, 2 * nao * nao + 4 * per * nao * height),
        compiler_params=params(),
        name="fully_transformed",
    )(virt, *blocks, *rest)


def shards(coulomb, occupied, virtual, tile_mask):
    rows = lax.axis_size("row")
    cols = lax.axis_size("col")
    pdev, mrow, ncol = coulomb.shape
    jpart = mrow // cols
    nao = mrow * rows
    mine = pdev // rows
    row_idx = lax.axis_index("row")
    col_idx = lax.axis_index("col")
    aux_idx = lax.axis_index("aux")
    col_order = col_idx ^ jnp.arange(cols, dtype=jnp.int32)
    tiles_r = mrow // TILE
    tiles_c = ncol // TILE
    tiles = lax.dynamic_slice(
        tile_mask, (row_idx * tiles_r, col_idx * tiles_c), (tiles_r, tiles_c)
    )
    by_source = coulomb.reshape(rows, mine, mrow, ncol)

    def along_row(value):
        return lax.all_to_all(value, "row", split_axis=0, concat_axis=0, tiled=True)

    def along_col(blocks):
        return [swapped(block, "col", step) for step, block in enumerate(blocks)]

    large, small = mine // 2, max(1, mine // 8)
    halves, last = large // 2, mine - large - small

    masked_small = masked_piece(by_source, tiles, large, small, [])
    masked_large = masked_piece(by_source, tiles, 0, large, [masked_small])
    masked_last = masked_piece(by_source, tiles, large + small, last, [masked_large])
    moved_small = along_row(masked_small)
    moved_large = along_row(masked_large)

    share = cols * lax.axis_size("aux")
    place = (col_idx * lax.axis_size("aux") + aux_idx).astype(jnp.int32)
    whole = own_parts([occupied, virtual], place, mrow // share, [masked_small])
    whole = lax.all_gather(whole, "row", axis=0, tiled=False)
    whole = ordered(whole, [moved_small, masked_large])
    whole = lax.all_gather(whole, ("col", "aux"), axis=0, tiled=False)
    occ_t = occupied_order(whole, col_order, jpart, [masked_last])
    virt = virtual_order(whole, col_order, ncol, [occ_t])

    half = half_transformed(occ_t, moved_small, 0, small, cols, [virt])
    first = fully_transformed(
        along_col(half), virt, rows, None, large // small, large + small, [half[0]]
    )
    released = ordered(masked_last, [moved_large, first])
    moved_last = along_row(released)

    latest, spread = [released], []
    for number in range(2):
        half = half_transformed(occ_t, moved_large, number * halves, halves, cols, latest)
        latest = [half[0]]
        spread.append(along_col(half))
    for number, blocks in enumerate(spread):
        first = fully_transformed(
            blocks, virt, rows, first, number, large + small, latest if number == 0 else []
        )
    back = [along_row(first)]

    strips = masked_strips(coulomb, tiles, col_order[:-1], jpart, [first])
    strips = along_col(strips)
    theirs = [swapped(value, "aux", 1) for value in strips]

    half = half_transformed(occ_t, moved_last, 0, last, cols, [first])
    second = fully_transformed(
        along_col(half), virt, rows, None, 0, last, [half[0]] + strips[1:]
    )
    back.append(along_row(second))
    strips.append(swapped(masked_strips(coulomb, tiles, col_order[-1:], jpart, [second])[0], "col", cols - 1))
    theirs.append(swapped(strips[-1], "aux", 1))

    parts = [
        contracted(back[0], [strips[:-1], theirs[:-1]], 0, [second])
        + contracted(back[0], [strips[-1:], theirs[-1:]], cols - 1, [second]),
        contracted(back[1], [strips, theirs], 0, [second]),
    ]
    chi = jnp.concatenate(parts, axis=1)
    chi = jnp.where(aux_idx == 0, chi, chi[:, :, ::-1]).reshape(pdev, 2 * pdev)
    copies = jnp.broadcast_to(chi[None], (rows * cols, *chi.shape))
    copies = lax.all_to_all(copies, ("row", "col"), split_axis=0, concat_axis=0, tiled=True)
    chi = copies.sum(axis=0)
    return chi / NAO


def solution(mesh):
    placed = (P("aux", "row", "col"), P("row", None), P("row", None), P())
    return jax.shard_map(
        shards, mesh=mesh, in_specs=placed, out_specs=P("aux", None), check_vma=False
    )
```

```python
import jax
import jax.numpy as jnp
from jax import lax
from jax.experimental import pallas as pl
from jax.experimental.pallas import tpu as pltpu
from jax.sharding import PartitionSpec as P

NAO = 2048
TILE = 128
VMEM_BYTES = 48 * 2**20
F32 = jnp.float32
BF16 = jnp.bfloat16
ANY = pl.BlockSpec(memory_space=pl.ANY)
WHOLE = pl.BlockSpec(memory_space=pltpu.VMEM)


def swapped(value, axis, apart):
    if apart == 0:
        return value
    pairs = [(source, source ^ apart) for source in range(lax.axis_size(axis))]
    return lax.ppermute(value, axis, pairs)


def cost(flops, moved):
    return pl.CostEstimate(flops=flops, bytes_accessed=moved, transcendentals=0)


def params():
    return pltpu.CompilerParams(vmem_limit_bytes=VMEM_BYTES)


def ordered(value, after):
    def body(*refs):
        del refs

    return pl.pallas_call(
        body,
        in_specs=[ANY] * (1 + len(after)),
        out_specs=ANY,
        out_shape=jax.ShapeDtypeStruct(value.shape, value.dtype),
        input_output_aliases={0: 0},
        name="ordered",
    )(value, *after)


def own_parts(blocks, place, part, after):
    count, nao = len(blocks), blocks[0].shape[1]

    def body(place_ref, *refs):
        for index in range(count):
            refs[count + len(after)][index] = refs[index][...]

    return pl.pallas_call(
        body,
        grid_spec=pltpu.PrefetchScalarGridSpec(
            num_scalar_prefetch=1,
            grid=(1,),
            in_specs=[pl.BlockSpec((part, nao), lambda i, place: (place[0], 0))] * count
            + [ANY] * len(after),
            out_specs=pl.BlockSpec((count, part, nao), lambda i, place: (0, 0, 0)),
        ),
        out_shape=jax.ShapeDtypeStruct((count, part, nao), BF16),
        name="own_parts",
    )(place.reshape(1), *blocks, *after)


def along_line(mine, row_idx, after):
    rows = lax.axis_size("row")
    up, down, ups, downs = mine, mine, [], []
    for step in range(1, rows):
        up = lax.ppermute(up, "row", [(at, at + 1) for at in range(step - 1, rows - 1)])
        down = lax.ppermute(down, "row", [(at, at - 1) for at in range(1, rows - step + 1)])
        ups.append(up)
        downs.append(down)
    count = 2 * (rows - 1)

    def body(row_ref, own, *refs):
        target = refs[count + len(after)]
        here = row_ref[0]
        target[here] = own[...]
        for step in range(1, rows):

            @pl.when(here >= step)
            def _():
                target[here - step] = refs[step - 1][...]

            @pl.when(here + step < rows)
            def _():
                target[here + step] = refs[rows - 1 + step - 1][...]

    return pl.pallas_call(
        body,
        in_specs=[pl.BlockSpec(memory_space=pltpu.SMEM)] + [WHOLE] * (1 + count) + [ANY] * len(after),
        out_specs=WHOLE,
        out_shape=jax.ShapeDtypeStruct((rows, *mine.shape), BF16),
        cost_estimate=cost(0, 4 * rows * mine.size),
        compiler_params=params(),
        name="along_line",
    )(row_idx.astype(jnp.int32).reshape(1), mine, *ups, *downs, *after)


def masked_piece(by_source, tiles, first, per, after):
    rows, _, mrow, ncol = by_source.shape

    def body(tiles_ref, source, *refs):
        target = refs[len(after)]
        for down in range(mrow // TILE):
            for across in range(ncol // TILE):
                keep = tiles_ref[down, across] != 0
                here = slice(down * TILE, (down + 1) * TILE), slice(across * TILE, (across + 1) * TILE)
                block = source[:, 0, here[0], here[1]]
                target[:, 0, here[0], here[1]] = jnp.where(keep, block, jnp.zeros_like(block))

    shape = (rows, 1, mrow, ncol)
    return pl.pallas_call(
        body,
        grid_spec=pltpu.PrefetchScalarGridSpec(
            num_scalar_prefetch=1,
            grid=(per,),
            in_specs=[pl.BlockSpec(shape, lambda i, t: (0, first + i, 0, 0))] + [ANY] * len(after),
            out_specs=pl.BlockSpec(shape, lambda i, t: (0, i, 0, 0)),
        ),
        out_shape=jax.ShapeDtypeStruct((rows, per, mrow, ncol), BF16),
        cost_estimate=cost(0, 4 * rows * per * mrow * ncol),
        compiler_params=params(),
        name="masked_piece",
    )(tiles, by_source, *after)


def masked_strips(coulomb, tiles, order, jpart, after):
    count = order.shape[0]
    pdev, mrow, ncol = coulomb.shape
    some = pdev // 4

    def body(order_ref, tiles_ref, *refs):
        ins, outs = refs[:count], refs[count + len(after) :]
        for step, (source, target) in enumerate(zip(ins, outs)):
            down = lax.div(order_ref[step] * jpart, TILE)
            for across in range(ncol // TILE):
                keep = tiles_ref[down, across] != 0
                span = slice(across * TILE, (across + 1) * TILE)
                block = source[:, :, span]
                target[:, :, span] = jnp.where(keep, block, jnp.zeros_like(block))

    def strip(step):
        return pl.BlockSpec((some, jpart, ncol), lambda p, order, tiles: (p, order[step], 0))

    return pl.pallas_call(
        body,
        grid_spec=pltpu.PrefetchScalarGridSpec(
            num_scalar_prefetch=2,
            grid=(pdev // some,),
            in_specs=[strip(step) for step in range(count)] + [ANY] * len(after),
            out_specs=[pl.BlockSpec((some, jpart, ncol), lambda p, order, tiles: (p, 0, 0))] * count,
        ),
        out_shape=[jax.ShapeDtypeStruct((pdev, jpart, ncol), BF16)] * count,
        cost_estimate=cost(0, 4 * count * pdev * jpart * ncol),
        compiler_params=params(),
        name="masked_strips",
    )(order, tiles, *([coulomb] * count), *after)


def occupied_order(whole, order, jpart, after):
    share, rows, _, part, nao = whole.shape
    mrow = share * part
    cols = order.shape[0]

    def body(order_ref, source, *refs):
        target, flipped = refs[len(after)], refs[len(after) + 1]
        flipped[...] = source[...].reshape(mrow, mrow).T
        for step in range(cols):
            first = pl.multiple_of(order_ref[step] * jpart, jpart)
            target[step, 0] = flipped[pl.ds(first, jpart), :]

    result = pl.pallas_call(
        body,
        grid_spec=pltpu.PrefetchScalarGridSpec(
            num_scalar_prefetch=1,
            grid=(rows, rows),
            in_specs=[pl.BlockSpec((share, 1, 1, part, mrow), lambda i, k, o: (0, k, 0, 0, i))]
            + [ANY] * len(after),
            out_specs=pl.BlockSpec((cols, 1, jpart, mrow), lambda i, k, o: (0, i, 0, k)),
            scratch_shapes=[pltpu.VMEM((mrow, mrow), BF16)],
        ),
        out_shape=jax.ShapeDtypeStruct((cols, rows, jpart, nao), BF16),
        cost_estimate=cost(0, 4 * nao * nao),
        compiler_params=params(),
        name="occupied_order",
    )(order, whole, *after)
    return result.reshape(nao, nao)


def virtual_order(whole, order, ncol, after):
    share, rows, _, part, nao = whole.shape
    cols = order.shape[0]
    units = ncol // part
    groups = share // units

    def body(order_ref, source, *refs):
        refs[len(after)][...] = source[...].reshape(ncol, ncol)

    return pl.pallas_call(
        body,
        grid_spec=pltpu.PrefetchScalarGridSpec(
            num_scalar_prefetch=1,
            grid=(cols, cols),
            in_specs=[
                pl.BlockSpec(
                    (units, 1, 1, part, ncol),
                    lambda i, k, o: (lax.rem(o[i], groups), lax.div(o[i], groups), 1, 0, o[k]),
                )
            ]
            + [ANY] * len(after),
            out_specs=pl.BlockSpec((ncol, ncol), lambda i, k, o: (i, k)),
        ),
        out_shape=jax.ShapeDtypeStruct((nao, nao), BF16),
        cost_estimate=cost(0, 4 * nao * nao),
        compiler_params=params(),
        name="virtual_order",
    )(order, whole, *after)


def contracted(returned, strips, first, after):
    rows, per, jpart, nao = returned.shape
    pdev, _, ncol = strips[0][0].shape
    left = rows * per
    group = min(jpart, 32 if left <= 8 else 16)
    tall = min(jpart, 32)
    steps = len(strips[0])
    count = len(strips) * steps
    flat = [value for half in strips for value in half]
    width, place = (ncol, first) if steps == 1 else (nao, 0)
    begin = first * ncol - place * width

    def body(returned_ref, *refs):
        ins, target = refs[:count], refs[count + len(after)]

        @pl.when(pl.program_id(0) == 0)
        def _():
            target[...] = jnp.zeros_like(target)

        shape = (group, left * group)
        equal = lax.broadcasted_iota(jnp.int32, shape, 0) == (
            lax.rem(lax.broadcasted_iota(jnp.int32, shape, 1), group)
        )
        for lower in range(0, tall, group):
            here = slice(lower, lower + group)
            mine = returned_ref[:, :, here, begin : begin + steps * ncol]
            mine = mine.reshape(left * group, steps * ncol)
            for half in range(len(strips)):
                other = [
                    ref[:, here, :].reshape(pdev * group, ncol)
                    for ref in ins[half * steps : (half + 1) * steps]
                ]
                total = lax.dot_general(
                    jnp.concatenate(other, axis=1),
                    mine,
                    (((1,), (1,)), ((), ())),
                    preferred_element_type=F32,
                )
                total = jnp.where(equal[None], total.reshape(pdev, group, left * group), 0.0)
                target[half] += jnp.sum(total, axis=1)

    result = pl.pallas_call(
        body,
        grid=(jpart // tall,),
        in_specs=[pl.BlockSpec((rows, per, tall, width), lambda i: (0, 0, i, place))]
        + [pl.BlockSpec((pdev, tall, ncol), lambda i: (0, i, 0))] * count
        + [ANY] * len(after),
        out_specs=pl.BlockSpec((len(strips), pdev, left * group), lambda i: (0, 0, 0)),
        out_shape=jax.ShapeDtypeStruct((len(strips), pdev, left * group), F32),
        cost_estimate=cost(
            2 * count * pdev * left * group * jpart * ncol,
            2 * jpart * ncol * (count * pdev + steps * left),
        ),
        compiler_params=params(),
        name="contracted",
    )(returned, *flat, *after)
    result = result.reshape(len(strips), pdev, rows, per, group).sum(axis=-1)
    return result.transpose(2, 3, 0, 1)


def half_transformed(occ_t, moved, first, per, parts, after):
    nao = occ_t.shape[0]
    rows, _, mrow, ncol = moved.shape
    span = nao // parts
    chunk = min(span, 256)

    def body(occ_ref, moved_ref, *refs):
        for part, target in enumerate(refs[len(after) :]):

            @pl.loop(0, span // chunk)
            def _(turn):
                local = pl.multiple_of(turn * chunk, chunk)
                here = pl.ds(pl.multiple_of(part * span + local, chunk), chunk)
                for one in range(per):
                    total = jnp.zeros((chunk, ncol), F32)
                    for row in range(rows):
                        left = occ_ref[here, row * mrow : (row + 1) * mrow]
                        total += jnp.dot(left, moved_ref[row, one], preferred_element_type=F32)
                    target[one, pl.ds(local, chunk), :] = total.astype(BF16)

    return pl.pallas_call(
        body,
        grid=(1,),
        in_specs=[
            pl.BlockSpec((nao, nao), lambda i: (0, 0), pipeline_mode=pl.Buffered(1)),
            pl.BlockSpec(
                (rows, per, mrow, ncol),
                lambda i: (0, first // per, 0, 0),
                pipeline_mode=pl.Buffered(1),
            ),
        ]
        + [ANY] * len(after),
        out_specs=[
            pl.BlockSpec((per, span, ncol), lambda i: (0, 0, 0), pipeline_mode=pl.Buffered(1))
        ]
        * parts,
        out_shape=[jax.ShapeDtypeStruct((per, span, ncol), BF16)] * parts,
        cost_estimate=cost(2 * per * nao * nao * ncol, 2 * nao * nao + 4 * per * nao * ncol),
        compiler_params=params(),
        name="half_transformed",
    )(occ_t, moved, *after)


def fully_transformed(blocks, virt, rows, base, index, total, after):
    nao = virt.shape[0]
    per, height, ncol = blocks[0].shape
    span = height // rows
    chunk = 256
    count = len(blocks)
    rest = ([] if base is None else [base]) + after

    def body(virt_ref, *refs):
        ins, target = refs[:count], refs[count + len(rest)]

        @pl.loop(0, nao // chunk)
        def _(turn):
            across = pl.ds(pl.multiple_of(turn * chunk, chunk), chunk)
            for one in range(per):
                total = jnp.zeros((height, chunk), F32)
                for step, block in enumerate(ins):
                    right = virt_ref[step * ncol : (step + 1) * ncol, across]
                    total += jnp.dot(block[one], right, preferred_element_type=F32)
                done = total.astype(BF16)
                for row in range(rows):
                    target[row, one, :, across] = done[row * span : (row + 1) * span]

    def alone(shape, place):
        return pl.BlockSpec(shape, lambda i: place, pipeline_mode=pl.Buffered(1))

    return pl.pallas_call(
        body,
        grid=(1,),
        in_specs=[alone((nao, nao), (0, 0))]
        + [alone((per, height, ncol), (0, 0, 0))] * count
        + [ANY] * len(rest),
        out_specs=alone((rows, per, span, nao), (0, index, 0, 0)),
        out_shape=jax.ShapeDtypeStruct((rows, total, span, nao), BF16),
        input_output_aliases={} if base is None else {1 + count: 0},
        cost_estimate=cost(2 * per * nao * nao * height, 2 * nao * nao + 4 * per * nao * height),
        compiler_params=params(),
        name="fully_transformed",
    )(virt, *blocks, *rest)


def shards(coulomb, occupied, virtual, tile_mask):
    rows = lax.axis_size("row")
    cols = lax.axis_size("col")
    pdev, mrow, ncol = coulomb.shape
    jpart = mrow // cols
    nao = mrow * rows
    mine = pdev // rows
    row_idx = lax.axis_index("row")
    col_idx = lax.axis_index("col")
    aux_idx = lax.axis_index("aux")
    col_order = col_idx ^ jnp.arange(cols, dtype=jnp.int32)
    tiles_r = mrow // TILE
    tiles_c = ncol // TILE
    tiles = lax.dynamic_slice(
        tile_mask, (row_idx * tiles_r, col_idx * tiles_c), (tiles_r, tiles_c)
    )
    by_source = coulomb.reshape(rows, mine, mrow, ncol)

    def along_row(value):
        return lax.all_to_all(value, "row", split_axis=0, concat_axis=0, tiled=True)

    def along_col(blocks):
        return [swapped(block, "col", step) for step, block in enumerate(blocks)]

    large, small = mine // 2, max(1, mine // 8)
    halves, last = large // 2, mine - large - small

    masked_small = masked_piece(by_source, tiles, large, small, [])
    masked_large = masked_piece(by_source, tiles, 0, large, [masked_small])
    masked_last = masked_piece(by_source, tiles, large + small, last, [masked_large])
    moved_small = along_row(masked_small)
    moved_large = along_row(masked_large)

    share = cols * lax.axis_size("aux")
    place = (col_idx * lax.axis_size("aux") + aux_idx).astype(jnp.int32)
    whole = own_parts([occupied, virtual], place, mrow // share, [masked_small])
    whole = along_line(whole, row_idx, [moved_small, masked_large])
    whole = lax.all_gather(whole, ("col", "aux"), axis=0, tiled=False)
    occ_t = occupied_order(whole, col_order, jpart, [masked_last])
    virt = virtual_order(whole, col_order, ncol, [occ_t])

    half = half_transformed(occ_t, moved_small, 0, small, cols, [virt])
    first = fully_transformed(
        along_col(half), virt, rows, None, large // small, large + small, [half[0]]
    )
    released = ordered(masked_last, [moved_large, first])
    moved_last = along_row(released)

    latest, spread = [released], []
    for number in range(2):
        half = half_transformed(occ_t, moved_large, number * halves, halves, cols, latest)
        latest = [half[0]]
        spread.append(along_col(half))
    for number, blocks in enumerate(spread):
        first = fully_transformed(
            blocks, virt, rows, first, number, large + small, latest if number == 0 else []
        )
    back = [along_row(first)]

    strips = masked_strips(coulomb, tiles, col_order[:-1], jpart, [first])
    strips = along_col(strips)
    theirs = [swapped(value, "aux", 1) for value in strips]

    half = half_transformed(occ_t, moved_last, 0, last, cols, [first])
    second = fully_transformed(
        along_col(half), virt, rows, None, 0, last, [half[0]] + strips[1:]
    )
    back.append(along_row(second))
    strips.append(swapped(masked_strips(coulomb, tiles, col_order[-1:], jpart, [second])[0], "col", cols - 1))
    theirs.append(swapped(strips[-1], "aux", 1))

    parts = [
        contracted(back[0], [strips[:-1], theirs[:-1]], 0, [second])
        + contracted(back[0], [strips[-1:], theirs[-1:]], cols - 1, [second]),
        contracted(back[1], [strips, theirs], 0, [second]),
    ]
    chi = jnp.concatenate(parts, axis=1)
    chi = jnp.where(aux_idx == 0, chi, chi[:, :, ::-1]).reshape(pdev, 2 * pdev)
    copies = jnp.broadcast_to(chi[None], (rows * cols, *chi.shape))
    copies = lax.all_to_all(copies, ("row", "col"), split_axis=0, concat_axis=0, tiled=True)
    chi = copies.sum(axis=0)
    return chi / NAO


def solution(mesh):
    placed = (P("aux", "row", "col"), P("row", None), P("row", None), P())
    return jax.shard_map(
        shards, mesh=mesh, in_specs=placed, out_specs=P("aux", None), check_vma=False
    )
```

```python
import jax
import jax.numpy as jnp
from jax import lax
from jax.experimental import pallas as pl
from jax.experimental.pallas import tpu as pltpu
from jax.sharding import PartitionSpec as P

NAO = 2048
TILE = 128
VMEM_BYTES = 48 * 2**20
F32 = jnp.float32
BF16 = jnp.bfloat16
ANY = pl.BlockSpec(memory_space=pl.ANY)
WHOLE = pl.BlockSpec(memory_space=pltpu.VMEM)


def swapped(value, axis, apart):
    if apart == 0:
        return value
    pairs = [(source, source ^ apart) for source in range(lax.axis_size(axis))]
    return lax.ppermute(value, axis, pairs)


def cost(flops, moved):
    return pl.CostEstimate(flops=flops, bytes_accessed=moved, transcendentals=0)


def params():
    return pltpu.CompilerParams(vmem_limit_bytes=VMEM_BYTES)


def ordered(value, after):
    def body(*refs):
        del refs

    return pl.pallas_call(
        body,
        in_specs=[ANY] * (1 + len(after)),
        out_specs=ANY,
        out_shape=jax.ShapeDtypeStruct(value.shape, value.dtype),
        input_output_aliases={0: 0},
        name="ordered",
    )(value, *after)


def own_parts(blocks, place, part, after):
    count, nao = len(blocks), blocks[0].shape[1]

    def body(place_ref, *refs):
        for index in range(count):
            refs[count + len(after)][index] = refs[index][...]

    return pl.pallas_call(
        body,
        grid_spec=pltpu.PrefetchScalarGridSpec(
            num_scalar_prefetch=1,
            grid=(1,),
            in_specs=[pl.BlockSpec((part, nao), lambda i, place: (place[0], 0))] * count
            + [ANY] * len(after),
            out_specs=pl.BlockSpec((count, part, nao), lambda i, place: (0, 0, 0)),
        ),
        out_shape=jax.ShapeDtypeStruct((count, part, nao), BF16),
        name="own_parts",
    )(place.reshape(1), *blocks, *after)


def masked_piece(by_source, tiles, first, per, after):
    rows, _, mrow, ncol = by_source.shape

    def body(tiles_ref, source, *refs):
        target = refs[len(after)]
        for down in range(mrow // TILE):
            for across in range(ncol // TILE):
                keep = tiles_ref[down, across] != 0
                here = slice(down * TILE, (down + 1) * TILE), slice(across * TILE, (across + 1) * TILE)
                block = source[:, 0, here[0], here[1]]
                target[:, 0, here[0], here[1]] = jnp.where(keep, block, jnp.zeros_like(block))

    shape = (rows, 1, mrow, ncol)
    return pl.pallas_call(
        body,
        grid_spec=pltpu.PrefetchScalarGridSpec(
            num_scalar_prefetch=1,
            grid=(per,),
            in_specs=[pl.BlockSpec(shape, lambda i, t: (0, first + i, 0, 0))] + [ANY] * len(after),
            out_specs=pl.BlockSpec(shape, lambda i, t: (0, i, 0, 0)),
        ),
        out_shape=jax.ShapeDtypeStruct((rows, per, mrow, ncol), BF16),
        cost_estimate=cost(0, 4 * rows * per * mrow * ncol),
        compiler_params=params(),
        name="masked_piece",
    )(tiles, by_source, *after)


def masked_strips(coulomb, tiles, order, jpart, after):
    count = order.shape[0]
    pdev, mrow, ncol = coulomb.shape
    some = pdev // 4

    def body(order_ref, tiles_ref, *refs):
        ins, outs = refs[:count], refs[count + len(after) :]
        for step, (source, target) in enumerate(zip(ins, outs)):
            down = lax.div(order_ref[step] * jpart, TILE)
            for across in range(ncol // TILE):
                keep = tiles_ref[down, across] != 0
                span = slice(across * TILE, (across + 1) * TILE)
                block = source[:, :, span]
                target[:, :, span] = jnp.where(keep, block, jnp.zeros_like(block))

    def strip(step):
        return pl.BlockSpec((some, jpart, ncol), lambda p, order, tiles: (p, order[step], 0))

    return pl.pallas_call(
        body,
        grid_spec=pltpu.PrefetchScalarGridSpec(
            num_scalar_prefetch=2,
            grid=(pdev // some,),
            in_specs=[strip(step) for step in range(count)] + [ANY] * len(after),
            out_specs=[pl.BlockSpec((some, jpart, ncol), lambda p, order, tiles: (p, 0, 0))] * count,
        ),
        out_shape=[jax.ShapeDtypeStruct((pdev, jpart, ncol), BF16)] * count,
        cost_estimate=cost(0, 4 * count * pdev * jpart * ncol),
        compiler_params=params(),
        name="masked_strips",
    )(order, tiles, *([coulomb] * count), *after)


def occupied_order(whole, order, jpart, after):
    share, rows, _, part, nao = whole.shape
    mrow = share * part
    cols = order.shape[0]

    def body(order_ref, source, *refs):
        target, flipped = refs[len(after)], refs[len(after) + 1]
        flipped[...] = source[...].reshape(mrow, mrow).T
        for step in range(cols):
            first = pl.multiple_of(order_ref[step] * jpart, jpart)
            target[step, 0] = flipped[pl.ds(first, jpart), :]

    result = pl.pallas_call(
        body,
        grid_spec=pltpu.PrefetchScalarGridSpec(
            num_scalar_prefetch=1,
            grid=(rows, rows),
            in_specs=[pl.BlockSpec((share, 1, 1, part, mrow), lambda i, k, o: (0, k, 0, 0, i))]
            + [ANY] * len(after),
            out_specs=pl.BlockSpec((cols, 1, jpart, mrow), lambda i, k, o: (0, i, 0, k)),
            scratch_shapes=[pltpu.VMEM((mrow, mrow), BF16)],
        ),
        out_shape=jax.ShapeDtypeStruct((cols, rows, jpart, nao), BF16),
        cost_estimate=cost(0, 4 * nao * nao),
        compiler_params=params(),
        name="occupied_order",
    )(order, whole, *after)
    return result.reshape(nao, nao)


def virtual_order(whole, order, ncol, after):
    share, rows, _, part, nao = whole.shape
    cols = order.shape[0]
    units = ncol // part
    groups = share // units

    def body(order_ref, source, *refs):
        refs[len(after)][...] = source[...].reshape(ncol, ncol)

    return pl.pallas_call(
        body,
        grid_spec=pltpu.PrefetchScalarGridSpec(
            num_scalar_prefetch=1,
            grid=(cols, cols),
            in_specs=[
                pl.BlockSpec(
                    (units, 1, 1, part, ncol),
                    lambda i, k, o: (lax.rem(o[i], groups), lax.div(o[i], groups), 1, 0, o[k]),
                )
            ]
            + [ANY] * len(after),
            out_specs=pl.BlockSpec((ncol, ncol), lambda i, k, o: (i, k)),
        ),
        out_shape=jax.ShapeDtypeStruct((nao, nao), BF16),
        cost_estimate=cost(0, 4 * nao * nao),
        compiler_params=params(),
        name="virtual_order",
    )(order, whole, *after)


def held(arrays, after):
    count = len(arrays)

    def body(*refs):
        ins, outs, sems = refs[:count], refs[count + len(after) : -1], refs[-1]
        copies = [
            pltpu.make_async_copy(source, target, sems.at[index])
            for index, (source, target) in enumerate(zip(ins, outs))
        ]
        for copy in copies:
            copy.start()
        for copy in copies:
            copy.wait()

    return pl.pallas_call(
        body,
        in_specs=[ANY] * (count + len(after)),
        out_specs=[WHOLE] * count,
        out_shape=[jax.ShapeDtypeStruct(value.shape, value.dtype) for value in arrays],
        scratch_shapes=[pltpu.SemaphoreType.DMA((count,))],
        cost_estimate=cost(0, sum(4 * value.size for value in arrays)),
        compiler_params=pltpu.CompilerParams(vmem_limit_bytes=24 * 2**20),
        name="held",
    )(*arrays, *after)


def contracted(returned, strips, first, after, near=False):
    rows, per, jpart, nao = returned.shape
    pdev, _, ncol = strips[0][0].shape
    left = rows * per
    group = min(jpart, 32 if left <= 8 else 16)
    tall = min(jpart, 32)
    steps = len(strips[0])
    count = len(strips) * steps
    flat = [value for half in strips for value in half]
    width, place = (ncol, first) if steps == 1 else (nao, 0)
    begin = first * ncol - place * width

    def body(returned_ref, *refs):
        ins, target = refs[:count], refs[count + len(after)]

        @pl.when(pl.program_id(0) == 0)
        def _():
            target[...] = jnp.zeros_like(target)

        shape = (group, left * group)
        equal = lax.broadcasted_iota(jnp.int32, shape, 0) == (
            lax.rem(lax.broadcasted_iota(jnp.int32, shape, 1), group)
        )
        for lower in range(0, tall, group):
            here = slice(lower, lower + group)
            mine = returned_ref[:, :, here, begin : begin + steps * ncol]
            mine = mine.reshape(left * group, steps * ncol)
            for half in range(len(strips)):
                spot = here
                if near and half == 0:
                    start = pl.program_id(0) * tall + lower
                    spot = pl.ds(pl.multiple_of(start, group), group)
                other = [
                    ref[:, spot, :].reshape(pdev * group, ncol)
                    for ref in ins[half * steps : (half + 1) * steps]
                ]
                total = lax.dot_general(
                    jnp.concatenate(other, axis=1),
                    mine,
                    (((1,), (1,)), ((), ())),
                    preferred_element_type=F32,
                )
                total = jnp.where(equal[None], total.reshape(pdev, group, left * group), 0.0)
                target[half] += jnp.sum(total, axis=1)

    result = pl.pallas_call(
        body,
        grid=(jpart // tall,),
        in_specs=[pl.BlockSpec((rows, per, tall, width), lambda i: (0, 0, i, place))]
        + [WHOLE if near else pl.BlockSpec((pdev, tall, ncol), lambda i: (0, i, 0))] * steps
        + [pl.BlockSpec((pdev, tall, ncol), lambda i: (0, i, 0))] * (count - steps)
        + [ANY] * len(after),
        out_specs=pl.BlockSpec((len(strips), pdev, left * group), lambda i: (0, 0, 0)),
        out_shape=jax.ShapeDtypeStruct((len(strips), pdev, left * group), F32),
        cost_estimate=cost(
            2 * count * pdev * left * group * jpart * ncol,
            2 * jpart * ncol * (count * pdev + steps * left),
        ),
        compiler_params=pltpu.CompilerParams(vmem_limit_bytes=(40 if near else 26) * 2**20),
        name="contracted",
    )(returned, *flat, *after)
    result = result.reshape(len(strips), pdev, rows, per, group).sum(axis=-1)
    return result.transpose(2, 3, 0, 1)


def half_transformed(occ_t, moved, first, per, parts, after):
    nao = occ_t.shape[0]
    rows, _, mrow, ncol = moved.shape
    span = nao // parts
    chunk = min(span, 256)

    def body(occ_ref, moved_ref, *refs):
        for part, target in enumerate(refs[len(after) :]):

            @pl.loop(0, span // chunk)
            def _(turn):
                local = pl.multiple_of(turn * chunk, chunk)
                here = pl.ds(pl.multiple_of(part * span + local, chunk), chunk)
                for one in range(per):
                    total = jnp.zeros((chunk, ncol), F32)
                    for row in range(rows):
                        left = occ_ref[here, row * mrow : (row + 1) * mrow]
                        total += jnp.dot(left, moved_ref[row, one], preferred_element_type=F32)
                    target[one, pl.ds(local, chunk), :] = total.astype(BF16)

    return pl.pallas_call(
        body,
        grid=(1,),
        in_specs=[
            pl.BlockSpec((nao, nao), lambda i: (0, 0), pipeline_mode=pl.Buffered(1)),
            pl.BlockSpec(
                (rows, per, mrow, ncol),
                lambda i: (0, first // per, 0, 0),
                pipeline_mode=pl.Buffered(1),
            ),
        ]
        + [ANY] * len(after),
        out_specs=[
            pl.BlockSpec((per, span, ncol), lambda i: (0, 0, 0), pipeline_mode=pl.Buffered(1))
        ]
        * parts,
        out_shape=[jax.ShapeDtypeStruct((per, span, ncol), BF16)] * parts,
        cost_estimate=cost(2 * per * nao * nao * ncol, 2 * nao * nao + 4 * per * nao * ncol),
        compiler_params=params(),
        name="half_transformed",
    )(occ_t, moved, *after)


def fully_transformed(blocks, virt, rows, base, index, total, after):
    nao = virt.shape[0]
    per, height, ncol = blocks[0].shape
    span = height // rows
    chunk = 256
    count = len(blocks)
    rest = ([] if base is None else [base]) + after

    def body(virt_ref, *refs):
        ins, target = refs[:count], refs[count + len(rest)]

        @pl.loop(0, nao // chunk)
        def _(turn):
            across = pl.ds(pl.multiple_of(turn * chunk, chunk), chunk)
            for one in range(per):
                total = jnp.zeros((height, chunk), F32)
                for step, block in enumerate(ins):
                    right = virt_ref[step * ncol : (step + 1) * ncol, across]
                    total += jnp.dot(block[one], right, preferred_element_type=F32)
                done = total.astype(BF16)
                for row in range(rows):
                    target[row, one, :, across] = done[row * span : (row + 1) * span]

    def alone(shape, place):
        return pl.BlockSpec(shape, lambda i: place, pipeline_mode=pl.Buffered(1))

    return pl.pallas_call(
        body,
        grid=(1,),
        in_specs=[alone((nao, nao), (0, 0))]
        + [alone((per, height, ncol), (0, 0, 0))] * count
        + [ANY] * len(rest),
        out_specs=alone((rows, per, span, nao), (0, index, 0, 0)),
        out_shape=jax.ShapeDtypeStruct((rows, total, span, nao), BF16),
        input_output_aliases={} if base is None else {1 + count: 0},
        cost_estimate=cost(2 * per * nao * nao * height, 2 * nao * nao + 4 * per * nao * height),
        compiler_params=params(),
        name="fully_transformed",
    )(virt, *blocks, *rest)


def shards(coulomb, occupied, virtual, tile_mask):
    rows = lax.axis_size("row")
    cols = lax.axis_size("col")
    pdev, mrow, ncol = coulomb.shape
    jpart = mrow // cols
    nao = mrow * rows
    mine = pdev // rows
    row_idx = lax.axis_index("row")
    col_idx = lax.axis_index("col")
    aux_idx = lax.axis_index("aux")
    col_order = col_idx ^ jnp.arange(cols, dtype=jnp.int32)
    tiles_r = mrow // TILE
    tiles_c = ncol // TILE
    tiles = lax.dynamic_slice(
        tile_mask, (row_idx * tiles_r, col_idx * tiles_c), (tiles_r, tiles_c)
    )
    by_source = coulomb.reshape(rows, mine, mrow, ncol)

    def along_row(value):
        return lax.all_to_all(value, "row", split_axis=0, concat_axis=0, tiled=True)

    def along_col(blocks):
        return [swapped(block, "col", step) for step, block in enumerate(blocks)]

    large, small = mine // 2, max(1, mine // 8)
    halves, last = large // 2, mine - large - small

    masked_small = masked_piece(by_source, tiles, large, small, [])
    masked_large = masked_piece(by_source, tiles, 0, large, [masked_small])
    masked_last = masked_piece(by_source, tiles, large + small, last, [masked_large])
    moved_small = along_row(masked_small)
    moved_large = along_row(masked_large)

    share = cols * lax.axis_size("aux")
    place = (col_idx * lax.axis_size("aux") + aux_idx).astype(jnp.int32)
    whole = own_parts([occupied, virtual], place, mrow // share, [masked_small])
    whole = lax.all_gather(whole, "row", axis=0, tiled=False)
    whole = ordered(whole, [moved_small, masked_large])
    whole = lax.all_gather(whole, ("col", "aux"), axis=0, tiled=False)
    occ_t = occupied_order(whole, col_order, jpart, [masked_last])
    virt = virtual_order(whole, col_order, ncol, [occ_t])

    half = half_transformed(occ_t, moved_small, 0, small, cols, [virt])
    first = fully_transformed(
        along_col(half), virt, rows, None, large // small, large + small, [half[0]]
    )
    released = ordered(masked_last, [moved_large, first])
    moved_last = along_row(released)

    latest, spread = [released], []
    for number in range(2):
        half = half_transformed(occ_t, moved_large, number * halves, halves, cols, latest)
        latest = [half[0]]
        spread.append(along_col(half))
    for number, blocks in enumerate(spread):
        first = fully_transformed(
            blocks, virt, rows, first, number, large + small, latest if number == 0 else []
        )
    back = [along_row(first)]

    strips = masked_strips(coulomb, tiles, col_order[:-1], jpart, [first])
    strips = along_col(strips)
    theirs = [swapped(value, "aux", 1) for value in strips]

    half = half_transformed(occ_t, moved_last, 0, last, cols, [first])
    second = fully_transformed(
        along_col(half), virt, rows, None, 0, last, [half[0]] + strips[1:]
    )
    back.append(along_row(second))
    strips.append(swapped(masked_strips(coulomb, tiles, col_order[-1:], jpart, [second])[0], "col", cols - 1))
    theirs.append(swapped(strips[-1], "aux", 1))

    parts = [
        contracted(back[0], [strips[:-1], theirs[:-1]], 0, [second])
        + contracted(back[0], [strips[-1:], theirs[-1:]], cols - 1, [second])
    ]
    parts.append(contracted(back[1], [held(strips, parts), theirs], 0, [second], True))
    chi = jnp.concatenate(parts, axis=1)
    chi = jnp.where(aux_idx == 0, chi, chi[:, :, ::-1]).reshape(pdev, 2 * pdev)
    copies = jnp.broadcast_to(chi[None], (rows * cols, *chi.shape))
    copies = lax.all_to_all(copies, ("row", "col"), split_axis=0, concat_axis=0, tiled=True)
    chi = copies.sum(axis=0)
    return chi / NAO


def solution(mesh):
    placed = (P("aux", "row", "col"), P("row", None), P("row", None), P())
    return jax.shard_map(
        shards, mesh=mesh, in_specs=placed, out_specs=P("aux", None), check_vma=False
    )
```

```python
import jax
import jax.numpy as jnp
from jax import lax
from jax.experimental import pallas as pl
from jax.experimental.pallas import tpu as pltpu
from jax.sharding import PartitionSpec as P

NAO = 2048
TILE = 128
VMEM_BYTES = 48 * 2**20
F32 = jnp.float32
BF16 = jnp.bfloat16
ANY = pl.BlockSpec(memory_space=pl.ANY)
WHOLE = pl.BlockSpec(memory_space=pltpu.VMEM)


def swapped(value, axis, apart):
    if apart == 0:
        return value
    pairs = [(source, source ^ apart) for source in range(lax.axis_size(axis))]
    return lax.ppermute(value, axis, pairs)


def cost(flops, moved):
    return pl.CostEstimate(flops=flops, bytes_accessed=moved, transcendentals=0)


def params():
    return pltpu.CompilerParams(vmem_limit_bytes=VMEM_BYTES)


def ordered(value, after):
    def body(*refs):
        del refs

    return pl.pallas_call(
        body,
        in_specs=[ANY] * (1 + len(after)),
        out_specs=ANY,
        out_shape=jax.ShapeDtypeStruct(value.shape, value.dtype),
        input_output_aliases={0: 0},
        name="ordered",
    )(value, *after)


def own_parts(blocks, place, part, after):
    count, nao = len(blocks), blocks[0].shape[1]

    def body(place_ref, *refs):
        for index in range(count):
            refs[count + len(after)][index] = refs[index][...]

    return pl.pallas_call(
        body,
        grid_spec=pltpu.PrefetchScalarGridSpec(
            num_scalar_prefetch=1,
            grid=(1,),
            in_specs=[pl.BlockSpec((part, nao), lambda i, place: (place[0], 0))] * count
            + [ANY] * len(after),
            out_specs=pl.BlockSpec((count, part, nao), lambda i, place: (0, 0, 0)),
        ),
        out_shape=jax.ShapeDtypeStruct((count, part, nao), BF16),
        name="own_parts",
    )(place.reshape(1), *blocks, *after)


def masked_piece(by_source, tiles, first, per, after):
    rows, _, mrow, ncol = by_source.shape

    def body(tiles_ref, source, *refs):
        target = refs[len(after)]
        down = pl.program_id(1)
        for across in range(ncol // TILE):
            keep = tiles_ref[down, across] != 0
            here = slice(across * TILE, (across + 1) * TILE)
            block = source[:, 0, :, here]
            target[:, 0, :, here] = jnp.where(keep, block, jnp.zeros_like(block))

    shape = (rows, 1, TILE, ncol)
    return pl.pallas_call(
        body,
        grid_spec=pltpu.PrefetchScalarGridSpec(
            num_scalar_prefetch=1,
            grid=(per, mrow // TILE),
            in_specs=[pl.BlockSpec(shape, lambda i, r, t: (0, first + i, r, 0))]
            + [ANY] * len(after),
            out_specs=pl.BlockSpec(shape, lambda i, r, t: (0, i, r, 0)),
        ),
        out_shape=jax.ShapeDtypeStruct((rows, per, mrow, ncol), BF16),
        cost_estimate=cost(0, 4 * rows * per * mrow * ncol),
        compiler_params=params(),
        name="masked_piece",
    )(tiles, by_source, *after)


def masked_strips(coulomb, tiles, order, jpart, after):
    count = order.shape[0]
    pdev, mrow, ncol = coulomb.shape
    some = pdev // 4

    def body(order_ref, tiles_ref, *refs):
        ins, outs = refs[:count], refs[count + len(after) :]
        for step, (source, target) in enumerate(zip(ins, outs)):
            down = lax.div(order_ref[step] * jpart, TILE)
            for across in range(ncol // TILE):
                keep = tiles_ref[down, across] != 0
                span = slice(across * TILE, (across + 1) * TILE)
                block = source[:, :, span]
                target[:, :, span] = jnp.where(keep, block, jnp.zeros_like(block))

    def strip(step):
        return pl.BlockSpec((some, jpart, ncol), lambda p, order, tiles: (p, order[step], 0))

    return pl.pallas_call(
        body,
        grid_spec=pltpu.PrefetchScalarGridSpec(
            num_scalar_prefetch=2,
            grid=(pdev // some,),
            in_specs=[strip(step) for step in range(count)] + [ANY] * len(after),
            out_specs=[pl.BlockSpec((some, jpart, ncol), lambda p, order, tiles: (p, 0, 0))] * count,
        ),
        out_shape=[jax.ShapeDtypeStruct((pdev, jpart, ncol), BF16)] * count,
        cost_estimate=cost(0, 4 * count * pdev * jpart * ncol),
        compiler_params=params(),
        name="masked_strips",
    )(order, tiles, *([coulomb] * count), *after)


def occupied_order(whole, order, jpart, after):
    share, rows, _, part, nao = whole.shape
    mrow = share * part
    cols = order.shape[0]

    def body(order_ref, source, *refs):
        target, flipped = refs[len(after)], refs[len(after) + 1]
        flipped[...] = source[...].reshape(mrow, mrow).T
        for step in range(cols):
            first = pl.multiple_of(order_ref[step] * jpart, jpart)
            target[step, 0] = flipped[pl.ds(first, jpart), :]

    result = pl.pallas_call(
        body,
        grid_spec=pltpu.PrefetchScalarGridSpec(
            num_scalar_prefetch=1,
            grid=(rows, rows),
            in_specs=[pl.BlockSpec((share, 1, 1, part, mrow), lambda i, k, o: (0, k, 0, 0, i))]
            + [ANY] * len(after),
            out_specs=pl.BlockSpec((cols, 1, jpart, mrow), lambda i, k, o: (0, i, 0, k)),
            scratch_shapes=[pltpu.VMEM((mrow, mrow), BF16)],
        ),
        out_shape=jax.ShapeDtypeStruct((cols, rows, jpart, nao), BF16),
        cost_estimate=cost(0, 4 * nao * nao),
        compiler_params=params(),
        name="occupied_order",
    )(order, whole, *after)
    return result.reshape(nao, nao)


def virtual_order(whole, order, ncol, after):
    share, rows, _, part, nao = whole.shape
    cols = order.shape[0]
    units = ncol // part
    groups = share // units

    def body(order_ref, source, *refs):
        refs[len(after)][...] = source[...].reshape(ncol, ncol)

    return pl.pallas_call(
        body,
        grid_spec=pltpu.PrefetchScalarGridSpec(
            num_scalar_prefetch=1,
            grid=(cols, cols),
            in_specs=[
                pl.BlockSpec(
                    (units, 1, 1, part, ncol),
                    lambda i, k, o: (lax.rem(o[i], groups), lax.div(o[i], groups), 1, 0, o[k]),
                )
            ]
            + [ANY] * len(after),
            out_specs=pl.BlockSpec((ncol, ncol), lambda i, k, o: (i, k)),
        ),
        out_shape=jax.ShapeDtypeStruct((nao, nao), BF16),
        cost_estimate=cost(0, 4 * nao * nao),
        compiler_params=params(),
        name="virtual_order",
    )(order, whole, *after)


def contracted(returned, strips, first, after):
    rows, per, jpart, nao = returned.shape
    pdev, _, ncol = strips[0][0].shape
    left = rows * per
    group = min(jpart, 32 if left <= 8 else 16)
    tall = min(jpart, 32)
    steps = len(strips[0])
    count = len(strips) * steps
    flat = [value for half in strips for value in half]
    width, place = (ncol, first) if steps == 1 else (nao, 0)
    begin = first * ncol - place * width

    def body(returned_ref, *refs):
        ins, target = refs[:count], refs[count + len(after)]

        @pl.when(pl.program_id(0) == 0)
        def _():
            target[...] = jnp.zeros_like(target)

        shape = (group, left * group)
        equal = lax.broadcasted_iota(jnp.int32, shape, 0) == (
            lax.rem(lax.broadcasted_iota(jnp.int32, shape, 1), group)
        )
        for lower in range(0, tall, group):
            here = slice(lower, lower + group)
            mine = returned_ref[:, :, here, begin : begin + steps * ncol]
            mine = mine.reshape(left * group, steps * ncol)
            for half in range(len(strips)):
                other = [
                    ref[:, here, :].reshape(pdev * group, ncol)
                    for ref in ins[half * steps : (half + 1) * steps]
                ]
                total = lax.dot_general(
                    jnp.concatenate(other, axis=1),
                    mine,
                    (((1,), (1,)), ((), ())),
                    preferred_element_type=F32,
                )
                total = jnp.where(equal[None], total.reshape(pdev, group, left * group), 0.0)
                target[half] += jnp.sum(total, axis=1)

    result = pl.pallas_call(
        body,
        grid=(jpart // tall,),
        in_specs=[pl.BlockSpec((rows, per, tall, width), lambda i: (0, 0, i, place))]
        + [pl.BlockSpec((pdev, tall, ncol), lambda i: (0, i, 0))] * count
        + [ANY] * len(after),
        out_specs=pl.BlockSpec((len(strips), pdev, left * group), lambda i: (0, 0, 0)),
        out_shape=jax.ShapeDtypeStruct((len(strips), pdev, left * group), F32),
        cost_estimate=cost(
            2 * count * pdev * left * group * jpart * ncol,
            2 * jpart * ncol * (count * pdev + steps * left),
        ),
        compiler_params=params(),
        name="contracted",
    )(returned, *flat, *after)
    result = result.reshape(len(strips), pdev, rows, per, group).sum(axis=-1)
    return result.transpose(2, 3, 0, 1)


def half_transformed(occ_t, moved, first, per, parts, after):
    nao = occ_t.shape[0]
    rows, _, mrow, ncol = moved.shape
    span = nao // parts
    chunk = min(span, 256)

    def body(occ_ref, moved_ref, *refs):
        for part, target in enumerate(refs[len(after) :]):

            @pl.loop(0, span // chunk)
            def _(turn):
                local = pl.multiple_of(turn * chunk, chunk)
                here = pl.ds(pl.multiple_of(part * span + local, chunk), chunk)
                for one in range(per):
                    total = jnp.zeros((chunk, ncol), F32)
                    for row in range(rows):
                        left = occ_ref[here, row * mrow : (row + 1) * mrow]
                        total += jnp.dot(left, moved_ref[row, one], preferred_element_type=F32)
                    target[one, pl.ds(local, chunk), :] = total.astype(BF16)

    return pl.pallas_call(
        body,
        grid=(1,),
        in_specs=[
            pl.BlockSpec((nao, nao), lambda i: (0, 0), pipeline_mode=pl.Buffered(1)),
            pl.BlockSpec(
                (rows, per, mrow, ncol),
                lambda i: (0, first // per, 0, 0),
                pipeline_mode=pl.Buffered(1),
            ),
        ]
        + [ANY] * len(after),
        out_specs=[
            pl.BlockSpec((per, span, ncol), lambda i: (0, 0, 0), pipeline_mode=pl.Buffered(1))
        ]
        * parts,
        out_shape=[jax.ShapeDtypeStruct((per, span, ncol), BF16)] * parts,
        cost_estimate=cost(2 * per * nao * nao * ncol, 2 * nao * nao + 4 * per * nao * ncol),
        compiler_params=params(),
        name="half_transformed",
    )(occ_t, moved, *after)


def fully_transformed(blocks, virt, rows, base, index, total, after):
    nao = virt.shape[0]
    per, height, ncol = blocks[0].shape
    span = height // rows
    chunk = 256
    count = len(blocks)
    rest = ([] if base is None else [base]) + after

    def body(virt_ref, *refs):
        ins, target = refs[:count], refs[count + len(rest)]

        @pl.loop(0, nao // chunk)
        def _(turn):
            across = pl.ds(pl.multiple_of(turn * chunk, chunk), chunk)
            for one in range(per):
                total = jnp.zeros((height, chunk), F32)
                for step, block in enumerate(ins):
                    right = virt_ref[step * ncol : (step + 1) * ncol, across]
                    total += jnp.dot(block[one], right, preferred_element_type=F32)
                done = total.astype(BF16)
                for row in range(rows):
                    target[row, one, :, across] = done[row * span : (row + 1) * span]

    def alone(shape, place):
        return pl.BlockSpec(shape, lambda i: place, pipeline_mode=pl.Buffered(1))

    return pl.pallas_call(
        body,
        grid=(1,),
        in_specs=[alone((nao, nao), (0, 0))]
        + [alone((per, height, ncol), (0, 0, 0))] * count
        + [ANY] * len(rest),
        out_specs=alone((rows, per, span, nao), (0, index, 0, 0)),
        out_shape=jax.ShapeDtypeStruct((rows, total, span, nao), BF16),
        input_output_aliases={} if base is None else {1 + count: 0},
        cost_estimate=cost(2 * per * nao * nao * height, 2 * nao * nao + 4 * per * nao * height),
        compiler_params=params(),
        name="fully_transformed",
    )(virt, *blocks, *rest)


def shards(coulomb, occupied, virtual, tile_mask):
    rows = lax.axis_size("row")
    cols = lax.axis_size("col")
    pdev, mrow, ncol = coulomb.shape
    jpart = mrow // cols
    nao = mrow * rows
    mine = pdev // rows
    row_idx = lax.axis_index("row")
    col_idx = lax.axis_index("col")
    aux_idx = lax.axis_index("aux")
    col_order = col_idx ^ jnp.arange(cols, dtype=jnp.int32)
    tiles_r = mrow // TILE
    tiles_c = ncol // TILE
    tiles = lax.dynamic_slice(
        tile_mask, (row_idx * tiles_r, col_idx * tiles_c), (tiles_r, tiles_c)
    )
    by_source = coulomb.reshape(rows, mine, mrow, ncol)

    def along_row(value):
        return lax.all_to_all(value, "row", split_axis=0, concat_axis=0, tiled=True)

    def along_col(blocks):
        return [swapped(block, "col", step) for step, block in enumerate(blocks)]

    large, small = mine // 2, max(1, mine // 8)
    halves, last = large // 2, mine - large - small

    masked_small = masked_piece(by_source, tiles, large, small, [])
    masked_large = masked_piece(by_source, tiles, 0, large, [masked_small])
    masked_last = masked_piece(by_source, tiles, large + small, last, [masked_large])
    moved_small = along_row(masked_small)
    moved_large = along_row(masked_large)

    share = cols * lax.axis_size("aux")
    place = (col_idx * lax.axis_size("aux") + aux_idx).astype(jnp.int32)
    whole = own_parts([occupied, virtual], place, mrow // share, [masked_small])
    whole = lax.all_gather(whole, "row", axis=0, tiled=False)
    whole = ordered(whole, [moved_small, masked_large])
    whole = lax.all_gather(whole, ("col", "aux"), axis=0, tiled=False)
    occ_t = occupied_order(whole, col_order, jpart, [masked_last])
    virt = virtual_order(whole, col_order, ncol, [occ_t])

    half = half_transformed(occ_t, moved_small, 0, small, cols, [virt])
    first = fully_transformed(
        along_col(half), virt, rows, None, large // small, large + small, [half[0]]
    )
    released = ordered(masked_last, [moved_large, first])
    moved_last = along_row(released)

    latest, spread = [released], []
    for number in range(2):
        half = half_transformed(occ_t, moved_large, number * halves, halves, cols, latest)
        latest = [half[0]]
        spread.append(along_col(half))
    for number, blocks in enumerate(spread):
        first = fully_transformed(
            blocks, virt, rows, first, number, large + small, latest if number == 0 else []
        )
    back = [along_row(first)]

    strips = masked_strips(coulomb, tiles, col_order[:-1], jpart, [first])
    strips = along_col(strips)
    theirs = [swapped(value, "aux", 1) for value in strips]

    half = half_transformed(occ_t, moved_last, 0, last, cols, [first])
    second = fully_transformed(
        along_col(half), virt, rows, None, 0, last, [half[0]] + strips[1:]
    )
    back.append(along_row(second))
    strips.append(swapped(masked_strips(coulomb, tiles, col_order[-1:], jpart, [second])[0], "col", cols - 1))
    theirs.append(swapped(strips[-1], "aux", 1))

    parts = [
        contracted(back[0], [strips[:-1], theirs[:-1]], 0, [second])
        + contracted(back[0], [strips[-1:], theirs[-1:]], cols - 1, [second]),
        contracted(back[1], [strips, theirs], 0, [second]),
    ]
    chi = jnp.concatenate(parts, axis=1)
    chi = jnp.where(aux_idx == 0, chi, chi[:, :, ::-1]).reshape(pdev, 2 * pdev)
    copies = jnp.broadcast_to(chi[None], (rows * cols, *chi.shape))
    copies = lax.all_to_all(copies, ("row", "col"), split_axis=0, concat_axis=0, tiled=True)
    chi = copies.sum(axis=0)
    return chi / NAO


def solution(mesh):
    placed = (P("aux", "row", "col"), P("row", None), P("row", None), P())
    return jax.shard_map(
        shards, mesh=mesh, in_specs=placed, out_specs=P("aux", None), check_vma=False
    )
```
